128 devices in a mesh: rep: 8 (over z_lo, y), shard: 16 (over z_hi, x, core).
Axes of the slice: x: 4, y: 4, z: 4 (z_hi: 2, z_lo: 2; z = z_hi * 2 + z_lo), core: 2. Of those that a mesh axis runs over, the one named last changes fastest.
Arguments:
- tokens: bfloat16 [16384, 2048], P(('rep', 'shard')), may hold values from -6 to 6
- cotangent: bfloat16 [16384, 2048], P(('rep', 'shard')), may hold values from -6 to 6
- starts: int32 [16384], P(('rep', 'shard')), may hold values from 0 to 2047, as said below
- attn_gain: bfloat16 [2048], P('shard'), may hold values from 0.5 to 1.5
- query_key_value_weight: bfloat16 [2048, 2560], P('shard'), may hold values from -0.125 to 0.125
- w_out: bfloat16 [2048, 2048], P('shard'), may hold values from -0.5 to 0.5
- ffn_gain: bfloat16 [2048], P('shard'), may hold values from 0.5 to 1.5
- w_gate_up: bfloat16 [2048, 11264], P('shard'), may hold values from -0.125 to 0.125
- w_down: bfloat16 [5632, 2048], P('shard'), may hold values from -0.078125 to 0.078125
Outputs:
- mixed_out: bfloat16 [16384, 2048], P(('rep', 'shard'))
- input_grad: bfloat16 [16384, 2048], P(('rep', 'shard'))
- grad_attn_gain: float32 [2048], P('shard')
- grad_qkv: float32 [2048, 2560], P('shard')
- grad_out: float32 [2048, 2048], P('shard')
- grad_ffn_gain: float32 [2048], P('shard')
- grad_gate_up: float32 [2048, 11264], P('shard')
- grad_down: float32 [5632, 2048], P('shard')
The draws below stay inside these ranges and needn't reach their ends.
Inputs may be any that keep to these rules, and one draw needn't show every extreme that they name: Each sequence of 2048 tokens is a pack of contiguous documents; starts is the same for all tokens of a document, equals the index of its first token within the sequence, is 0 for the first document, and is never above the token's own index.
All inputs are finite; a program needn't handle non-finite values.
Results may differ from the reference program's by a relative error of at most 0.024.
Values may be sent and summed in bfloat16 or wider, within the bound.
No kernel may reach another device: no remote copies, remote signals or barrier semaphores. Data moves between devices by JAX's collectives and lax.ppermute only.
A program may use at most 576 MiB of HBM per device.

```python
import math
import jax
import jax.numpy as jnp
from jax import lax

MODEL_DIM = 2048
QUERY_HEADS = 32
KEY_VALUE_HEADS = 4
HEAD_SIZE = 64
FF = 5632
TOK_DEV = 128
LENGTH = 2048
TOKENS = 16384
N_REP = 8


def draw_starts(key, part):
    key = jax.random.fold_in(key, 11)
    first_key, second_key = jax.random.split(key)
    doc_begin = jax.random.randint(first_key, (N_REP, 1), 1, TOK_DEV // 2 + 1)
    doc_end = jax.random.randint(second_key, (N_REP, 1), LENGTH - TOK_DEV // 2, LENGTH)
    places = jnp.arange(LENGTH, dtype=jnp.int32)[None, :]
    result = jnp.where(places < doc_begin, 0, jnp.where(places < doc_end, doc_begin, doc_end))
    return result.reshape(-1).astype(jnp.int32)


def block_scale(rng, shape, cuts, smallest, largest):
    gain, own = 1.0, jax.random.fold_in(rng, 6)
    for dim, blocks in cuts:
        steps = jnp.exp(jax.random.uniform(jax.random.fold_in(own, dim), (blocks,), jnp.float32, smallest / len(cuts), largest / len(cuts)))
        gain = gain * jnp.repeat(steps, shape[dim] // blocks).reshape([-1 if axis == dim else 1 for axis in range(len(shape))])
    return gain


def centred(stream_key, dims, scale, reach, cuts=(), kind=jnp.bfloat16):
    gain = block_scale(stream_key, dims, cuts, -0.22, 0.18) if cuts else 1.0
    drawn = jax.random.normal(stream_key, dims, jnp.float32) * scale * gain
    return jnp.minimum(jnp.maximum(drawn, -reach), reach).astype(kind)


def setup_inputs(seed: int = 0) -> dict:
    streams_of = jax.random.split(jax.random.key(seed), 10)
    tokens = centred(streams_of[0], (TOKENS, MODEL_DIM), 1.0, 6.0, ((0, 128),))
    cotangent = centred(streams_of[1], (TOKENS, MODEL_DIM), 1.0, 6.0, ((0, 128),))
    starts = draw_starts(jax.random.fold_in(streams_of[9], 71), 0)
    attn_gain = jnp.clip(1.0 + 0.1 * jax.random.normal(streams_of[3], (MODEL_DIM,), jnp.float32), 0.5, 1.5).astype(jnp.bfloat16)
    query_key_value_weight = centred(streams_of[4], (MODEL_DIM, MODEL_DIM + 2 * KEY_VALUE_HEADS * HEAD_SIZE), MODEL_DIM ** -0.5, 0.125, ((0, 16),))
    w_out = centred(streams_of[5], (MODEL_DIM, MODEL_DIM), (MODEL_DIM // 16) ** -0.5, 0.5, ((0, 16),))
    ffn_gain = jnp.clip(1.0 + 0.1 * jax.random.normal(streams_of[6], (MODEL_DIM,), jnp.float32), 0.5, 1.5).astype(jnp.bfloat16)
    w_gate_up = centred(streams_of[7], (MODEL_DIM, 2 * FF), MODEL_DIM ** -0.5, 0.125, ((0, 16),))
    w_down = centred(streams_of[8], (FF, MODEL_DIM), FF ** -0.5, 0.078125, ((0, 16),))
    return {"tokens": tokens, "cotangent": cotangent, "starts": starts, "attn_gain": attn_gain, "query_key_value_weight": query_key_value_weight, "w_out": w_out, "ffn_gain": ffn_gain, "w_gate_up": w_gate_up, "w_down": w_down}


EPS = 1e-05
ROPE_BASE = 10000.0
NEGATIVE_FILLER = -1e+30

@jax.custom_vjp
def lower_precision(v):
    return lax.optimization_barrier(v.astype(jnp.bfloat16)).astype(jnp.float32)

@jax.custom_vjp
def low_back(v):
    return v

def low_keep(v):
    return (lower_precision(v), None)

def low_pass(kept, grad):
    return (grad,)

def back_keep(v):
    return (v, None)

def back_low(kept, grad):
    return (lower_precision(grad),)
lower_precision.defvjp(low_keep, low_pass)
low_back.defvjp(back_keep, back_low)

def matmul_hi(left, right):
    return jnp.dot(left, right, precision=lax.Precision.HIGHEST)

def rope_tables(positions):
    half_size = HEAD_SIZE // 2
    freqs = jnp.exp(jnp.arange(half_size, dtype=jnp.float32) * (-2.0 * math.log(ROPE_BASE) / HEAD_SIZE))
    angles = positions.astype(jnp.float32)[:, None] * freqs[None, :]
    cosine_table = jnp.concatenate([jnp.cos(angles), jnp.cos(angles)], axis=1)
    sine_table = jnp.concatenate([jnp.sin(angles), jnp.sin(angles)], axis=1)
    return (cosine_table, sine_table)

def apply_rotary(vectors, cosine_table, sine_table):
    half_size = vectors.shape[-1] // 2
    turned = jnp.concatenate([-vectors[..., half_size:], vectors[..., :half_size]], axis=-1)
    return vectors * cosine_table[:, None, :] + turned * sine_table[:, None, :]

def attention(query_matrix, key_rows, value_rows, seq_start):
    seq_len = query_matrix.shape[0]
    rows_per_block = min(512, seq_len)
    block_total = seq_len // rows_per_block
    group_members = QUERY_HEADS // KEY_VALUE_HEADS
    scale = 1.0 / math.sqrt(HEAD_SIZE)
    query_block_list = query_matrix.reshape(block_total, rows_per_block, KEY_VALUE_HEADS, group_members, HEAD_SIZE)
    indices = jnp.arange(seq_len, dtype=jnp.int32)
    row_blocks = indices.reshape(block_total, rows_per_block)
    start_blocks = seq_start.reshape(block_total, rows_per_block)

    @jax.checkpoint
    def one_block(block_in):
        query_blk, query_rows, query_starts = block_in
        scores = jnp.einsum('tgmd,sgd->gmts', query_blk, key_rows, precision=lax.Precision.HIGHEST) * scale
        scores = low_back(scores)
        allowed = (indices[None, :] >= query_starts[:, None]) & (indices[None, :] <= query_rows[:, None])
        masked = jnp.where(allowed, scores, NEGATIVE_FILLER)
        row_max = lax.optimization_barrier(jnp.max(masked, axis=-1, keepdims=True))
        expos = jnp.exp(masked - row_max)
        weights_p = lower_precision(expos / lax.optimization_barrier(jnp.sum(expos, axis=-1, keepdims=True)))
        result = jnp.einsum('gmts,sgd->tgmd', weights_p, value_rows, precision=lax.Precision.HIGHEST)
        return result.reshape(rows_per_block, QUERY_HEADS * HEAD_SIZE)
    mapped = lax.map(one_block, (query_block_list, row_blocks, start_blocks))
    return mapped.reshape(seq_len, QUERY_HEADS * HEAD_SIZE)

def layer(inputs, seq_start, attn_gain, query_key_value_weight, w_out, ffn_gain, w_gate_up, w_down):
    row_total = inputs.shape[0]
    key_value_columns = KEY_VALUE_HEADS * HEAD_SIZE
    rstd_one = lax.rsqrt(lax.optimization_barrier(jnp.mean(inputs * inputs, axis=1, keepdims=True)) + EPS)
    normed_one = lower_precision(inputs * rstd_one * attn_gain[None, :])
    query_key_value_whole = low_back(matmul_hi(normed_one, query_key_value_weight))
    positions = jnp.arange(row_total, dtype=jnp.int32) - seq_start
    cosine_table, sine_table = rope_tables(positions)
    query_matrix = lower_precision(apply_rotary(query_key_value_whole[:, :MODEL_DIM].reshape(row_total, QUERY_HEADS, HEAD_SIZE), cosine_table, sine_table))
    key_rows = lower_precision(apply_rotary(query_key_value_whole[:, MODEL_DIM:MODEL_DIM + key_value_columns].reshape(row_total, KEY_VALUE_HEADS, HEAD_SIZE), cosine_table, sine_table))
    value_rows = lower_precision(query_key_value_whole[:, MODEL_DIM + key_value_columns:].reshape(row_total, KEY_VALUE_HEADS, HEAD_SIZE))
    attended_rows = attention(query_matrix, key_rows, value_rows, seq_start)
    attended_b = lower_precision(low_back(attended_rows))
    hidden_mid = inputs + low_back(matmul_hi(attended_b, w_out))
    rstd_two = lax.rsqrt(lax.optimization_barrier(jnp.mean(hidden_mid * hidden_mid, axis=1, keepdims=True)) + EPS)
    normed_two = lower_precision(hidden_mid * rstd_two * ffn_gain[None, :])
    gate_up = low_back(matmul_hi(normed_two, w_gate_up))
    gate_part = gate_up[:, :FF]
    up_part = gate_up[:, FF:]
    activated = lower_precision(gate_part * jax.nn.sigmoid(gate_part) * up_part)
    return hidden_mid + matmul_hi(activated, w_down)

def reference(tokens, cotangent, starts, attn_gain, query_key_value_weight, w_out, ffn_gain, w_gate_up, w_down):
    params = tuple((weight.astype(jnp.float32) for weight in (attn_gain, query_key_value_weight, w_out, ffn_gain, w_gate_up, w_down)))
    inputs = tokens.astype(jnp.float32).reshape(N_REP, LENGTH, MODEL_DIM)
    cots = cotangent.astype(jnp.float32).reshape(N_REP, LENGTH, MODEL_DIM)
    seq_starts = starts.reshape(N_REP, LENGTH)

    def one_sequence(totals, seq_in):
        seq_tokens, seq_cot, seq_start = seq_in

        def forward(value_rows, *weights):
            return layer(value_rows, seq_start, *weights)
        result, pull_back = jax.vjp(forward, seq_tokens, *params)
        grads = pull_back(seq_cot)
        totals = tuple((first + second for first, second in zip(totals, grads[1:])))
        return (totals, (result, grads[0]))
    zeros_init = tuple((jnp.zeros_like(weight) for weight in params))
    totals, (results, d_inputs) = lax.scan(one_sequence, zeros_init, (inputs, cots, seq_starts))
    return (results.reshape(TOKENS, MODEL_DIM).astype(jnp.bfloat16), d_inputs.reshape(TOKENS, MODEL_DIM).astype(jnp.bfloat16), totals[0], totals[1], totals[2], totals[3], totals[4], totals[5])
```

```python
import math

import jax
import jax.numpy as jnp
from jax import lax
from jax.experimental import pallas as pl
from jax.experimental.pallas import tpu as pltpu
from jax.sharding import Mesh
from jax.sharding import PartitionSpec as P

QUERY_HEADS = 32
KEY_VALUE_HEADS = 4
HEAD_SIZE = 64
GROUP = QUERY_HEADS // KEY_VALUE_HEADS
EPS = 1e-05
ROPE_BASE = 10000.0
NEG = -1e30
BLOCK = 128
CHUNK = 2 * BLOCK
SCALE = 1.0 / math.sqrt(HEAD_SIZE)

AXES = ("zlo", "y", "zhi", "x", "core")
REP = ("zlo", "y")
SHARD = ("zhi", "x", "core")
CHIP = ("zhi", "x")
YZ = ("zlo", "y", "zhi")
YZC = ("zlo", "y", "zhi", "core")
NX = 4

F32 = jnp.float32
BF16 = jnp.bfloat16


def exchange(a, axes):
    return lax.all_to_all(a, axes, split_axis=0, concat_axis=0, tiled=True)


def everywhere(a, axes, n):
    return exchange(jnp.broadcast_to(a[None], (n,) + a.shape), axes)


def swap(a, axis):
    return lax.ppermute(a, axis, [(0, 1), (1, 0)])


def in_order(coord, mine, other, axis):
    return jnp.where(
        coord == 0, jnp.stack([mine, other], axis=axis), jnp.stack([other, mine], axis=axis)
    )


def mm(left, right, dims, out=F32):
    return lax.dot_general(
        left, right, ((dims[0], dims[1]), ((), ())), preferred_element_type=F32
    ).astype(out)


def rms_forward(rows):
    rstd = lax.rsqrt(jnp.mean(rows * rows, axis=1, keepdims=True) + EPS)
    return rows * rstd, rstd


def rms_backward(d_normed, scaled, rstd, gain):
    gain_term = jnp.sum(d_normed * scaled, axis=0)
    inner = d_normed * gain[None, :]
    d_values = rstd * (inner - scaled * jnp.mean(inner * scaled, axis=1, keepdims=True))
    return d_values, gain_term


def heads_to_lanes(ref):
    return jnp.concatenate(
        [ref[HEAD_SIZE * h : HEAD_SIZE * (h + 1), :] for h in range(GROUP)], axis=1
    )


def chunk_slots(c, zhi, core):
    base = ((c // 4) ^ zhi) * 8 + c % 4
    return base + 4 * core, base + 4 * (1 - core)


def allowed_mask(c, st, block):
    keys = lax.broadcasted_iota(jnp.int32, (CHUNK, 1), 0) + c * CHUNK
    lanes = lax.broadcasted_iota(jnp.int32, (1, GROUP * BLOCK), 1) % BLOCK
    return (keys >= st) & (keys <= block * BLOCK + lanes)


def attention_forward(sc, q_ref, cos_ref, sin_ref, st_ref, kv_ref, o_ref, ob_ref, qr_ref, lse_ref):
    b = pl.program_id(0)
    zhi, core, first = sc[0], sc[1], sc[2 + b]
    block = zhi * 8 + 2 * b + core
    cos, sin = cos_ref[...], sin_ref[...]
    turned = []
    for h in range(GROUP):
        u1 = q_ref[HEAD_SIZE * h : HEAD_SIZE * h + 32, :]
        u2 = q_ref[HEAD_SIZE * h + 32 : HEAD_SIZE * h + 64, :]
        turned.append(jnp.concatenate([u1 * cos - u2 * sin, u2 * cos + u1 * sin], axis=0))
    q = jnp.concatenate(turned, axis=1).astype(BF16) * jnp.asarray(SCALE, BF16)
    qr_ref[0] = q
    st = jnp.concatenate([st_ref[0]] * GROUP, axis=1)

    def step(c, state):
        m, l, acc = state
        s0, s1 = chunk_slots(c, zhi, core)
        k = jnp.concatenate([kv_ref[s0, :HEAD_SIZE, :], kv_ref[s1, :HEAD_SIZE, :]], axis=1)
        v = jnp.concatenate([kv_ref[s0, HEAD_SIZE:, :], kv_ref[s1, HEAD_SIZE:, :]], axis=1)
        s = lax.dot_general(k, q, (((0,), (0,)), ((), ())), preferred_element_type=F32)
        s = jnp.where(allowed_mask(c, st, block), s, NEG)
        m2 = jnp.maximum(m, jnp.max(s, axis=0, keepdims=True))
        p = jnp.exp(s - m2)
        al = jnp.exp(m - m2)
        l = l * al + jnp.sum(p, axis=0, keepdims=True)
        acc = acc * al + lax.dot_general(
            v, p.astype(BF16), (((1,), (0,)), ((), ())), preferred_element_type=F32
        )
        return m2, l, acc

    rows = GROUP * BLOCK
    m, l, acc = lax.fori_loop(
        first,
        block // 2 + 1,
        step,
        (
            jnp.full((1, rows), NEG, F32),
            jnp.zeros((1, rows), F32),
            jnp.zeros((HEAD_SIZE, rows), F32),
        ),
    )
    o = acc / l
    for h in range(GROUP):
        part = o[:, BLOCK * h : BLOCK * (h + 1)]
        o_ref[HEAD_SIZE * h : HEAD_SIZE * (h + 1), :] = part
        ob_ref[HEAD_SIZE * h : HEAD_SIZE * (h + 1), :] = part.astype(BF16)
    lse_ref[0] = m + jnp.log(l)


def attention_backward(
    sc, qr_ref, do_ref, o_ref, lse_ref, cos_ref, sin_ref, st_ref, kv_ref, dq_ref, dkv_ref, acc_ref
):
    b = pl.program_id(0)
    zhi, core, first = sc[0], sc[1], sc[2 + b]
    block = zhi * 8 + 2 * b + core

    @pl.when(b == 0)
    def _():
        acc_ref[...] = jnp.zeros_like(acc_ref)

    q = qr_ref[0]
    do = heads_to_lanes(do_ref)
    delta = jnp.sum(do.astype(F32) * heads_to_lanes(o_ref), axis=0, keepdims=True)
    q_rows = q.T
    do_rows = do.T
    lse = lse_ref[0]
    st = jnp.concatenate([st_ref[0]] * GROUP, axis=1)

    def step(c, dq):
        s0, s1 = chunk_slots(c, zhi, core)
        k = jnp.concatenate([kv_ref[s0, :HEAD_SIZE, :], kv_ref[s1, :HEAD_SIZE, :]], axis=1)
        v = jnp.concatenate([kv_ref[s0, HEAD_SIZE:, :], kv_ref[s1, HEAD_SIZE:, :]], axis=1)
        s = lax.dot_general(k, q, (((0,), (0,)), ((), ())), preferred_element_type=F32)
        p = jnp.exp(jnp.where(allowed_mask(c, st, block), s, NEG) - lse)
        dp = lax.dot_general(v, do, (((0,), (0,)), ((), ())), preferred_element_type=F32)
        ds = (p * (dp - delta)).astype(BF16)
        pb = p.astype(BF16)
        dk = jnp.dot(ds, q_rows, preferred_element_type=F32)
        dv = jnp.dot(pb, do_rows, preferred_element_type=F32)
        both = jnp.concatenate([dk, dv], axis=1)
        acc_ref[s0] += both[:BLOCK]
        acc_ref[s1] += both[BLOCK:]
        return dq + jnp.dot(k, ds, preferred_element_type=F32)

    dq = lax.fori_loop(
        first, block // 2 + 1, step, jnp.zeros((HEAD_SIZE, GROUP * BLOCK), F32)
    )
    dq = dq * SCALE
    cos, sin = cos_ref[...], sin_ref[...]
    for h in range(GROUP):
        g1 = dq[:32, BLOCK * h : BLOCK * (h + 1)]
        g2 = dq[32:, BLOCK * h : BLOCK * (h + 1)]
        dq_ref[HEAD_SIZE * h : HEAD_SIZE * h + 32, :] = (g1 * cos + g2 * sin).astype(BF16)
        dq_ref[HEAD_SIZE * h + 32 : HEAD_SIZE * h + 64, :] = (g2 * cos - g1 * sin).astype(BF16)

    @pl.when(b == NX - 1)
    def _():
        for n in range(16):
            dkv_ref[n] = acc_ref[n].T.astype(BF16)


VMEM_LIMIT = 48 * 1024 * 1024


def call_forward(sc, qkv_t, cos, sin, st, kv):
    rows, toks = GROUP * HEAD_SIZE, NX * BLOCK
    lanes = GROUP * BLOCK
    tile = pl.BlockSpec((rows, BLOCK), lambda b, s: (0, b))
    trig = pl.BlockSpec((32, BLOCK), lambda b, s: (0, b))
    return pl.pallas_call(
        attention_forward,
        grid_spec=pltpu.PrefetchScalarGridSpec(
            num_scalar_prefetch=1,
            grid=(NX,),
            in_specs=[
                tile,
                trig,
                trig,
                pl.BlockSpec((1, 1, BLOCK), lambda b, s: (b, 0, 0)),
                pl.BlockSpec((16, BLOCK, BLOCK), lambda b, s: (0, 0, 0)),
            ],
            out_specs=[
                tile,
                tile,
                pl.BlockSpec((1, HEAD_SIZE, lanes), lambda b, s: (b, 0, 0)),
                pl.BlockSpec((1, 1, lanes), lambda b, s: (b, 0, 0)),
            ],
        ),
        out_shape=[
            jax.ShapeDtypeStruct((rows, toks), F32),
            jax.ShapeDtypeStruct((rows, toks), BF16),
            jax.ShapeDtypeStruct((NX, HEAD_SIZE, lanes), BF16),
            jax.ShapeDtypeStruct((NX, 1, lanes), F32),
        ],
        compiler_params=pltpu.CompilerParams(
            dimension_semantics=("arbitrary",), vmem_limit_bytes=VMEM_LIMIT
        ),
        cost_estimate=pl.CostEstimate(
            flops=4 * 512 * 1024 * 512, bytes_accessed=8 << 20, transcendentals=8 << 20
        ),
        name="attention_forward",
    )(sc, qkv_t, cos, sin, st, kv)


def call_backward(sc, qr, do, o, lse, cos, sin, st, kv):
    rows, toks = GROUP * HEAD_SIZE, NX * BLOCK
    lanes = GROUP * BLOCK
    tile = pl.BlockSpec((rows, BLOCK), lambda b, s: (0, b))
    trig = pl.BlockSpec((32, BLOCK), lambda b, s: (0, b))
    whole = pl.BlockSpec((16, BLOCK, BLOCK), lambda b, s: (0, 0, 0))
    return pl.pallas_call(
        attention_backward,
        grid_spec=pltpu.PrefetchScalarGridSpec(
            num_scalar_prefetch=1,
            grid=(NX,),
            in_specs=[
                pl.BlockSpec((1, HEAD_SIZE, lanes), lambda b, s: (b, 0, 0)),
                tile,
                tile,
                pl.BlockSpec((1, 1, lanes), lambda b, s: (b, 0, 0)),
                trig,
                trig,
                pl.BlockSpec((1, 1, BLOCK), lambda b, s: (b, 0, 0)),
                whole,
            ],
            out_specs=[tile, whole],
            scratch_shapes=[pltpu.VMEM((16, BLOCK, BLOCK), F32)],
        ),
        out_shape=[
            jax.ShapeDtypeStruct((rows, toks), BF16),
            jax.ShapeDtypeStruct((16, BLOCK, BLOCK), BF16),
        ],
        compiler_params=pltpu.CompilerParams(
            dimension_semantics=("arbitrary",), vmem_limit_bytes=VMEM_LIMIT
        ),
        cost_estimate=pl.CostEstimate(
            flops=10 * 512 * 1024 * 512, bytes_accessed=8 << 20, transcendentals=8 << 20
        ),
        name="attention_backward",
    )(sc, qr, do, o, lse, cos, sin, st, kv)


def summed_x(part):
    rows = part.shape[0] // NX
    return exchange(part.reshape(NX, rows, -1), "x").astype(F32).sum(axis=0)


def gathered_x(a):
    full = everywhere(a, "x", NX)
    return full.reshape(NX * a.shape[0], *a.shape[1:])


def body(tok, cot, starts, gain_1, w_qkv, w_out, gain_2, w_gu, w_dn):
    zlo, y, zhi, x, core = (lax.axis_index(a) for a in AXES)
    replica = zlo * 4 + y
    rows, dim = tok.shape
    q_cols = GROUP * HEAD_SIZE
    ff_shard = w_dn.shape[0]
    ff = 4 * ff_shard
    slab = rows // 8

    wide = jnp.concatenate(
        [
            w_qkv[:, :dim].reshape(rows, NX, q_cols),
            w_qkv[:, dim : dim + 256].reshape(rows, NX, HEAD_SIZE),
            w_qkv[:, dim + 256 :].reshape(rows, NX, HEAD_SIZE),
        ],
        axis=2,
    ).transpose(1, 0, 2)
    qkv_cols = wide.shape[2]
    wide = jnp.broadcast_to(wide[None], (2,) + wide.shape).reshape(8, rows, qkv_cols)
    wide = exchange(wide, CHIP)
    toks = gathered_x(tok)
    gains = everywhere(jnp.stack([gain_1, gain_2]), SHARD, 16)
    st = gathered_x(starts).reshape(NX, 1, rows)
    wq = in_order(core, wide, swap(wide, "core"), 1).reshape(dim, qkv_cols)
    gain_one = gains[:, 0].reshape(dim).astype(F32)
    gain_two = gains[:, 1].reshape(dim).astype(F32)

    def to_heads(first):
        pairs = []
        for s_zhi in range(2):
            for s_x in range(NX):
                d_zhi = s_x % 2 if first else 1 - s_x % 2
                pairs.append((s_zhi * NX + s_x, d_zhi * NX + 2 * s_zhi + s_x // 2))
        return pairs

    part_a = lax.ppermute(w_out, CHIP, to_heads(True))
    part_b = lax.ppermute(w_out, CHIP, to_heads(False))
    wo = in_order(zhi, part_a, part_b, 0)
    wo = in_order(core, wo, swap(wo, "core"), 1).reshape(q_cols, dim)

    gu_slab = lax.dynamic_slice_in_dim(w_gu, replica * slab, slab, axis=0)
    gu_slab = gu_slab.reshape(slab, 2, 2, NX, 2 * ff_shard).transpose(3, 0, 1, 2, 4)
    gu_slab = exchange(gu_slab.reshape(NX, slab, 2 * ff), "x").reshape(NX * slab, 2 * ff)
    dn_slab = lax.dynamic_slice_in_dim(w_dn, replica * 256, 256, axis=1)
    dn_slab = dn_slab.reshape(11, 32, 256).transpose(1, 0, 2).reshape(32, 2 * ff)
    ffn = lax.all_gather(jnp.concatenate([gu_slab, dn_slab]), YZC, axis=0)
    wgu = ffn[:, : NX * slab].reshape(2, 4, 2, 2, NX, slab, 2 * ff)
    wgu = wgu.transpose(2, 4, 3, 0, 1, 5, 6).reshape(dim, 2 * ff)
    wdn = ffn[:, NX * slab :].reshape(2, 4, 2, 2, 32, 11, 256)
    wdn = wdn.transpose(2, 3, 5, 4, 0, 1, 6).reshape(ff, dim)

    inputs = tok.astype(F32)
    scaled_one, rstd_one = rms_forward(inputs)
    all_scaled, _ = rms_forward(toks.astype(F32))
    n1 = (all_scaled * gain_one[None, :]).astype(BF16)
    qkv_t = mm(wq, n1, ((0,), (1,)))
    block_ids = zhi * 8 + 2 * jnp.arange(NX, dtype=jnp.int32) + core
    where_at = block_ids[:, None] * rows + jnp.arange(rows, dtype=jnp.int32)[None, :]
    pos = (where_at - st[:, 0]).reshape(1, NX * rows).astype(F32)
    freqs = jnp.exp(jnp.arange(32, dtype=F32) * (-2.0 * math.log(ROPE_BASE) / HEAD_SIZE))
    angles = freqs[:, None] * pos
    cos, sin = jnp.cos(angles), jnp.sin(angles)
    k1, k2 = qkv_t[q_cols : q_cols + 32], qkv_t[q_cols + 32 : q_cols + 64]
    kv = jnp.concatenate([k1 * cos - k2 * sin, k2 * cos + k1 * sin, qkv_t[q_cols + 64 :]], axis=0)
    kv = kv.astype(BF16).reshape(2 * HEAD_SIZE, NX, rows).transpose(1, 0, 2)
    kv = jnp.concatenate([kv, swap(kv, "core")], axis=0)
    kv = jnp.concatenate([kv, swap(kv, "zhi")], axis=0)
    firsts = jnp.min(st, axis=(1, 2)) // CHUNK
    sc = jnp.concatenate([zhi[None], core[None], firsts]).astype(jnp.int32)
    o, ob, qr, lse = call_forward(sc, qkv_t, cos, sin, st, kv)
    hidden = inputs + summed_x(mm(ob, wo, ((0,), (0,)), BF16))

    cots = gathered_x(cot)
    scaled_two, rstd_two = rms_forward(hidden)
    n2 = gathered_x((scaled_two * gain_two[None, :]).astype(BF16))
    d_act = mm(cots, wdn, ((1,), (1,)))
    gate_up = mm(n2, wgu, ((1,), (0,)))
    gate, up = gate_up[:, :ff], gate_up[:, ff:]
    sig = jax.nn.sigmoid(gate)
    silu = gate * sig
    act = (silu * up).astype(BF16)
    d_gate = d_act * up * (sig * (1.0 + gate * (1.0 - sig)))
    d_gu = jnp.concatenate([d_gate, d_act * silu], axis=1).astype(BF16)
    d_n2 = summed_x(mm(d_gu, wgu, ((1,), (1,)), BF16))
    mixed = hidden + summed_x(mm(act, wdn, ((1,), (0,)), BF16))

    g_gu = mm(n2, d_gu, ((0,), (0,)), BF16)
    g_dn = mm(act, cots, ((0,), (0,)), BF16)

    def over_tokens(t):
        t = exchange(t, "core").astype(F32).sum(axis=0).astype(BF16)
        return exchange(t, YZ).astype(F32).sum(axis=0).astype(BF16)

    g_gu = g_gu.reshape(2, NX, 2, 2, 4, slab, 2 * ff).transpose(2, 3, 4, 0, 1, 5, 6)
    g_gu = over_tokens(g_gu.reshape(2, 16, NX, slab, 2 * ff))
    g_dn = g_dn.reshape(2, 2, ff_shard, 2, 4, 256).transpose(1, 3, 4, 0, 2, 5)
    g_dn = over_tokens(g_dn.reshape(2, 16, ff_shard, 256))
    g_gu = exchange(g_gu, "x").reshape(NX, slab, 2, 2, 2 * ff_shard)
    g_gu = lax.all_gather(g_gu, REP, axis=0)
    g_gu = g_gu.transpose(0, 2, 3, 4, 1, 5).reshape(rows, w_gu.shape[1]).astype(F32)
    g_dn = lax.all_gather(g_dn, REP, axis=0)
    g_dn = g_dn.transpose(1, 0, 2).reshape(ff_shard, dim).astype(F32)

    d_mid, gain_two_term = rms_backward(d_n2, scaled_two, rstd_two, gain_two)
    d_mid = cot.astype(F32) + d_mid
    d_br = gathered_x(d_mid.astype(BF16))
    do = mm(wo, d_br, ((1,), (1,)), BF16)
    dq, dkv = call_backward(sc, qr, do, o, lse, cos, sin, st, kv)
    g_out = mm(ob, d_br, ((1,), (0,)), BF16)
    dkv = dkv.reshape(2, 2, NX, 2 * HEAD_SIZE, rows)
    dkv = dkv[:, 0].astype(F32) + swap(dkv[:, 1], "core").astype(F32)
    dkv = dkv[0] + swap(dkv[1].astype(BF16), "zhi").astype(F32)
    dkv = dkv.transpose(1, 0, 2).reshape(2 * HEAD_SIZE, NX * rows)
    k1, k2 = dkv[:32], dkv[32:64]
    dkv = jnp.concatenate([k1 * cos + k2 * sin, k2 * cos - k1 * sin, dkv[64:]], axis=0)
    d_qkv = jnp.concatenate([dq, dkv.astype(BF16)], axis=0)
    d_n1 = summed_x(mm(d_qkv, wq, ((0,), (1,)), BF16))
    g_qkv = mm(n1, d_qkv, ((0,), (1,)), BF16)
    d_in, gain_one_term = rms_backward(d_n1, scaled_one, rstd_one, gain_one)
    input_grad = (d_mid + d_in).astype(BF16)

    g_qkv = g_qkv.reshape(2, NX, 2, 2, 4, slab, qkv_cols).transpose(2, 3, 4, 0, 1, 5, 6)
    g_qkv = over_tokens(g_qkv.reshape(2, 16, NX, slab, qkv_cols))
    g_qkv = exchange(g_qkv, "x")
    g_qkv = everywhere(g_qkv, REP, 8).transpose(0, 2, 1, 3).reshape(rows, NX, qkv_cols)
    g_qkv = jnp.concatenate(
        [
            g_qkv[:, :, :q_cols].reshape(rows, dim),
            g_qkv[:, :, q_cols : q_cols + HEAD_SIZE].reshape(rows, 256),
            g_qkv[:, :, q_cols + HEAD_SIZE :].reshape(rows, 256),
        ],
        axis=1,
    ).astype(F32)
    g_out = g_out.reshape(2, 2, rows, 2, 4, 2, 128).transpose(1, 3, 4, 5, 0, 2, 6)
    g_out = over_tokens(g_out.reshape(2, 16, 2, rows, 128))

    def to_owners(first):
        return [(d, s) for s, d in to_heads(first)]

    same = jnp.where(zhi == 0, g_out[0], g_out[1])
    cross = jnp.where(zhi == 0, g_out[1], g_out[0])
    same = lax.ppermute(same, CHIP, to_owners(True))
    cross = lax.ppermute(cross, CHIP, to_owners(False))
    g_out = in_order(x % 2, same, cross, 1).reshape(rows, 256)
    g_out = everywhere(g_out, REP, 8).transpose(1, 0, 2).reshape(rows, dim).astype(F32)

    terms = jnp.stack([gain_one_term, gain_two_term]).reshape(2, 16, rows).transpose(1, 0, 2)
    terms = exchange(terms, SHARD).sum(axis=0)
    terms = everywhere(terms.astype(BF16), REP, 8).astype(F32).sum(axis=0)

    return (
        mixed.astype(BF16),
        input_grad,
        terms[0],
        g_qkv,
        g_out,
        terms[1],
        g_gu,
        g_dn,
    )


def solution(mesh):
    fine = Mesh(mesh.devices.reshape(2, 4, 2, 4, 2), AXES)
    row, two = P(AXES), P(AXES, None)
    vec, mat = P(SHARD), P(SHARD, None)
    return jax.shard_map(
        body,
        mesh=fine,
        in_specs=(two, two, row, vec, mat, mat, vec, mat, mat),
        out_specs=(two, two, vec, mat, mat, vec, mat, mat),
        check_vma=False,
    )
```

```python
import math

import jax
import jax.numpy as jnp
from jax import lax
from jax.experimental import pallas as pl
from jax.experimental.pallas import tpu as pltpu
from jax.sharding import Mesh
from jax.sharding import PartitionSpec as P

QUERY_HEADS = 32
KEY_VALUE_HEADS = 4
HEAD_SIZE = 64
GROUP = QUERY_HEADS // KEY_VALUE_HEADS
EPS = 1e-05
ROPE_BASE = 10000.0
NEG = -1e30
BLOCK = 128
CHUNK = 2 * BLOCK
SCALE = 1.0 / math.sqrt(HEAD_SIZE)

AXES = ("zlo", "y", "zhi", "x", "core")
REP = ("zlo", "y")
SHARD = ("zhi", "x", "core")
CHIP = ("zhi", "x")
YZ = ("zlo", "y", "zhi")
YZC = ("zlo", "y", "zhi", "core")
NX = 4

F32 = jnp.float32
BF16 = jnp.bfloat16


def exchange(a, axes):
    return lax.all_to_all(a, axes, split_axis=0, concat_axis=0, tiled=True)


def everywhere(a, axes, n):
    return exchange(jnp.broadcast_to(a[None], (n,) + a.shape), axes)


def swap(a, axis):
    return lax.ppermute(a, axis, [(0, 1), (1, 0)])


def in_order(coord, mine, other, axis):
    return jnp.where(
        coord == 0, jnp.stack([mine, other], axis=axis), jnp.stack([other, mine], axis=axis)
    )


def mm(left, right, dims, out=F32):
    return lax.dot_general(
        left, right, ((dims[0], dims[1]), ((), ())), preferred_element_type=F32
    ).astype(out)


def rms_forward(rows):
    rstd = lax.rsqrt(jnp.mean(rows * rows, axis=1, keepdims=True) + EPS)
    return rows * rstd, rstd


def rms_backward(d_normed, scaled, rstd, gain):
    gain_term = jnp.sum(d_normed * scaled, axis=0)
    inner = d_normed * gain[None, :]
    d_values = rstd * (inner - scaled * jnp.mean(inner * scaled, axis=1, keepdims=True))
    return d_values, gain_term


def heads_to_lanes(ref):
    return jnp.concatenate(
        [ref[HEAD_SIZE * h : HEAD_SIZE * (h + 1), :] for h in range(GROUP)], axis=1
    )


def chunk_slots(c, zhi, x, core):
    base = ((c // 4) ^ zhi) * 8 + ((c - x) & 3)
    return base + 4 * core, base + 4 * (1 - core)


def allowed_mask(c, st, block):
    keys = lax.broadcasted_iota(jnp.int32, (CHUNK, 1), 0) + c * CHUNK
    lanes = lax.broadcasted_iota(jnp.int32, (1, GROUP * BLOCK), 1) % BLOCK
    return (keys >= st) & (keys <= block * BLOCK + lanes)


def over_chunks(step, state, first, clear, last):
    clear = jnp.minimum(clear, last)
    state = lax.fori_loop(first, clear, lambda c, v: step(c, v, True), state)
    state = lax.fori_loop(clear, last, lambda c, v: step(c, v, False), state)
    return step(last, state, True)


def attention_forward(sc, q_ref, cos_ref, sin_ref, st_ref, kv_ref, o_ref, ob_ref, qr_ref, lse_ref):
    b = pl.program_id(0)
    zhi, x, core, first = sc[0], sc[1], sc[2], sc[3 + b]
    block = zhi * 8 + 2 * ((x + b) & 3) + core
    cos, sin = cos_ref[...], sin_ref[...]
    turned = []
    for h in range(GROUP):
        u1 = q_ref[HEAD_SIZE * h : HEAD_SIZE * h + 32, :]
        u2 = q_ref[HEAD_SIZE * h + 32 : HEAD_SIZE * h + 64, :]
        turned.append(jnp.concatenate([u1 * cos - u2 * sin, u2 * cos + u1 * sin], axis=0))
    q = jnp.concatenate(turned, axis=1).astype(BF16) * jnp.asarray(SCALE, BF16)
    qr_ref[0] = q
    st = jnp.concatenate([st_ref[0]] * GROUP, axis=1)

    def step(c, state, masked):
        m, l, acc = state
        s0, s1 = chunk_slots(c, zhi, x, core)
        k = jnp.concatenate([kv_ref[s0, :HEAD_SIZE, :], kv_ref[s1, :HEAD_SIZE, :]], axis=1)
        v = jnp.concatenate([kv_ref[s0, HEAD_SIZE:, :], kv_ref[s1, HEAD_SIZE:, :]], axis=1)
        s = lax.dot_general(k, q, (((0,), (0,)), ((), ())), preferred_element_type=F32)
        if masked:
            s = jnp.where(allowed_mask(c, st, block), s, NEG)
        m2 = jnp.maximum(m, jnp.max(s, axis=0, keepdims=True))
        p = jnp.exp(s - m2)
        al = jnp.exp(m - m2)
        l = l * al + jnp.sum(p, axis=0, keepdims=True)
        acc = acc * al + lax.dot_general(
            v, p.astype(BF16), (((1,), (0,)), ((), ())), preferred_element_type=F32
        )
        return m2, l, acc

    rows = GROUP * BLOCK
    state = (
        jnp.full((1, rows), NEG, F32),
        jnp.zeros((1, rows), F32),
        jnp.zeros((HEAD_SIZE, rows), F32),
    )
    m, l, acc = over_chunks(step, state, first, sc[7 + b], block // 2)
    o = acc / l
    for h in range(GROUP):
        part = o[:, BLOCK * h : BLOCK * (h + 1)]
        o_ref[HEAD_SIZE * h : HEAD_SIZE * (h + 1), :] = part
        ob_ref[HEAD_SIZE * h : HEAD_SIZE * (h + 1), :] = part.astype(BF16)
    lse_ref[0] = m + jnp.log(l)


def attention_backward(
    sc, qr_ref, do_ref, o_ref, lse_ref, cos_ref, sin_ref, st_ref, kv_ref, dq_ref, dkv_ref, acc_ref
):
    b = pl.program_id(0)
    zhi, x, core, first = sc[0], sc[1], sc[2], sc[3 + b]
    block = zhi * 8 + 2 * ((x + b) & 3) + core

    @pl.when(b == 0)
    def _():
        acc_ref[...] = jnp.zeros_like(acc_ref)

    q = qr_ref[0]
    do = heads_to_lanes(do_ref)
    delta = jnp.sum(do.astype(F32) * heads_to_lanes(o_ref), axis=0, keepdims=True)
    q_rows = q.T
    do_rows = do.T
    lse = lse_ref[0]
    st = jnp.concatenate([st_ref[0]] * GROUP, axis=1)

    def step(c, dq, masked):
        s0, s1 = chunk_slots(c, zhi, x, core)
        k = jnp.concatenate([kv_ref[s0, :HEAD_SIZE, :], kv_ref[s1, :HEAD_SIZE, :]], axis=1)
        v = jnp.concatenate([kv_ref[s0, HEAD_SIZE:, :], kv_ref[s1, HEAD_SIZE:, :]], axis=1)
        s = lax.dot_general(k, q, (((0,), (0,)), ((), ())), preferred_element_type=F32)
        if masked:
            s = jnp.where(allowed_mask(c, st, block), s, NEG)
        p = jnp.exp(s - lse)
        dp = lax.dot_general(v, do, (((0,), (0,)), ((), ())), preferred_element_type=F32)
        ds = (p * (dp - delta)).astype(BF16)
        pb = p.astype(BF16)
        dk = jnp.dot(ds, q_rows, preferred_element_type=F32)
        dv = jnp.dot(pb, do_rows, preferred_element_type=F32)
        both = jnp.concatenate([dk, dv], axis=1)
        acc_ref[s0] += both[:BLOCK]
        acc_ref[s1] += both[BLOCK:]
        return dq + jnp.dot(k, ds, preferred_element_type=F32)

    dq = jnp.zeros((HEAD_SIZE, GROUP * BLOCK), F32)
    dq = over_chunks(step, dq, first, sc[7 + b], block // 2)
    dq = dq * SCALE
    cos, sin = cos_ref[...], sin_ref[...]
    for h in range(GROUP):
        g1 = dq[:32, BLOCK * h : BLOCK * (h + 1)]
        g2 = dq[32:, BLOCK * h : BLOCK * (h + 1)]
        dq_ref[HEAD_SIZE * h : HEAD_SIZE * h + 32, :] = (g1 * cos + g2 * sin).astype(BF16)
        dq_ref[HEAD_SIZE * h + 32 : HEAD_SIZE * h + 64, :] = (g2 * cos - g1 * sin).astype(BF16)

    @pl.when(b == NX - 1)
    def _():
        for n in range(16):
            dkv_ref[n] = acc_ref[n].T.astype(BF16)


VMEM_LIMIT = 48 * 1024 * 1024


def call_forward(sc, qkv_t, cos, sin, st, kv):
    rows, toks = GROUP * HEAD_SIZE, NX * BLOCK
    lanes = GROUP * BLOCK
    tile = pl.BlockSpec((rows, BLOCK), lambda b, s: (0, b))
    trig = pl.BlockSpec((32, BLOCK), lambda b, s: (0, b))
    return pl.pallas_call(
        attention_forward,
        grid_spec=pltpu.PrefetchScalarGridSpec(
            num_scalar_prefetch=1,
            grid=(NX,),
            in_specs=[
                tile,
                trig,
                trig,
                pl.BlockSpec((1, 1, BLOCK), lambda b, s: (b, 0, 0)),
                pl.BlockSpec((16, BLOCK, BLOCK), lambda b, s: (0, 0, 0)),
            ],
            out_specs=[
                tile,
                tile,
                pl.BlockSpec((1, HEAD_SIZE, lanes), lambda b, s: (b, 0, 0)),
                pl.BlockSpec((1, 1, lanes), lambda b, s: (b, 0, 0)),
            ],
        ),
        out_shape=[
            jax.ShapeDtypeStruct((rows, toks), F32),
            jax.ShapeDtypeStruct((rows, toks), BF16),
            jax.ShapeDtypeStruct((NX, HEAD_SIZE, lanes), BF16),
            jax.ShapeDtypeStruct((NX, 1, lanes), F32),
        ],
        compiler_params=pltpu.CompilerParams(
            dimension_semantics=("arbitrary",), vmem_limit_bytes=VMEM_LIMIT
        ),
        cost_estimate=cost(1 << 20, 1 << 16),
        name="attention_forward",
    )(sc, qkv_t, cos, sin, st, kv)


def call_backward(sc, qr, do, o, lse, cos, sin, st, kv):
    rows, toks = GROUP * HEAD_SIZE, NX * BLOCK
    lanes = GROUP * BLOCK
    tile = pl.BlockSpec((rows, BLOCK), lambda b, s: (0, b))
    trig = pl.BlockSpec((32, BLOCK), lambda b, s: (0, b))
    whole = pl.BlockSpec((16, BLOCK, BLOCK), lambda b, s: (0, 0, 0))
    return pl.pallas_call(
        attention_backward,
        grid_spec=pltpu.PrefetchScalarGridSpec(
            num_scalar_prefetch=1,
            grid=(NX,),
            in_specs=[
                pl.BlockSpec((1, HEAD_SIZE, lanes), lambda b, s: (b, 0, 0)),
                tile,
                tile,
                pl.BlockSpec((1, 1, lanes), lambda b, s: (b, 0, 0)),
                trig,
                trig,
                pl.BlockSpec((1, 1, BLOCK), lambda b, s: (b, 0, 0)),
                whole,
            ],
            out_specs=[tile, whole],
            scratch_shapes=[pltpu.VMEM((16, BLOCK, BLOCK), F32)],
        ),
        out_shape=[
            jax.ShapeDtypeStruct((rows, toks), BF16),
            jax.ShapeDtypeStruct((16, BLOCK, BLOCK), BF16),
        ],
        compiler_params=pltpu.CompilerParams(
            dimension_semantics=("arbitrary",), vmem_limit_bytes=VMEM_LIMIT
        ),
        cost_estimate=cost(1 << 20, 1 << 16),
        name="attention_backward",
    )(sc, qr, do, o, lse, cos, sin, st, kv)


def project(
    sc, t0, t1, t2a, t2b, t3, mine, other, cos_ref, sin_ref, n_ref, q_ref, kv_ref, w_ref, gain_ref
):
    for ref, c in ((mine, sc[0]), (other, 1 - sc[0])):
        for chip in range(8):
            at = pl.ds(pl.multiple_of((2 * chip + c) * BLOCK, BLOCK), BLOCK)
            w_ref[at, :] = ref[chip, :BLOCK, :]
            info = ref[chip, BLOCK:, :].astype(F32)
            gain_ref[0:1, at] = info[0:1, :BLOCK]
            gain_ref[1:2, at] = info[0:1, BLOCK : 2 * BLOCK]
    for j, t_refs in enumerate(((t0,), (t1,), (t2a, t2b), (t3,))):
        cols = slice(BLOCK * j, BLOCK * (j + 1))
        v = jnp.concatenate([t[...] for t in t_refs], axis=0).astype(F32)
        rstd = lax.rsqrt(jnp.mean(v * v, axis=1, keepdims=True) + EPS)
        n = (v * rstd * gain_ref[0:1, :]).astype(BF16)
        n_ref[cols, :] = n
        qkv = jnp.dot(n, w_ref[...], preferred_element_type=F32).T
        rows = GROUP * HEAD_SIZE
        q_ref[:, cols] = qkv[:rows]
        cos, sin = cos_ref[:, cols], sin_ref[:, cols]
        k1, k2 = qkv[rows : rows + 32], qkv[rows + 32 : rows + 64]
        kv_ref[j, :32, :] = (k1 * cos - k2 * sin).astype(BF16)
        kv_ref[j, 32:64, :] = (k2 * cos + k1 * sin).astype(BF16)
        kv_ref[j, 64:, :] = qkv[rows + 64 :].astype(BF16)


def params(*semantics):
    return pltpu.CompilerParams(
        dimension_semantics=semantics or None, vmem_limit_bytes=VMEM_LIMIT
    )


def cost(flops, moved):
    return pl.CostEstimate(flops=flops, bytes_accessed=moved, transcendentals=0)


def call_project(sc, toks, mine, other, cos, sin):
    dim, cols = toks[0].shape[1], mine.shape[2]
    vmem = pl.BlockSpec(memory_space=pltpu.VMEM)
    return pl.pallas_call(
        project,
        in_specs=[pl.BlockSpec(memory_space=pltpu.SMEM)] + [vmem] * 9,
        out_specs=[vmem] * 5,
        out_shape=[
            jax.ShapeDtypeStruct((NX * BLOCK, dim), BF16),
            jax.ShapeDtypeStruct((GROUP * HEAD_SIZE, NX * BLOCK), F32),
            jax.ShapeDtypeStruct((NX, 2 * HEAD_SIZE, BLOCK), BF16),
            jax.ShapeDtypeStruct((dim, cols), BF16),
            jax.ShapeDtypeStruct((2, dim), F32),
        ],
        compiler_params=params(),
        cost_estimate=cost(1 << 20, 1 << 16),
        name="project",
    )(sc, *toks, mine, other, cos, sin)


def out_project(sc, o_ref, a_ref, b_ref, a2_ref, b2_ref, p0, p1, p2, p3, w_ref):
    first, core = sc[0], sc[1]
    for ref, p, c in (
        (a_ref, first, core),
        (b_ref, 1 - first, core),
        (a2_ref, first, 1 - core),
        (b2_ref, 1 - first, 1 - core),
    ):
        w_ref[pl.ds(pl.multiple_of((2 * p + c) * BLOCK, BLOCK), BLOCK), :] = ref[...]
    for half in range(2):
        at = slice(1024 * half, 1024 * (half + 1))
        d = lax.dot_general(
            o_ref[...], w_ref[:, at], (((0,), (0,)), ((), ())), preferred_element_type=F32
        ).astype(BF16)
        for j, p in enumerate((p0, p1, p2, p3)):
            p[:, at] = d[BLOCK * j : BLOCK * (j + 1)]


def call_out_project(sc, o, *w):
    vmem = pl.BlockSpec(memory_space=pltpu.VMEM)
    return pl.pallas_call(
        out_project,
        in_specs=[pl.BlockSpec(memory_space=pltpu.SMEM)] + [vmem] * 5,
        out_specs=[vmem] * 5,
        out_shape=[jax.ShapeDtypeStruct((BLOCK, 2048), BF16)] * 4
        + [jax.ShapeDtypeStruct((4 * BLOCK, 2048), BF16)],
        compiler_params=params(),
        cost_estimate=cost(1 << 20, 1 << 16),
        name="out_project",
    )(sc, o, *w)


def spread(in_ref, gu_ref, dn_ref, qkv_ref, out_ref, terms_ref):
    for x in range(NX):
        for half in range(2):
            at, to = FF_TILE * (2 * x + half), FF_TILE * (4 * half + x)
            gu_ref[:, to : to + FF_TILE] = in_ref[0, :, at : at + FF_TILE].astype(F32)
    base = 8 * FF_TILE
    for t in range(22):
        at = base + 2 * FF_TILE * (t % 2) + 256 * (t // 2)
        dn_ref[16 * t : 16 * (t + 1), :] = in_ref[0, :, at : at + 256].astype(F32)
    base += 4 * FF_TILE
    k, v = [], []
    for x in range(NX):
        at = base + 640 * x
        qkv_ref[:, 512 * x : 512 * (x + 1)] = in_ref[0, :, at : at + 512].astype(F32)
        k.append(in_ref[0, :, at + 512 : at + 576].astype(F32))
        v.append(in_ref[0, :, at + 576 : at + 640].astype(F32))
    qkv_ref[:, 2048:2304] = jnp.concatenate(k, axis=1)
    qkv_ref[:, 2304:] = jnp.concatenate(v, axis=1)
    base += 640 * NX
    for t in range(8):
        at = base + 256 * t
        out_ref[16 * t : 16 * (t + 1), :] = in_ref[0, :, at : at + 256].astype(F32)
    base += 2048
    row = in_ref[0, :, base : base + 256].astype(F32)
    terms = jnp.concatenate([row[0:1, :BLOCK], row[0:1, BLOCK:]], axis=0)

    @pl.when(pl.program_id(0) == 0)
    def _():
        terms_ref[...] = terms

    @pl.when(pl.program_id(0) > 0)
    def _():
        terms_ref[...] += terms


def call_spread(both):
    return pl.pallas_call(
        spread,
        grid=(8,),
        in_specs=[pl.BlockSpec((1, 16, both.shape[2]), lambda r: (r, 0, 0))],
        out_specs=[
            pl.BlockSpec((16, 8 * FF_TILE), lambda r: (r, 0)),
            pl.BlockSpec((352, 256), lambda r: (0, r)),
            pl.BlockSpec((16, 2560), lambda r: (r, 0)),
            pl.BlockSpec((BLOCK, 256), lambda r: (0, r)),
            pl.BlockSpec((2, BLOCK), lambda r: (0, 0)),
        ],
        out_shape=[
            jax.ShapeDtypeStruct((BLOCK, 8 * FF_TILE), F32),
            jax.ShapeDtypeStruct((352, 2048), F32),
            jax.ShapeDtypeStruct((BLOCK, 2560), F32),
            jax.ShapeDtypeStruct((BLOCK, 2048), F32),
            jax.ShapeDtypeStruct((2, BLOCK), F32),
        ],
        compiler_params=params("arbitrary"),
        cost_estimate=cost(1 << 20, 1 << 16),
        name="spread",
    )(both)


FF_TILE = 1408


def pack(sc, w_ref, g1_ref, g2_ref, st_ref, gu_ref, dn_ref, wide_ref, gus_ref, dns_ref):
    st = st_ref[...]
    info = [g1_ref[...].astype(F32), g2_ref[...].astype(F32)]
    info += [(st // 256).astype(F32), (st % 256).astype(F32), jnp.zeros((1, BLOCK), F32)]
    info = jnp.broadcast_to(jnp.concatenate(info, axis=1), (16, 5 * BLOCK)).astype(BF16)
    for x in range(NX):
        j = (x - sc[1]) & 3
        k = w_ref[:, 2048 + 64 * x : 2048 + 64 * (x + 1)]
        v = w_ref[:, 2304 + 64 * x : 2304 + 64 * (x + 1)]
        kv = jnp.concatenate([k, v], axis=1)
        for zhi in range(2):
            wide_ref[NX * zhi + x, :BLOCK, :512] = w_ref[:, 512 * x : 512 * (x + 1)]
            wide_ref[NX * zhi + x, :BLOCK, 512:] = kv
            wide_ref[NX * zhi + x, BLOCK:, :] = info
        gus_ref[j, :, :FF_TILE] = gu_ref[:, FF_TILE * x : FF_TILE * (x + 1)]
        up = 4 * FF_TILE + FF_TILE * x
        gus_ref[j, :, FF_TILE:] = gu_ref[:, up : up + FF_TILE]
    for j in range(11):
        dns_ref[:, 256 * j : 256 * (j + 1)] = dn_ref[32 * j : 32 * (j + 1), :]


def call_pack(sc, w_qkv, gain_1, gain_2, starts, w_gu, w_dn):
    vec = pl.BlockSpec((1, BLOCK), lambda i, s: (0, 0))
    return pl.pallas_call(
        pack,
        grid_spec=pltpu.PrefetchScalarGridSpec(
            num_scalar_prefetch=1,
            grid=(1,),
            in_specs=[
                pl.BlockSpec((BLOCK, 2560), lambda i, s: (0, 0)),
                vec,
                vec,
                vec,
                pl.BlockSpec((16, 8 * FF_TILE), lambda i, s: (s[0], 0)),
                pl.BlockSpec((352, 256), lambda i, s: (0, s[0])),
            ],
            out_specs=[
                pl.BlockSpec((8, BLOCK + 16, 640), lambda i, s: (0, 0, 0)),
                pl.BlockSpec((NX, 16, 2 * FF_TILE), lambda i, s: (0, 0, 0)),
                pl.BlockSpec((32, 2 * FF_TILE), lambda i, s: (0, 0)),
            ],
        ),
        out_shape=[
            jax.ShapeDtypeStruct((8, BLOCK + 16, 640), BF16),
            jax.ShapeDtypeStruct((NX, 16, 2 * FF_TILE), BF16),
            jax.ShapeDtypeStruct((32, 2 * FF_TILE), BF16),
        ],
        compiler_params=params("arbitrary"),
        cost_estimate=cost(1 << 20, 1 << 16),
        name="pack",
    )(sc, w_qkv, gain_1[None], gain_2[None], starts[None], w_gu, w_dn)


def down_back(c0, c1, c2, c3, w_ref, d_ref, wdn_ref):
    r = pl.program_id(0)
    for p in range(2):
        for c in range(2):
            for j in range(11):
                at = (2 * p + c) * 352 + 32 * j
                wdn_ref[at : at + 32, :] = w_ref[0, p, c, :, 256 * j : 256 * (j + 1)]
    cots = jnp.concatenate([c0[...], c1[...], c2[...], c3[...]], axis=0)
    part = lax.dot_general(
        cots, wdn_ref[...], (((1,), (1,)), ((), ())), preferred_element_type=F32
    )

    @pl.when(r == 0)
    def _():
        d_ref[...] = part

    @pl.when(r > 0)
    def _():
        d_ref[...] += part


def call_down_back(cots, ffn):
    return pl.pallas_call(
        down_back,
        grid=(8,),
        in_specs=[pl.BlockSpec((BLOCK, 256), lambda r: (0, r))] * 4
        + [pl.BlockSpec((1, 2, 2, 32, 2 * FF_TILE), lambda r: (r, 0, 0, 2, 0))],
        out_specs=[
            pl.BlockSpec((NX * BLOCK, FF_TILE), lambda r: (0, 0)),
            pl.BlockSpec((FF_TILE, 256), lambda r: (0, r)),
        ],
        out_shape=[
            jax.ShapeDtypeStruct((NX * BLOCK, FF_TILE), F32),
            jax.ShapeDtypeStruct((FF_TILE, 2048), BF16),
        ],
        compiler_params=params("arbitrary"),
        cost_estimate=cost(1 << 33, 1 << 20),
        name="down_back",
    )(*cots, ffn)


def natural(w_ref, pick, me):
    parts = []
    for zhi, x, c in pick:
        at = pl.ds(pl.multiple_of(((me - x) & 3) * 16, 16), 16)
        parts.append(w_ref[:, zhi, c, at, :].reshape(BLOCK, BLOCK))
    return jnp.concatenate(parts, axis=0)


ORDER = [(zhi, x, c) for zhi in range(2) for x in range(NX) for c in range(2)]
FF_STEPS = FF_TILE // BLOCK


def feed_forward(
    sc, n0, n1, n2, n3, wg_ref, wu_ref, w_ref, d_ref, o0, o1, o2, o3, act_ref, dgu_ref, n_s, act_s, dg_s
):
    k = pl.program_id(0)

    @pl.when(k == 0)
    def _():
        for j, n in enumerate((n0, n1, n2, n3)):
            n_s[BLOCK * j : BLOCK * (j + 1), :] = n[...]

    @pl.when(k < FF_STEPS)
    def _():
        w = [natural(ref, ORDER, sc[0]) for ref in (wg_ref, wu_ref)]
        w = jnp.concatenate(w, axis=1)
        both = jnp.dot(n_s[...], w, preferred_element_type=F32)
        gate, up = both[:, :BLOCK], both[:, BLOCK:]
        d_act = d_ref[...]
        sig = 1.0 / (1.0 + jnp.exp(-gate))
        silu = gate * sig
        at = pl.ds(pl.multiple_of(k * BLOCK, BLOCK), BLOCK)
        up_at = pl.ds(pl.multiple_of(FF_TILE + k * BLOCK, BLOCK), BLOCK)
        act_s[:, at] = (silu * up).astype(BF16)
        d_gate = d_act * up * (sig * (1.0 + gate * (1.0 - sig)))
        dg_s[:, at] = d_gate.astype(BF16)
        dg_s[:, up_at] = (d_act * silu).astype(BF16)

    @pl.when(k == FF_STEPS)
    def _():
        act_ref[...] = act_s[...]
        dgu_ref[...] = dg_s[...]

    @pl.when(k >= FF_STEPS)
    def _():
        w = jnp.concatenate(
            [w_ref[:, 0, c].reshape(BLOCK, 2 * FF_TILE) for c in range(2)], axis=0
        )
        d = lax.dot_general(
            dg_s[...], w, (((1,), (1,)), ((), ())), preferred_element_type=F32
        ).astype(BF16)
        for j, o in enumerate((o0, o1, o2, o3)):
            o[...] = d[BLOCK * j : BLOCK * (j + 1)]


def call_feed_forward(x, n2, ffn, d_act):
    def tile(k):
        return jnp.minimum(k, FF_STEPS - 1)

    def later(k):
        return jnp.maximum(k - FF_STEPS, 0)

    def row_block(k, s):
        return (0, later(k) >> 2, 0, (s[0] - later(k)) & 3, 0)

    whole = pl.BlockSpec((BLOCK, 2048), lambda k, s: (0, 0))
    out = pl.BlockSpec((BLOCK, 256), lambda k, s: (0, later(k)))
    return pl.pallas_call(
        feed_forward,
        grid_spec=pltpu.PrefetchScalarGridSpec(
            num_scalar_prefetch=1,
            grid=(FF_STEPS + 8,),
            in_specs=[whole] * 4
            + [
                pl.BlockSpec((8, 2, 2, 64, BLOCK), lambda k, s: (0, 0, 0, 0, tile(k))),
                pl.BlockSpec((8, 2, 2, 64, BLOCK), lambda k, s: (0, 0, 0, 0, FF_STEPS + tile(k))),
                pl.BlockSpec((8, 1, 2, 16, 2 * FF_TILE), row_block),
                pl.BlockSpec((NX * BLOCK, BLOCK), lambda k, s: (0, tile(k))),
            ],
            out_specs=[out] * 4
            + [
                pl.BlockSpec((NX * BLOCK, FF_TILE), lambda k, s: (0, 0)),
                pl.BlockSpec((NX * BLOCK, 2 * FF_TILE), lambda k, s: (0, 0)),
            ],
            scratch_shapes=[
                pltpu.VMEM((NX * BLOCK, 2048), BF16),
                pltpu.VMEM((NX * BLOCK, FF_TILE), BF16),
                pltpu.VMEM((NX * BLOCK, 2 * FF_TILE), BF16),
            ],
        ),
        out_shape=[jax.ShapeDtypeStruct((BLOCK, 2048), BF16)] * 4
        + [
            jax.ShapeDtypeStruct((NX * BLOCK, FF_TILE), BF16),
            jax.ShapeDtypeStruct((NX * BLOCK, 2 * FF_TILE), BF16),
        ],
        compiler_params=params("arbitrary"),
        cost_estimate=cost(1 << 20, 1 << 16),
        name="feed_forward",
    )(x[None], *n2, ffn, ffn, ffn, d_act)


def ffn_grads(sc, n0, n1, n2, n3, dgu_ref, act_ref, c0, c1, c2, c3, *rest):
    i = pl.program_id(0)
    added, outs, act_t, g_ref = rest[:-4], rest[-4:-2], rest[-2], rest[-1]

    def put(which, place, value):
        if added:
            value = value + added[which][place].astype(F32)
        outs[which][place] = value.astype(BF16)

    @pl.when(i < NX)
    def _():
        lhs = []
        for zhi in range(2):
            shard = (zhi * NX + jnp.minimum(i, NX - 1)) * 2 + sc[0]
            at = pl.ds(pl.multiple_of(shard * BLOCK, BLOCK), BLOCK)
            lhs.append(jnp.concatenate([n[:, at] for n in (n0, n1, n2, n3)], axis=0))
        lhs = jnp.concatenate(lhs, axis=1)
        for half in range(2):
            cols = slice(FF_TILE * half, FF_TILE * (half + 1))
            g_ref[:, :FF_TILE] = lax.dot_general(
                lhs, dgu_ref[:, cols], (((0,), (0,)), ((), ())), preferred_element_type=F32
            )
            for zhi in range(2):
                for zlo in range(2):
                    for y in range(4):
                        row = zhi * BLOCK + (zlo * 4 + y) * 16
                        part = g_ref[row : row + 16, :FF_TILE]
                        put(0, (y, zlo * 2 + zhi, slice(None), cols), part)

    @pl.when(i == NX)
    def _():
        act_t[...] = act_ref[...].T

    @pl.when(i >= NX)
    def _():
        lhs = []
        for p in range(2):
            for j in range(11):
                row = (2 * p + sc[0]) * 352 + 32 * j + 16 * (i - NX)
                lhs.append(act_t[pl.ds(pl.multiple_of(row, 16), 16), :])
        lhs = jnp.concatenate(lhs, axis=0)
        for zlo in range(2):
            cols = slice(1024 * zlo, 1024 * (zlo + 1))
            cots = jnp.concatenate([c[:, cols] for c in (c0, c1, c2, c3)], axis=0)
            g = jnp.dot(lhs, cots, preferred_element_type=F32)
            for p in range(2):
                for j in range(11):
                    row = p * 176 + 16 * j
                    for y in range(4):
                        part = g[row : row + 16, 256 * y : 256 * (y + 1)]
                        to = slice(256 * j, 256 * (j + 1))
                        put(1, (zlo * 2 + p, y, slice(None), to), part)


def call_ffn_grads(core, n2, d_gu, act, cots, *added):
    const = pl.BlockSpec((BLOCK, 2048), lambda i, s: (0, 0))
    tile = (4, 4, 16, 2 * FF_TILE)
    outs = [
        pl.BlockSpec(tile, lambda i, s: (0, 0, jnp.minimum(i, NX - 1), 0)),
        pl.BlockSpec(tile, lambda i, s: (0, 0, jnp.maximum(i - NX, 0), 0)),
    ]
    return pl.pallas_call(
        ffn_grads,
        grid_spec=pltpu.PrefetchScalarGridSpec(
            num_scalar_prefetch=1,
            grid=(NX + 2,),
            in_specs=[const] * 4
            + [pl.BlockSpec((NX * BLOCK, 2 * FF_TILE), lambda i, s: (0, 0))]
            + [pl.BlockSpec((NX * BLOCK, FF_TILE), lambda i, s: (0, 0))]
            + [const] * 4
            + outs[: len(added)],
            out_specs=outs,
            scratch_shapes=[
                pltpu.VMEM((FF_TILE, NX * BLOCK), BF16),
                pltpu.VMEM((2 * BLOCK, FF_TILE), F32),
            ],
        ),
        out_shape=[
            jax.ShapeDtypeStruct((4, 4, 64, 2 * FF_TILE), BF16),
            jax.ShapeDtypeStruct((4, 4, 32, 2 * FF_TILE), BF16),
        ],
        compiler_params=params("arbitrary"),
        cost_estimate=cost(1 << 33, 1 << 20),
        name="ffn_grads_mine" if added else "ffn_grads_other",
    )(core[None], *n2, d_gu, act, *cots, *added)


def attention_grads(sc, n_ref, dq_ref, o_ref, db_ref, *rest):
    added, out_ref, qkv_s, out_s = rest[:-3], rest[-3], rest[-2], rest[-1]

    def put(place, value):
        if added:
            value = value + added[0][place].astype(F32)
        out_ref[place] = value.astype(BF16)

    for zhi in range(2):
        lhs = []
        for x in range(NX):
            at = pl.ds(pl.multiple_of(((zhi * NX + x) * 2 + sc[0]) * BLOCK, BLOCK), BLOCK)
            lhs.append(n_ref[:, at])
        lhs = jnp.concatenate(lhs, axis=1)
        qkv_s[...] = lax.dot_general(
            lhs, dq_ref[...], (((0,), (1,)), ((), ())), preferred_element_type=F32
        )
        for x in range(NX):
            for replica in range(8):
                row = BLOCK * x + 16 * replica
                to = slice(16 * x, 16 * (x + 1))
                put((replica % 4, replica // 4 * 2 + zhi, to, slice(0, 640)), qkv_s[row : row + 16, :])
    for p in range(2):
        rows = o_ref[pl.ds(pl.multiple_of((2 * p + sc[0]) * BLOCK, BLOCK), BLOCK), :]
        out_s[...] = jnp.dot(rows, db_ref[...], preferred_element_type=F32)
        for replica in range(8):
            for half in range(2):
                part = out_s[64 * half : 64 * (half + 1), 256 * replica : 256 * (replica + 1)]
                at = 640 + 256 * half
                put((replica % 4, replica // 4 * 2 + p, slice(None), slice(at, at + 256)), part)


def call_attention_grads(core, n1, d_qkv, ob, d_br, *added):
    vmem = pl.BlockSpec(memory_space=pltpu.VMEM)
    return pl.pallas_call(
        attention_grads,
        in_specs=[pl.BlockSpec(memory_space=pltpu.SMEM)] + [vmem] * (4 + len(added)),
        out_specs=vmem,
        out_shape=jax.ShapeDtypeStruct((4, 4, 64, 1152), BF16),
        scratch_shapes=[pltpu.VMEM((4 * BLOCK, 640), F32), pltpu.VMEM((BLOCK, 2048), F32)],
        compiler_params=params(),
        cost_estimate=cost(1 << 33, 1 << 20),
        name="attention_grads_mine" if added else "attention_grads_other",
    )(core[None], n1, d_qkv, ob, d_br, *added)


def shift_x(a, k):
    return lax.ppermute(a, "x", [(i, (i + k) % NX) for i in range(NX)])


def gathered_x(a, between=lambda: ()):
    half = a.shape[0] // 2
    t1, t3 = shift_x(a, 3), shift_x(a, 1)
    t1, t3 = lax.optimization_barrier((t1, t3, *between()))[:2]
    return [a, t1, jnp.concatenate([shift_x(t1[:half], 3), shift_x(t3[half:], 1)]), t3]


def moved_x(parts):
    half = parts[2].shape[0] // 2
    up, down = shift_x(parts[2][:half], 1), shift_x(parts[2][half:], 3)
    up = (parts[1][:half].astype(F32) + up.astype(F32)).astype(BF16)
    down = (parts[3][half:].astype(F32) + down.astype(F32)).astype(BF16)
    up = jnp.concatenate([up, parts[1][half:]])
    down = jnp.concatenate([parts[3][:half], down])
    return [parts[0], shift_x(up, 1), shift_x(down, 3)]


def added(parts):
    return sum(p.astype(F32) for p in parts)


def summed_x(parts):
    return added(moved_x(parts))


def sent(parts, axes, me=0):
    out = []
    for j in range(4):
        part = lax.dynamic_index_in_dim(parts, (me + j) % 4, 0, keepdims=False)
        out.append(lax.ppermute(part, axes, [(i, (i + j) % 4) for i in range(4)]) if j else part)
    return out


def total(parts):
    return parts.astype(F32).sum(axis=0).astype(BF16)


def pieces(a):
    return [a[BLOCK * j : BLOCK * (j + 1)] for j in range(NX)]


def summed(t, axes):
    return exchange(t, axes).astype(F32).sum(axis=0).astype(BF16)


def to_heads(first):
    pairs = []
    for s_zhi in range(2):
        for s_x in range(NX):
            d_zhi = s_x % 2 if first else 1 - s_x % 2
            pairs.append((s_zhi * NX + s_x, d_zhi * NX + 2 * s_zhi + s_x // 2))
    return pairs


def to_owners(first):
    return [(d, s) for s, d in to_heads(first)]


def after(a, *others):
    return lax.optimization_barrier((a, *others))[0]


def body(tok, cot, starts, gain_1, w_qkv, w_out, gain_2, w_gu, w_dn):
    zlo, y, zhi, x, core = (lax.axis_index(a) for a in AXES)
    replica = zlo * 4 + y
    rows, dim = tok.shape
    q_cols = GROUP * HEAD_SIZE
    ff_shard = w_dn.shape[0]
    slab = rows // 8

    t1, t3 = shift_x(tok, 3), shift_x(tok, 1)
    toks = [tok, t1, shift_x(t1[: rows // 2], 3), shift_x(t3[rows // 2 :], 1), t3]
    w_far = swap(w_out, "zhi")
    place = jnp.stack([replica, x])
    wide, gu_slab, dn_slab = call_pack(place, w_qkv, gain_1, gain_2, starts, w_gu, w_dn)
    qkv_cols = wide.shape[2]
    wide = exchange(wide, CHIP)

    gu_slab = jnp.concatenate(sent(gu_slab, "x"), axis=0)
    dn_slab = lax.ppermute(dn_slab, CHIP, to_heads(True))
    slabs = jnp.concatenate([gu_slab, dn_slab])
    slabs = after(slabs, wide, t1, t3)
    ffn = lax.all_gather(slabs, YZC, axis=0)
    ffn = ffn.reshape(8, 2, 2, NX * slab + 32, 2 * FF_TILE)

    inputs = tok.astype(F32)
    scaled_one, rstd_one = rms_forward(inputs)
    blocks = (x + jnp.arange(NX, dtype=jnp.int32)) % NX
    block_ids = zhi * 8 + 2 * blocks + core
    st = lax.dynamic_slice_in_dim(wide, zhi * NX, NX, 0)[:, rows, 2 * rows : 4 * rows]
    st = st.astype(F32).reshape(NX, 2, rows)
    st = (st[:, 0] * 256.0 + st[:, 1]).astype(jnp.int32)[blocks]
    where_at = block_ids[:, None] * rows + jnp.arange(rows, dtype=jnp.int32)[None, :]
    pos = (where_at - st).reshape(1, NX * rows).astype(F32)
    freqs = jnp.exp(jnp.arange(32, dtype=F32) * (-2.0 * math.log(ROPE_BASE) / HEAD_SIZE))
    angles = freqs[:, None] * pos
    cos, sin = jnp.cos(angles), jnp.sin(angles)
    n1, q_t, kv, wq, gains = call_project(core[None], toks, wide, swap(wide, "core"), cos, sin)
    gain_one, gain_two = gains[0], gains[1]
    kv = jnp.concatenate([kv, swap(kv, "core")], axis=0)
    near, far = jnp.where(zhi == 0, w_out, w_far), jnp.where(zhi == 0, w_far, w_out)
    even = x % 2 == 0
    part_a, part_b = jnp.where(even, near, far), jnp.where(even, far, near)
    part_a, part_b, cot_in = lax.optimization_barrier((part_a, part_b, cot, kv))[:3]
    kv = jnp.concatenate([kv, swap(kv, "zhi")], axis=0)
    part_a = lax.ppermute(part_a, "x", [(0, 0), (1, 2), (2, 1), (3, 3)])
    part_b = lax.ppermute(part_b, "x", [(0, 2), (1, 0), (2, 3), (3, 1)])
    firsts = jnp.min(st, axis=1) // CHUNK
    clears = (jnp.max(st, axis=1) + CHUNK - 1) // CHUNK
    sc = jnp.concatenate([zhi[None], x[None], core[None], firsts, clears]).astype(jnp.int32)
    st = st[:, None, :]
    o, ob, qr, lse = call_forward(sc, q_t, cos, sin, st, kv)
    cots = [cot_in, shift_x(cot_in, 3), shift_x(cot_in, 2), shift_x(cot_in, 1)]
    ob, *cots = lax.optimization_barrier((ob, *cots))
    part_a, part_b = after(part_a, ob), after(part_b, ob)
    *parts, wo = call_out_project(
        jnp.stack([x // 2, core]), ob, part_a, part_b, swap(part_a, "core"), swap(part_b, "core")
    )
    hidden = inputs + summed_x(parts)

    d_act, wdn = call_down_back(cots, ffn)
    scaled_two, rstd_two = rms_forward(hidden)
    n2 = gathered_x((scaled_two * gain_two[None, :]).astype(BF16))
    *d_n2, act, d_gu = call_feed_forward(x, n2, ffn, d_act)

    other = call_ffn_grads(1 - core, n2, d_gu, act, cots)
    d_n2 = moved_x(d_n2)
    other = lax.optimization_barrier((*other, *d_n2[1:]))[:2]
    other = [swap(g, "core") for g in other]
    g_gu, g_dn = call_ffn_grads(core, n2, d_gu, act, cots, *other)
    d_mid, gain_two_term = rms_backward(added(d_n2), scaled_two, rstd_two, gain_two)
    d_mid = cot.astype(F32) + d_mid
    d_br = gathered_x(d_mid.astype(BF16), lambda: (g_gu, g_dn))
    z = zlo * 2 + zhi
    g_gu = exchange(g_gu.reshape(4, 4 * 64, 2 * FF_TILE), "y")
    g_dn = sent(g_dn, ("zlo", "zhi"), z)
    d_br = jnp.concatenate(d_br)

    do = mm(wo, d_br, ((1,), (1,)), BF16)
    dq, dkv = call_backward(sc, qr, do, o, lse, cos, sin, st, kv)
    dkv, *g_dn = lax.optimization_barrier((dkv, *g_dn))
    dkv = dkv.reshape(2, 2, NX, 2 * HEAD_SIZE, rows)
    dkv = dkv[:, 0].astype(F32) + swap(dkv[:, 1], "core").astype(F32)
    dkv = dkv[0] + swap(dkv[1].astype(BF16), "zhi").astype(F32)
    g_dn = added(g_dn).astype(BF16)
    dkv = dkv.transpose(1, 0, 2).reshape(2 * HEAD_SIZE, NX * rows)
    k1, k2 = dkv[:32], dkv[32:64]
    dkv = jnp.concatenate([k1 * cos + k2 * sin, k2 * cos - k1 * sin, dkv[64:]], axis=0)
    d_qkv = jnp.concatenate([dq, dkv.astype(BF16)], axis=0)
    d_qkv, g_gu = lax.optimization_barrier((d_qkv, g_gu))
    g_gu = exchange(total(g_gu.reshape(4, 4, 64, 2 * FF_TILE)), ("zlo", "zhi"))
    d_n1 = mm(d_qkv, wq, ((0,), (1,)), BF16)
    d_qkv, ob, g_dn = lax.optimization_barrier((d_qkv, ob, g_dn, d_n1))[:3]
    d_n1 = moved_x(pieces(d_n1))
    other = swap(call_attention_grads(1 - core, n1, d_qkv, ob, d_br), "core")
    g_attn = call_attention_grads(core, n1, d_qkv, ob, d_br, other)
    g_dn = sent(g_dn, "y", y)

    g_gu = after(g_gu, g_attn)
    g_attn = sent(g_attn, "y", y)
    d_n1 = lax.optimization_barrier((*d_n1, *g_attn))[:3]
    act = after(act, *d_n1)
    mixed = moved_x(pieces(mm(act, wdn, ((1,), (0,)), BF16)))
    d_in, gain_one_term = rms_backward(added(d_n1), scaled_one, rstd_one, gain_one)
    input_grad = (d_mid + d_in).astype(BF16)
    g_attn = sent(added(g_attn).astype(BF16), ("zlo", "zhi"), z)
    g_gu = exchange(total(g_gu).reshape(NX, slab, 2 * FF_TILE), "x")
    g_dn = lax.ppermute(added(g_dn).astype(BF16), CHIP, to_owners(True))
    both = [g_gu[j] for j in range(NX)] + [g_dn[:slab], g_dn[slab:]]
    g_attn = added(g_attn).astype(BF16)
    g_out = lax.ppermute(g_attn[:, 640:], CHIP, to_owners(True))
    g_out = [g_out[slab * j : slab * (j + 1), 256 * h : 256 * h + 256] for h in (0, 1) for j in range(4)]
    g_qkv = exchange(g_attn[:, :640].reshape(NX, slab, qkv_cols), "x")
    terms = jnp.stack([gain_one_term, gain_two_term]).reshape(2, 16, rows).transpose(1, 0, 2)
    terms = exchange(terms, SHARD).sum(axis=0).reshape(1, 2 * rows)
    terms = jnp.broadcast_to(terms, (slab, 2 * rows)).astype(BF16)
    both += [g_qkv[j] for j in range(NX)] + g_out + [terms]
    both = lax.all_gather(jnp.concatenate(both, axis=1), REP, axis=0)
    g_gu, g_dn, g_qkv, g_out, terms = call_spread(both)
    mixed = hidden + added(mixed)

    return (
        mixed.astype(BF16),
        input_grad,
        terms[0],
        g_qkv,
        g_out,
        terms[1],
        g_gu,
        g_dn,
    )


def solution(mesh):
    fine = Mesh(mesh.devices.reshape(2, 4, 2, 4, 2), AXES)
    row, two = P(AXES), P(AXES, None)
    vec, mat = P(SHARD), P(SHARD, None)
    return jax.shard_map(
        body,
        mesh=fine,
        in_specs=(two, two, row, vec, mat, mat, vec, mat, mat),
        out_specs=(two, two, vec, mat, mat, vec, mat, mat),
        check_vma=False,
    )
```

```python
import math

import jax
import jax.numpy as jnp
from jax import lax
from jax.experimental import pallas as pl
from jax.experimental.pallas import tpu as pltpu
from jax.sharding import Mesh
from jax.sharding import PartitionSpec as P

QUERY_HEADS = 32
KEY_VALUE_HEADS = 4
HEAD_SIZE = 64
GROUP = QUERY_HEADS // KEY_VALUE_HEADS
EPS = 1e-05
ROPE_BASE = 10000.0
NEG = -1e30
BLOCK = 128
CHUNK = 4 * BLOCK
SCALE = 1.0 / math.sqrt(HEAD_SIZE)

AXES = ("zlo", "y", "zhi", "x", "core")
REP = ("zlo", "y")
SHARD = ("zhi", "x", "core")
CHIP = ("zhi", "x")
YZ = ("zlo", "y", "zhi")
YZC = ("zlo", "y", "zhi", "core")
NX = 4

F32 = jnp.float32
BF16 = jnp.bfloat16


def exchange(a, axes):
    return lax.all_to_all(a, axes, split_axis=0, concat_axis=0, tiled=True)


def everywhere(a, axes, n):
    return exchange(jnp.broadcast_to(a[None], (n,) + a.shape), axes)


def swap(a, axis):
    return lax.ppermute(a, axis, [(0, 1), (1, 0)])


def in_order(coord, mine, other, axis):
    return jnp.where(
        coord == 0, jnp.stack([mine, other], axis=axis), jnp.stack([other, mine], axis=axis)
    )


def mm(left, right, dims, out=F32):
    return lax.dot_general(
        left, right, ((dims[0], dims[1]), ((), ())), preferred_element_type=F32
    ).astype(out)


def rms_forward(rows):
    rstd = lax.rsqrt(jnp.mean(rows * rows, axis=1, keepdims=True) + EPS)
    return rows * rstd, rstd


def rms_backward(d_normed, scaled, rstd, gain):
    gain_term = jnp.sum(d_normed * scaled, axis=0)
    inner = d_normed * gain[None, :]
    d_values = rstd * (inner - scaled * jnp.mean(inner * scaled, axis=1, keepdims=True))
    return d_values, gain_term


def heads_to_lanes(ref):
    return jnp.concatenate(
        [ref[HEAD_SIZE * h : HEAD_SIZE * (h + 1), :] for h in range(GROUP)], axis=1
    )


def chunk_slots(c, zhi, x, core):
    slots = []
    for i in range(CHUNK // BLOCK):
        n = c * (CHUNK // BLOCK) + i
        slots.append(((n >> 3) ^ zhi) * 8 + ((n & 1) ^ core) * 4 + (((n >> 1) - x) & 3))
    return slots


def allowed_mask(c, st, block):
    keys = lax.broadcasted_iota(jnp.int32, (CHUNK, 1), 0) + c * CHUNK
    lanes = lax.broadcasted_iota(jnp.int32, (1, GROUP * BLOCK), 1) % BLOCK
    return (keys >= st) & (keys <= block * BLOCK + lanes)


def over_chunks(step, state, first, clear, last):
    clear = jnp.minimum(clear, last)
    state = lax.fori_loop(first, clear, lambda c, v: step(c, v, True), state)
    state = lax.fori_loop(clear, last, lambda c, v: step(c, v, False), state)
    return step(last, state, True)


def attention_forward(sc, q_ref, cos_ref, sin_ref, st_ref, kv_ref, o_ref, ob_ref, qr_ref, lse_ref):
    b = pl.program_id(0)
    zhi, x, core, first = sc[0], sc[1], sc[2], sc[3 + b]
    block = zhi * 8 + 2 * ((x + b) & 3) + core
    cos, sin = cos_ref[...], sin_ref[...]
    turned = []
    for h in range(GROUP):
        u1 = q_ref[HEAD_SIZE * h : HEAD_SIZE * h + 32, :]
        u2 = q_ref[HEAD_SIZE * h + 32 : HEAD_SIZE * h + 64, :]
        turned.append(jnp.concatenate([u1 * cos - u2 * sin, u2 * cos + u1 * sin], axis=0))
    q = jnp.concatenate(turned, axis=1).astype(BF16) * jnp.asarray(SCALE, BF16)
    qr_ref[0] = q
    st = jnp.concatenate([st_ref[0]] * GROUP, axis=1)

    def step(c, state, masked):
        m, l, acc = state
        slots = chunk_slots(c, zhi, x, core)
        k = jnp.concatenate([kv_ref[n, :HEAD_SIZE, :] for n in slots], axis=1)
        v = jnp.concatenate([kv_ref[n, HEAD_SIZE:, :] for n in slots], axis=1)
        s = lax.dot_general(k, q, (((0,), (0,)), ((), ())), preferred_element_type=F32)
        if masked:
            s = jnp.where(allowed_mask(c, st, block), s, NEG)
        m2 = jnp.maximum(m, jnp.max(s, axis=0, keepdims=True))
        p = jnp.exp(s - m2)
        al = jnp.exp(m - m2)
        l = l * al + jnp.sum(p, axis=0, keepdims=True)
        acc = acc * al + lax.dot_general(
            v, p.astype(BF16), (((1,), (0,)), ((), ())), preferred_element_type=F32
        )
        return m2, l, acc

    rows = GROUP * BLOCK
    state = (
        jnp.full((1, rows), NEG, F32),
        jnp.zeros((1, rows), F32),
        jnp.zeros((HEAD_SIZE, rows), F32),
    )
    m, l, acc = over_chunks(step, state, first, sc[7 + b], block // (CHUNK // BLOCK))
    o = acc / l
    for h in range(GROUP):
        part = o[:, BLOCK * h : BLOCK * (h + 1)]
        o_ref[HEAD_SIZE * h : HEAD_SIZE * (h + 1), :] = part
        ob_ref[HEAD_SIZE * h : HEAD_SIZE * (h + 1), :] = part.astype(BF16)
    lse_ref[0] = m + jnp.log(l)


def attention_backward(
    sc, qr_ref, do_ref, o_ref, lse_ref, cos_ref, sin_ref, st_ref, kv_ref, dq_ref, dkv_ref, acc_ref
):
    b = pl.program_id(0)
    zhi, x, core, first = sc[0], sc[1], sc[2], sc[3 + b]
    block = zhi * 8 + 2 * ((x + b) & 3) + core

    @pl.when(b == 0)
    def _():
        acc_ref[...] = jnp.zeros_like(acc_ref)

    q = qr_ref[0]
    do = heads_to_lanes(do_ref)
    delta = jnp.sum(do.astype(F32) * heads_to_lanes(o_ref), axis=0, keepdims=True)
    q_rows = q.T
    do_rows = do.T
    lse = lse_ref[0]
    st = jnp.concatenate([st_ref[0]] * GROUP, axis=1)

    def step(c, dq, masked):
        slots = chunk_slots(c, zhi, x, core)
        k = jnp.concatenate([kv_ref[n, :HEAD_SIZE, :] for n in slots], axis=1)
        v = jnp.concatenate([kv_ref[n, HEAD_SIZE:, :] for n in slots], axis=1)
        s = lax.dot_general(k, q, (((0,), (0,)), ((), ())), preferred_element_type=F32)
        if masked:
            s = jnp.where(allowed_mask(c, st, block), s, NEG)
        p = jnp.exp(s - lse)
        dp = lax.dot_general(v, do, (((0,), (0,)), ((), ())), preferred_element_type=F32)
        ds = (p * (dp - delta)).astype(BF16)
        pb = p.astype(BF16)
        dk = jnp.dot(ds, q_rows, preferred_element_type=F32)
        dv = jnp.dot(pb, do_rows, preferred_element_type=F32)
        both = jnp.concatenate([dk, dv], axis=1)
        for i, n in enumerate(slots):
            acc_ref[n] += both[BLOCK * i : BLOCK * (i + 1)]
        return dq + jnp.dot(k, ds, preferred_element_type=F32)

    dq = jnp.zeros((HEAD_SIZE, GROUP * BLOCK), F32)
    dq = over_chunks(step, dq, first, sc[7 + b], block // (CHUNK // BLOCK))
    dq = dq * SCALE
    cos, sin = cos_ref[...], sin_ref[...]
    for h in range(GROUP):
        g1 = dq[:32, BLOCK * h : BLOCK * (h + 1)]
        g2 = dq[32:, BLOCK * h : BLOCK * (h + 1)]
        dq_ref[HEAD_SIZE * h : HEAD_SIZE * h + 32, :] = (g1 * cos + g2 * sin).astype(BF16)
        dq_ref[HEAD_SIZE * h + 32 : HEAD_SIZE * h + 64, :] = (g2 * cos - g1 * sin).astype(BF16)

    @pl.when(b == NX - 1)
    def _():
        for n in range(16):
            dkv_ref[n] = acc_ref[n].T.astype(BF16)


VMEM_LIMIT = 48 * 1024 * 1024


def call_forward(sc, qkv_t, cos, sin, st, kv):
    rows, toks = GROUP * HEAD_SIZE, NX * BLOCK
    lanes = GROUP * BLOCK
    tile = pl.BlockSpec((rows, BLOCK), lambda b, s: (0, b))
    trig = pl.BlockSpec((32, BLOCK), lambda b, s: (0, b))
    return pl.pallas_call(
        attention_forward,
        grid_spec=pltpu.PrefetchScalarGridSpec(
            num_scalar_prefetch=1,
            grid=(NX,),
            in_specs=[
                tile,
                trig,
                trig,
                pl.BlockSpec((1, 1, BLOCK), lambda b, s: (b, 0, 0)),
                pl.BlockSpec((16, BLOCK, BLOCK), lambda b, s: (0, 0, 0)),
            ],
            out_specs=[
                tile,
                tile,
                pl.BlockSpec((1, HEAD_SIZE, lanes), lambda b, s: (b, 0, 0)),
                pl.BlockSpec((1, 1, lanes), lambda b, s: (b, 0, 0)),
            ],
        ),
        out_shape=[
            jax.ShapeDtypeStruct((rows, toks), F32),
            jax.ShapeDtypeStruct((rows, toks), BF16),
            jax.ShapeDtypeStruct((NX, HEAD_SIZE, lanes), BF16),
            jax.ShapeDtypeStruct((NX, 1, lanes), F32),
        ],
        compiler_params=pltpu.CompilerParams(
            dimension_semantics=("arbitrary",), vmem_limit_bytes=VMEM_LIMIT
        ),
        cost_estimate=cost(1 << 20, 1 << 16),
        name="attention_forward",
    )(sc, qkv_t, cos, sin, st, kv)


def call_backward(sc, qr, do, o, lse, cos, sin, st, kv):
    rows, toks = GROUP * HEAD_SIZE, NX * BLOCK
    lanes = GROUP * BLOCK
    tile = pl.BlockSpec((rows, BLOCK), lambda b, s: (0, b))
    trig = pl.BlockSpec((32, BLOCK), lambda b, s: (0, b))
    whole = pl.BlockSpec((16, BLOCK, BLOCK), lambda b, s: (0, 0, 0))
    return pl.pallas_call(
        attention_backward,
        grid_spec=pltpu.PrefetchScalarGridSpec(
            num_scalar_prefetch=1,
            grid=(NX,),
            in_specs=[
                pl.BlockSpec((1, HEAD_SIZE, lanes), lambda b, s: (b, 0, 0)),
                tile,
                tile,
                pl.BlockSpec((1, 1, lanes), lambda b, s: (b, 0, 0)),
                trig,
                trig,
                pl.BlockSpec((1, 1, BLOCK), lambda b, s: (b, 0, 0)),
                whole,
            ],
            out_specs=[tile, whole],
            scratch_shapes=[pltpu.VMEM((16, BLOCK, BLOCK), F32)],
        ),
        out_shape=[
            jax.ShapeDtypeStruct((rows, toks), BF16),
            jax.ShapeDtypeStruct((16, BLOCK, BLOCK), BF16),
        ],
        compiler_params=pltpu.CompilerParams(
            dimension_semantics=("arbitrary",), vmem_limit_bytes=VMEM_LIMIT
        ),
        cost_estimate=cost(1 << 20, 1 << 16),
        name="attention_backward",
    )(sc, qr, do, o, lse, cos, sin, st, kv)


def project(
    sc, t0, t1, t2a, t2b, t3, mine, other, cos_ref, sin_ref, n_ref, q_ref, kv_ref, w_ref, gain_ref
):
    for ref, c in ((mine, sc[0]), (other, 1 - sc[0])):
        for chip in range(8):
            at = pl.ds(pl.multiple_of((2 * chip + c) * BLOCK, BLOCK), BLOCK)
            w_ref[at, :] = ref[chip, :BLOCK, :]
            info = ref[chip, BLOCK:, :].astype(F32)
            gain_ref[0:1, at] = info[0:1, :BLOCK]
            gain_ref[1:2, at] = info[0:1, BLOCK : 2 * BLOCK]
    for j, t_refs in enumerate(((t0,), (t1,), (t2a, t2b), (t3,))):
        cols = slice(BLOCK * j, BLOCK * (j + 1))
        v = jnp.concatenate([t[...] for t in t_refs], axis=0).astype(F32)
        rstd = lax.rsqrt(jnp.mean(v * v, axis=1, keepdims=True) + EPS)
        n = (v * rstd * gain_ref[0:1, :]).astype(BF16)
        n_ref[cols, :] = n
        qkv = jnp.dot(n, w_ref[...], preferred_element_type=F32).T
        rows = GROUP * HEAD_SIZE
        q_ref[:, cols] = qkv[:rows]
        cos, sin = cos_ref[:, cols], sin_ref[:, cols]
        k1, k2 = qkv[rows : rows + 32], qkv[rows + 32 : rows + 64]
        kv_ref[j, :32, :] = (k1 * cos - k2 * sin).astype(BF16)
        kv_ref[j, 32:64, :] = (k2 * cos + k1 * sin).astype(BF16)
        kv_ref[j, 64:, :] = qkv[rows + 64 :].astype(BF16)


def params(*semantics):
    return pltpu.CompilerParams(
        dimension_semantics=semantics or None, vmem_limit_bytes=VMEM_LIMIT
    )


def cost(flops, moved):
    return pl.CostEstimate(flops=flops, bytes_accessed=moved, transcendentals=0)


def call_project(sc, toks, mine, other, cos, sin):
    dim, cols = toks[0].shape[1], mine.shape[2]
    vmem = pl.BlockSpec(memory_space=pltpu.VMEM)
    return pl.pallas_call(
        project,
        in_specs=[pl.BlockSpec(memory_space=pltpu.SMEM)] + [vmem] * 9,
        out_specs=[vmem] * 5,
        out_shape=[
            jax.ShapeDtypeStruct((NX * BLOCK, dim), BF16),
            jax.ShapeDtypeStruct((GROUP * HEAD_SIZE, NX * BLOCK), F32),
            jax.ShapeDtypeStruct((NX, 2 * HEAD_SIZE, BLOCK), BF16),
            jax.ShapeDtypeStruct((dim, cols), BF16),
            jax.ShapeDtypeStruct((2, dim), F32),
        ],
        compiler_params=params(),
        cost_estimate=cost(1 << 20, 1 << 16),
        name="project",
    )(sc, *toks, mine, other, cos, sin)


def out_project(sc, o_ref, a_ref, b_ref, a2_ref, b2_ref, p0, p1, p2, p3, w_ref):
    first, core = sc[0], sc[1]
    for ref, p, c in (
        (a_ref, first, core),
        (b_ref, 1 - first, core),
        (a2_ref, first, 1 - core),
        (b2_ref, 1 - first, 1 - core),
    ):
        w_ref[pl.ds(pl.multiple_of((2 * p + c) * BLOCK, BLOCK), BLOCK), :] = ref[...]
    for half in range(2):
        at = slice(1024 * half, 1024 * (half + 1))
        d = lax.dot_general(
            o_ref[...], w_ref[:, at], (((0,), (0,)), ((), ())), preferred_element_type=F32
        ).astype(BF16)
        for j, p in enumerate((p0, p1, p2, p3)):
            p[:, at] = d[BLOCK * j : BLOCK * (j + 1)]


def call_out_project(sc, o, *w):
    vmem = pl.BlockSpec(memory_space=pltpu.VMEM)
    return pl.pallas_call(
        out_project,
        in_specs=[pl.BlockSpec(memory_space=pltpu.SMEM)] + [vmem] * 5,
        out_specs=[vmem] * 5,
        out_shape=[jax.ShapeDtypeStruct((BLOCK, 2048), BF16)] * 4
        + [jax.ShapeDtypeStruct((4 * BLOCK, 2048), BF16)],
        compiler_params=params(),
        cost_estimate=cost(1 << 20, 1 << 16),
        name="out_project",
    )(sc, o, *w)


def spread(in_ref, gu_ref, dn_ref, qkv_ref, out_ref, terms_ref):
    def part(row, rows, at, width):
        return in_ref[0, row : row + rows, at : at + width].astype(F32)

    for x in range(NX):
        for half in range(2):
            to = FF_TILE * (4 * half + x)
            gu_ref[:, to : to + FF_TILE] = part(16 * x, 16, FF_TILE * half, FF_TILE)
    for j in range(11):
        dn_ref[32 * j : 32 * (j + 1), :] = part(64, 32, 256 * j, 256)
    k, v = [], []
    for x in range(NX):
        row, at = 96 + 16 * (x % 2), 1152 * (x // 2)
        qkv_ref[:, 512 * x : 512 * (x + 1)] = part(row, 16, at, 512)
        k.append(part(row, 16, at + 512, 64))
        v.append(part(row, 16, at + 576, 64))
    qkv_ref[:, 2048:2304] = jnp.concatenate(k, axis=1)
    qkv_ref[:, 2304:] = jnp.concatenate(v, axis=1)
    for upper in range(2):
        for half in range(2):
            at = 1152 * upper + 640 + 256 * half
            to = 64 * half + 32 * upper
            out_ref[to : to + 32, :] = part(96, 32, at, 256)
    row = part(96, 16, 2304, 256)
    terms = jnp.concatenate([row[0:1, :BLOCK], row[0:1, BLOCK:]], axis=0)

    @pl.when(pl.program_id(0) == 0)
    def _():
        terms_ref[...] = terms

    @pl.when(pl.program_id(0) > 0)
    def _():
        terms_ref[...] += terms


def call_spread(both):
    return pl.pallas_call(
        spread,
        grid=(8,),
        in_specs=[pl.BlockSpec((1,) + both.shape[1:], lambda r: (r, 0, 0))],
        out_specs=[
            pl.BlockSpec((16, 8 * FF_TILE), lambda r: (r, 0)),
            pl.BlockSpec((352, 256), lambda r: (0, r)),
            pl.BlockSpec((16, 2560), lambda r: (r, 0)),
            pl.BlockSpec((BLOCK, 256), lambda r: (0, r)),
            pl.BlockSpec((2, BLOCK), lambda r: (0, 0)),
        ],
        out_shape=[
            jax.ShapeDtypeStruct((BLOCK, 8 * FF_TILE), F32),
            jax.ShapeDtypeStruct((352, 2048), F32),
            jax.ShapeDtypeStruct((BLOCK, 2560), F32),
            jax.ShapeDtypeStruct((BLOCK, 2048), F32),
            jax.ShapeDtypeStruct((2, BLOCK), F32),
        ],
        compiler_params=params("arbitrary"),
        cost_estimate=cost(1 << 20, 1 << 16),
        name="spread",
    )(both)


FF_TILE = 1408


def pack(sc, w_ref, g1_ref, g2_ref, st_ref, gu_ref, dn_ref, wide_ref, gus_ref, dns_ref):
    st = st_ref[...]
    info = [g1_ref[...].astype(F32), g2_ref[...].astype(F32)]
    info += [(st // 256).astype(F32), (st % 256).astype(F32), jnp.zeros((1, BLOCK), F32)]
    info = jnp.broadcast_to(jnp.concatenate(info, axis=1), (16, 5 * BLOCK)).astype(BF16)
    for x in range(NX):
        j = (x - sc[1]) & 3
        k = w_ref[:, 2048 + 64 * x : 2048 + 64 * (x + 1)]
        v = w_ref[:, 2304 + 64 * x : 2304 + 64 * (x + 1)]
        kv = jnp.concatenate([k, v], axis=1)
        for zhi in range(2):
            wide_ref[NX * zhi + x, :BLOCK, :512] = w_ref[:, 512 * x : 512 * (x + 1)]
            wide_ref[NX * zhi + x, :BLOCK, 512:] = kv
            wide_ref[NX * zhi + x, BLOCK:, :] = info
        gus_ref[j, :, :FF_TILE] = gu_ref[:, FF_TILE * x : FF_TILE * (x + 1)]
        up = 4 * FF_TILE + FF_TILE * x
        gus_ref[j, :, FF_TILE:] = gu_ref[:, up : up + FF_TILE]
    for j in range(11):
        dns_ref[:, 256 * j : 256 * (j + 1)] = dn_ref[32 * j : 32 * (j + 1), :]


def call_pack(sc, w_qkv, gain_1, gain_2, starts, w_gu, w_dn):
    vec = pl.BlockSpec((1, BLOCK), lambda i, s: (0, 0))
    return pl.pallas_call(
        pack,
        grid_spec=pltpu.PrefetchScalarGridSpec(
            num_scalar_prefetch=1,
            grid=(1,),
            in_specs=[
                pl.BlockSpec((BLOCK, 2560), lambda i, s: (0, 0)),
                vec,
                vec,
                vec,
                pl.BlockSpec((16, 8 * FF_TILE), lambda i, s: (s[0], 0)),
                pl.BlockSpec((352, 256), lambda i, s: (0, s[0])),
            ],
            out_specs=[
                pl.BlockSpec((8, BLOCK + 16, 640), lambda i, s: (0, 0, 0)),
                pl.BlockSpec((NX, 16, 2 * FF_TILE), lambda i, s: (0, 0, 0)),
                pl.BlockSpec((32, 2 * FF_TILE), lambda i, s: (0, 0)),
            ],
        ),
        out_shape=[
            jax.ShapeDtypeStruct((8, BLOCK + 16, 640), BF16),
            jax.ShapeDtypeStruct((NX, 16, 2 * FF_TILE), BF16),
            jax.ShapeDtypeStruct((32, 2 * FF_TILE), BF16),
        ],
        compiler_params=params("arbitrary"),
        cost_estimate=cost(1 << 20, 1 << 16),
        name="pack",
    )(sc, w_qkv, gain_1[None], gain_2[None], starts[None], w_gu, w_dn)


def down_back(c0, c1, c2, c3, w_ref, d_ref, wdn_ref):
    r = pl.program_id(0)
    for p in range(2):
        for c in range(2):
            for j in range(11):
                at = (2 * p + c) * 352 + 32 * j
                wdn_ref[at : at + 32, :] = w_ref[0, p, c, :, 256 * j : 256 * (j + 1)]
    cots = jnp.concatenate([c0[...], c1[...], c2[...], c3[...]], axis=0)
    part = lax.dot_general(
        cots, wdn_ref[...], (((1,), (1,)), ((), ())), preferred_element_type=F32
    )

    @pl.when(r == 0)
    def _():
        d_ref[...] = part

    @pl.when(r > 0)
    def _():
        d_ref[...] += part


def call_down_back(cots, ffn):
    return pl.pallas_call(
        down_back,
        grid=(8,),
        in_specs=[pl.BlockSpec((BLOCK, 256), lambda r: (0, r))] * 4
        + [pl.BlockSpec((1, 2, 2, 32, 2 * FF_TILE), lambda r: (r, 0, 0, 2, 0))],
        out_specs=[
            pl.BlockSpec((NX * BLOCK, FF_TILE), lambda r: (0, 0)),
            pl.BlockSpec((FF_TILE, 256), lambda r: (0, r)),
        ],
        out_shape=[
            jax.ShapeDtypeStruct((NX * BLOCK, FF_TILE), F32),
            jax.ShapeDtypeStruct((FF_TILE, 2048), BF16),
        ],
        compiler_params=params("arbitrary"),
        cost_estimate=cost(1 << 33, 1 << 20),
        name="down_back",
    )(*cots, ffn)


def natural(w_ref, pick, me):
    parts = []
    for zhi, x, c in pick:
        at = pl.ds(pl.multiple_of(((me - x) & 3) * 16, 16), 16)
        parts.append(w_ref[:, zhi, c, at, :].reshape(BLOCK, BLOCK))
    return jnp.concatenate(parts, axis=0)


ORDER = [(zhi, x, c) for zhi in range(2) for x in range(NX) for c in range(2)]
FF_STEPS = FF_TILE // BLOCK


def feed_forward(
    sc, n0, n1, n2, n3, wg_ref, wu_ref, w_ref, d_ref, o0, o1, o2, o3, act_ref, dgu_ref, n_s, act_s, dg_s
):
    k = pl.program_id(0)

    @pl.when(k == 0)
    def _():
        for j, n in enumerate((n0, n1, n2, n3)):
            n_s[BLOCK * j : BLOCK * (j + 1), :] = n[...]

    @pl.when(k < FF_STEPS)
    def _():
        w = [natural(ref, ORDER, sc[0]) for ref in (wg_ref, wu_ref)]
        w = jnp.concatenate(w, axis=1)
        both = jnp.dot(n_s[...], w, preferred_element_type=F32)
        gate, up = both[:, :BLOCK], both[:, BLOCK:]
        d_act = d_ref[...]
        sig = 1.0 / (1.0 + jnp.exp(-gate))
        silu = gate * sig
        at = pl.ds(pl.multiple_of(k * BLOCK, BLOCK), BLOCK)
        up_at = pl.ds(pl.multiple_of(FF_TILE + k * BLOCK, BLOCK), BLOCK)
        act_s[:, at] = (silu * up).astype(BF16)
        d_gate = d_act * up * (sig * (1.0 + gate * (1.0 - sig)))
        dg_s[:, at] = d_gate.astype(BF16)
        dg_s[:, up_at] = (d_act * silu).astype(BF16)

    @pl.when(k == FF_STEPS)
    def _():
        act_ref[...] = act_s[...]
        dgu_ref[...] = dg_s[...]

    @pl.when(k >= FF_STEPS)
    def _():
        w = jnp.concatenate(
            [w_ref[:, 0, c].reshape(BLOCK, 2 * FF_TILE) for c in range(2)], axis=0
        )
        d = lax.dot_general(
            dg_s[...], w, (((1,), (1,)), ((), ())), preferred_element_type=F32
        ).astype(BF16)
        for j, o in enumerate((o0, o1, o2, o3)):
            o[...] = d[BLOCK * j : BLOCK * (j + 1)]


def call_feed_forward(x, n2, ffn, d_act):
    def tile(k):
        return jnp.minimum(k, FF_STEPS - 1)

    def later(k):
        return jnp.maximum(k - FF_STEPS, 0)

    def row_block(k, s):
        return (0, later(k) >> 2, 0, (s[0] - later(k)) & 3, 0)

    whole = pl.BlockSpec((BLOCK, 2048), lambda k, s: (0, 0))
    out = pl.BlockSpec((BLOCK, 256), lambda k, s: (0, later(k)))
    return pl.pallas_call(
        feed_forward,
        grid_spec=pltpu.PrefetchScalarGridSpec(
            num_scalar_prefetch=1,
            grid=(FF_STEPS + 8,),
            in_specs=[whole] * 4
            + [
                pl.BlockSpec((8, 2, 2, 64, BLOCK), lambda k, s: (0, 0, 0, 0, tile(k))),
                pl.BlockSpec((8, 2, 2, 64, BLOCK), lambda k, s: (0, 0, 0, 0, FF_STEPS + tile(k))),
                pl.BlockSpec((8, 1, 2, 16, 2 * FF_TILE), row_block),
                pl.BlockSpec((NX * BLOCK, BLOCK), lambda k, s: (0, tile(k))),
            ],
            out_specs=[out] * 4
            + [
                pl.BlockSpec((NX * BLOCK, FF_TILE), lambda k, s: (0, 0)),
                pl.BlockSpec((NX * BLOCK, 2 * FF_TILE), lambda k, s: (0, 0)),
            ],
            scratch_shapes=[
                pltpu.VMEM((NX * BLOCK, 2048), BF16),
                pltpu.VMEM((NX * BLOCK, FF_TILE), BF16),
                pltpu.VMEM((NX * BLOCK, 2 * FF_TILE), BF16),
            ],
        ),
        out_shape=[jax.ShapeDtypeStruct((BLOCK, 2048), BF16)] * 4
        + [
            jax.ShapeDtypeStruct((NX * BLOCK, FF_TILE), BF16),
            jax.ShapeDtypeStruct((NX * BLOCK, 2 * FF_TILE), BF16),
        ],
        compiler_params=params("arbitrary"),
        cost_estimate=cost(1 << 20, 1 << 16),
        name="feed_forward",
    )(x[None], *n2, ffn, ffn, ffn, d_act)


def ffn_grads(sc, n0, n1, n2, n3, dgu_ref, act_ref, c0, c1, c2, c3, *rest):
    i = pl.program_id(0)
    added, outs, act_t, g_ref = rest[:-4], rest[-4:-2], rest[-2], rest[-1]

    def put(which, place, value):
        if added:
            value = value + added[which][place].astype(F32)
        outs[which][place] = value.astype(BF16)

    @pl.when(i < NX)
    def _():
        lhs = []
        for zhi in range(2):
            shard = (zhi * NX + jnp.minimum(i, NX - 1)) * 2 + sc[0]
            at = pl.ds(pl.multiple_of(shard * BLOCK, BLOCK), BLOCK)
            lhs.append(jnp.concatenate([n[:, at] for n in (n0, n1, n2, n3)], axis=0))
        lhs = jnp.concatenate(lhs, axis=1)
        for half in range(2):
            cols = slice(FF_TILE * half, FF_TILE * (half + 1))
            g_ref[:, :FF_TILE] = lax.dot_general(
                lhs, dgu_ref[:, cols], (((0,), (0,)), ((), ())), preferred_element_type=F32
            )
            for zhi in range(2):
                for zlo in range(2):
                    for y in range(4):
                        row = zhi * BLOCK + (zlo * 4 + y) * 16
                        part = g_ref[row : row + 16, :FF_TILE]
                        put(0, (y, zlo * 2 + zhi, slice(None), cols), part)

    @pl.when(i == NX)
    def _():
        act_t[...] = act_ref[...].T

    @pl.when(i >= NX)
    def _():
        lhs = []
        for p in range(2):
            for j in range(11):
                row = (2 * p + sc[0]) * 352 + 32 * j + 16 * (i - NX)
                lhs.append(act_t[pl.ds(pl.multiple_of(row, 16), 16), :])
        lhs = jnp.concatenate(lhs, axis=0)
        for zlo in range(2):
            cols = slice(1024 * zlo, 1024 * (zlo + 1))
            cots = jnp.concatenate([c[:, cols] for c in (c0, c1, c2, c3)], axis=0)
            g = jnp.dot(lhs, cots, preferred_element_type=F32)
            for p in range(2):
                for j in range(11):
                    row = p * 176 + 16 * j
                    for y in range(4):
                        part = g[row : row + 16, 256 * y : 256 * (y + 1)]
                        to = slice(256 * j, 256 * (j + 1))
                        put(1, (zlo * 2 + p, y, slice(None), to), part)


def call_ffn_grads(core, n2, d_gu, act, cots, *added):
    const = pl.BlockSpec((BLOCK, 2048), lambda i, s: (0, 0))
    tile = (4, 4, 16, 2 * FF_TILE)
    outs = [
        pl.BlockSpec(tile, lambda i, s: (0, 0, jnp.minimum(i, NX - 1), 0)),
        pl.BlockSpec(tile, lambda i, s: (0, 0, jnp.maximum(i - NX, 0), 0)),
    ]
    return pl.pallas_call(
        ffn_grads,
        grid_spec=pltpu.PrefetchScalarGridSpec(
            num_scalar_prefetch=1,
            grid=(NX + 2,),
            in_specs=[const] * 4
            + [pl.BlockSpec((NX * BLOCK, 2 * FF_TILE), lambda i, s: (0, 0))]
            + [pl.BlockSpec((NX * BLOCK, FF_TILE), lambda i, s: (0, 0))]
            + [const] * 4
            + outs[: len(added)],
            out_specs=outs,
            scratch_shapes=[
                pltpu.VMEM((FF_TILE, NX * BLOCK), BF16),
                pltpu.VMEM((2 * BLOCK, FF_TILE), F32),
            ],
        ),
        out_shape=[
            jax.ShapeDtypeStruct((4, 4, 64, 2 * FF_TILE), BF16),
            jax.ShapeDtypeStruct((4, 4, 32, 2 * FF_TILE), BF16),
        ],
        compiler_params=params("arbitrary"),
        cost_estimate=cost(1 << 33, 1 << 20),
        name="ffn_grads_mine" if added else "ffn_grads_other",
    )(core[None], *n2, d_gu, act, *cots, *added)


def attention_grads(sc, n_ref, dq_ref, o_ref, db_ref, *rest):
    added, out_ref, qkv_s, out_s = rest[:-3], rest[-3], rest[-2], rest[-1]

    def put(place, value):
        if added:
            value = value + added[0][place].astype(F32)
        out_ref[place] = value.astype(BF16)

    for zhi in range(2):
        lhs = []
        for x in range(NX):
            at = pl.ds(pl.multiple_of(((zhi * NX + x) * 2 + sc[0]) * BLOCK, BLOCK), BLOCK)
            lhs.append(n_ref[:, at])
        lhs = jnp.concatenate(lhs, axis=1)
        qkv_s[...] = lax.dot_general(
            lhs, dq_ref[...], (((0,), (1,)), ((), ())), preferred_element_type=F32
        )
        for x in range(NX):
            for replica in range(8):
                row = BLOCK * x + 16 * replica
                to = slice(16 * x, 16 * (x + 1))
                put((replica % 4, replica // 4 * 2 + zhi, to, slice(0, 640)), qkv_s[row : row + 16, :])
    for p in range(2):
        rows = o_ref[pl.ds(pl.multiple_of((2 * p + sc[0]) * BLOCK, BLOCK), BLOCK), :]
        out_s[...] = jnp.dot(rows, db_ref[...], preferred_element_type=F32)
        for replica in range(8):
            for half in range(2):
                part = out_s[64 * half : 64 * (half + 1), 256 * replica : 256 * (replica + 1)]
                at = 640 + 256 * half
                put((replica % 4, replica // 4 * 2 + p, slice(None), slice(at, at + 256)), part)


def call_attention_grads(core, n1, d_qkv, ob, d_br, *added):
    vmem = pl.BlockSpec(memory_space=pltpu.VMEM)
    return pl.pallas_call(
        attention_grads,
        in_specs=[pl.BlockSpec(memory_space=pltpu.SMEM)] + [vmem] * (4 + len(added)),
        out_specs=vmem,
        out_shape=jax.ShapeDtypeStruct((4, 4, 64, 1152), BF16),
        scratch_shapes=[pltpu.VMEM((4 * BLOCK, 640), F32), pltpu.VMEM((BLOCK, 2048), F32)],
        compiler_params=params(),
        cost_estimate=cost(1 << 33, 1 << 20),
        name="attention_grads_mine" if added else "attention_grads_other",
    )(core[None], n1, d_qkv, ob, d_br, *added)


def shift_x(a, k):
    return lax.ppermute(a, "x", [(i, (i + k) % NX) for i in range(NX)])


def gathered_x(a, between=lambda: ()):
    half = a.shape[0] // 2
    t1, t3 = shift_x(a, 3), shift_x(a, 1)
    t1, t3 = lax.optimization_barrier((t1, t3, *between()))[:2]
    return [a, t1, jnp.concatenate([shift_x(t1[:half], 3), shift_x(t3[half:], 1)]), t3]


def moved_x(parts):
    half = parts[2].shape[0] // 2
    up, down = shift_x(parts[2][:half], 1), shift_x(parts[2][half:], 3)
    up = (parts[1][:half].astype(F32) + up.astype(F32)).astype(BF16)
    down = (parts[3][half:].astype(F32) + down.astype(F32)).astype(BF16)
    up = jnp.concatenate([up, parts[1][half:]])
    down = jnp.concatenate([parts[3][:half], down])
    return [parts[0], shift_x(up, 1), shift_x(down, 3)]


def added(parts):
    return sum(p.astype(F32) for p in parts)


def summed_x(parts):
    return added(moved_x(parts))


def sent(parts, axes, me=0):
    out = []
    for j in range(4):
        part = lax.dynamic_index_in_dim(parts, (me + j) % 4, 0, keepdims=False)
        out.append(lax.ppermute(part, axes, [(i, (i + j) % 4) for i in range(4)]) if j else part)
    return out


def total(parts):
    return parts.astype(F32).sum(axis=0).astype(BF16)


def pieces(a):
    return [a[BLOCK * j : BLOCK * (j + 1)] for j in range(NX)]


def summed(t, axes):
    return exchange(t, axes).astype(F32).sum(axis=0).astype(BF16)


def to_heads(first):
    pairs = []
    for s_zhi in range(2):
        for s_x in range(NX):
            d_zhi = s_x % 2 if first else 1 - s_x % 2
            pairs.append((s_zhi * NX + s_x, d_zhi * NX + 2 * s_zhi + s_x // 2))
    return pairs


def to_owners(first):
    return [(d, s) for s, d in to_heads(first)]


def after(a, *others):
    return lax.optimization_barrier((a, *others))[0]


def body(tok, cot, starts, gain_1, w_qkv, w_out, gain_2, w_gu, w_dn):
    zlo, y, zhi, x, core = (lax.axis_index(a) for a in AXES)
    replica = zlo * 4 + y
    rows, dim = tok.shape
    q_cols = GROUP * HEAD_SIZE
    ff_shard = w_dn.shape[0]
    slab = rows // 8

    t1, t3 = shift_x(tok, 3), shift_x(tok, 1)
    toks = [tok, t1, shift_x(t1[: rows // 2], 3), shift_x(t3[rows // 2 :], 1), t3]
    w_far = swap(w_out, "zhi")
    place = jnp.stack([replica, x])
    wide, gu_slab, dn_slab = call_pack(place, w_qkv, gain_1, gain_2, starts, w_gu, w_dn)
    qkv_cols = wide.shape[2]
    wide = exchange(wide, CHIP)

    gu_slab = jnp.concatenate(sent(gu_slab, "x"), axis=0)
    dn_slab = lax.ppermute(dn_slab, CHIP, to_heads(True))
    slabs = jnp.concatenate([gu_slab, dn_slab])
    slabs = after(slabs, wide, t1, t3)
    ffn = lax.all_gather(slabs, YZC, axis=0)
    ffn = ffn.reshape(8, 2, 2, NX * slab + 32, 2 * FF_TILE)

    inputs = tok.astype(F32)
    scaled_one, rstd_one = rms_forward(inputs)
    blocks = (x + jnp.arange(NX, dtype=jnp.int32)) % NX
    block_ids = zhi * 8 + 2 * blocks + core
    st = lax.dynamic_slice_in_dim(wide, zhi * NX, NX, 0)[:, rows, 2 * rows : 4 * rows]
    st = st.astype(F32).reshape(NX, 2, rows)
    st = (st[:, 0] * 256.0 + st[:, 1]).astype(jnp.int32)[blocks]
    where_at = block_ids[:, None] * rows + jnp.arange(rows, dtype=jnp.int32)[None, :]
    pos = (where_at - st).reshape(1, NX * rows).astype(F32)
    freqs = jnp.exp(jnp.arange(32, dtype=F32) * (-2.0 * math.log(ROPE_BASE) / HEAD_SIZE))
    angles = freqs[:, None] * pos
    cos, sin = jnp.cos(angles), jnp.sin(angles)
    n1, q_t, kv, wq, gains = call_project(core[None], toks, wide, swap(wide, "core"), cos, sin)
    gain_one, gain_two = gains[0], gains[1]
    kv = jnp.concatenate([kv, swap(kv, "core")], axis=0)
    near, far = jnp.where(zhi == 0, w_out, w_far), jnp.where(zhi == 0, w_far, w_out)
    even = x % 2 == 0
    part_a, part_b = jnp.where(even, near, far), jnp.where(even, far, near)
    part_a, part_b, cot_in = lax.optimization_barrier((part_a, part_b, cot, kv))[:3]
    kv = jnp.concatenate([kv, swap(kv, "zhi")], axis=0)
    part_a = lax.ppermute(part_a, "x", [(0, 0), (1, 2), (2, 1), (3, 3)])
    part_b = lax.ppermute(part_b, "x", [(0, 2), (1, 0), (2, 3), (3, 1)])
    firsts = jnp.min(st, axis=1) // CHUNK
    clears = (jnp.max(st, axis=1) + CHUNK - 1) // CHUNK
    sc = jnp.concatenate([zhi[None], x[None], core[None], firsts, clears]).astype(jnp.int32)
    st = st[:, None, :]
    o, ob, qr, lse = call_forward(sc, q_t, cos, sin, st, kv)
    cots = [cot_in, shift_x(cot_in, 3), shift_x(cot_in, 2), shift_x(cot_in, 1)]
    ob, *cots = lax.optimization_barrier((ob, *cots))
    part_a, part_b = after(part_a, ob), after(part_b, ob)
    *parts, wo = call_out_project(
        jnp.stack([x // 2, core]), ob, part_a, part_b, swap(part_a, "core"), swap(part_b, "core")
    )
    hidden = inputs + summed_x(parts)

    d_act, wdn = call_down_back(cots, ffn)
    scaled_two, rstd_two = rms_forward(hidden)
    n2 = gathered_x((scaled_two * gain_two[None, :]).astype(BF16), lambda: (d_act,))
    *d_n2, act, d_gu = call_feed_forward(x, n2, ffn, d_act)

    other = call_ffn_grads(1 - core, n2, d_gu, act, cots)
    d_n2 = moved_x(d_n2)
    other = lax.optimization_barrier((*other, *d_n2[1:]))[:2]
    other = [swap(g, "core") for g in other]
    g_gu, g_dn = call_ffn_grads(core, n2, d_gu, act, cots, *other)
    d_mid, gain_two_term = rms_backward(added(d_n2), scaled_two, rstd_two, gain_two)
    d_mid = cot.astype(F32) + d_mid
    d_br = gathered_x(d_mid.astype(BF16), lambda: (g_gu, g_dn))
    z = zlo * 2 + zhi
    g_gu = exchange(g_gu.reshape(4, 4 * 64, 2 * FF_TILE), "y")
    g_dn = sent(g_dn, ("zlo", "zhi"), z)
    d_br = jnp.concatenate(d_br)

    do = mm(wo, d_br, ((1,), (1,)), BF16)
    dq, dkv = call_backward(sc, qr, do, o, lse, cos, sin, st, kv)
    dkv, *g_dn = lax.optimization_barrier((dkv, *g_dn))
    dkv = dkv.reshape(2, 2, NX, 2 * HEAD_SIZE, rows)
    dkv = dkv[:, 0].astype(F32) + swap(dkv[:, 1], "core").astype(F32)
    dkv = dkv[0] + swap(dkv[1].astype(BF16), "zhi").astype(F32)
    g_dn = added(g_dn).astype(BF16)
    dkv = dkv.transpose(1, 0, 2).reshape(2 * HEAD_SIZE, NX * rows)
    k1, k2 = dkv[:32], dkv[32:64]
    dkv = jnp.concatenate([k1 * cos + k2 * sin, k2 * cos - k1 * sin, dkv[64:]], axis=0)
    d_qkv = jnp.concatenate([dq, dkv.astype(BF16)], axis=0)
    d_qkv, g_gu = lax.optimization_barrier((d_qkv, g_gu))
    d_n1 = mm(d_qkv, wq, ((0,), (1,)), BF16)
    d_qkv, ob, g_dn = lax.optimization_barrier((d_qkv, ob, g_dn, d_n1))[:3]
    d_n1 = moved_x(pieces(d_n1))
    other = swap(call_attention_grads(1 - core, n1, d_qkv, ob, d_br), "core")
    g_attn = call_attention_grads(core, n1, d_qkv, ob, d_br, other)

    g_gu, g_attn = lax.optimization_barrier((g_gu, g_attn))
    g_gu = exchange(total(g_gu.reshape(4, 4, 64, 2 * FF_TILE)), ("zlo", "zhi"))
    g_attn = sent(g_attn, "y", y)
    g_dn = sent(after(g_dn, g_attn[1]), "y", y)
    g_attn = sent(added(g_attn).astype(BF16), ("zlo", "zhi"), z)
    g_gu = exchange(total(g_gu).reshape(NX, slab, 2 * FF_TILE), "x")
    g_dn = lax.ppermute(added(g_dn).astype(BF16), CHIP, to_owners(True))
    *g_attn, g_gu, g_dn = lax.optimization_barrier((*g_attn, g_gu, g_dn))
    d_n1 = lax.optimization_barrier((*d_n1, *g_attn))[:3]
    act = after(act, *d_n1)
    mixed = moved_x(pieces(mm(act, wdn, ((1,), (0,)), BF16)))
    d_in, gain_one_term = rms_backward(added(d_n1), scaled_one, rstd_one, gain_one)
    input_grad = (d_mid + d_in).astype(BF16)
    g_attn = added(g_attn).astype(BF16)
    g_out = lax.ppermute(g_attn[:, 640:], CHIP, to_owners(True))
    g_qkv = jnp.stack(sent(g_attn[:, :640].reshape(NX, slab, qkv_cols), "x", x))
    g_qkv = g_qkv[(x - jnp.arange(NX, dtype=jnp.int32)) % NX]
    terms = jnp.stack([gain_one_term, gain_two_term]).reshape(2, 16, rows).transpose(1, 0, 2)
    terms = exchange(terms, SHARD).sum(axis=0).reshape(1, 2 * rows)
    terms = jnp.broadcast_to(terms, (32, 2 * rows)).astype(BF16)
    g_qkv = g_qkv.reshape(NX * slab, qkv_cols)
    attn = [g_qkv[:32], g_out[:32], g_qkv[32:], g_out[32:], terms, jnp.zeros_like(terms)]
    attn = jnp.concatenate(attn, axis=1)
    both = jnp.concatenate([g_gu.reshape(NX * slab, 2 * FF_TILE), g_dn, attn])
    both = lax.all_gather(both, REP, axis=0)
    g_gu, g_dn, g_qkv, g_out, terms = call_spread(both)
    mixed = hidden + added(mixed)

    return (
        mixed.astype(BF16),
        input_grad,
        terms[0],
        g_qkv,
        g_out,
        terms[1],
        g_gu,
        g_dn,
    )


def solution(mesh):
    fine = Mesh(mesh.devices.reshape(2, 4, 2, 4, 2), AXES)
    row, two = P(AXES), P(AXES, None)
    vec, mat = P(SHARD), P(SHARD, None)
    return jax.shard_map(
        body,
        mesh=fine,
        in_specs=(two, two, row, vec, mat, mat, vec, mat, mat),
        out_specs=(two, two, vec, mat, mat, vec, mat, mat),
        check_vma=False,
    )
```

```python
import math

import jax
import jax.numpy as jnp
from jax import lax
from jax.experimental import pallas as pl
from jax.experimental.pallas import tpu as pltpu
from jax.sharding import Mesh
from jax.sharding import PartitionSpec as P

QUERY_HEADS = 32
KEY_VALUE_HEADS = 4
HEAD_SIZE = 64
GROUP = QUERY_HEADS // KEY_VALUE_HEADS
EPS = 1e-05
ROPE_BASE = 10000.0
NEG = -1e30
BLOCK = 128
CHUNK = 4 * BLOCK
SCALE = 1.0 / math.sqrt(HEAD_SIZE)

AXES = ("zlo", "y", "zhi", "x", "core")
REP = ("zlo", "y")
SHARD = ("zhi", "x", "core")
CHIP = ("zhi", "x")
YZ = ("zlo", "y", "zhi")
YZC = ("zlo", "y", "zhi", "core")
NX = 4

F32 = jnp.float32
BF16 = jnp.bfloat16


def exchange(a, axes):
    return lax.all_to_all(a, axes, split_axis=0, concat_axis=0, tiled=True)


def everywhere(a, axes, n):
    return exchange(jnp.broadcast_to(a[None], (n,) + a.shape), axes)


def swap(a, axis):
    return lax.ppermute(a, axis, [(0, 1), (1, 0)])


def in_order(coord, mine, other, axis):
    return jnp.where(
        coord == 0, jnp.stack([mine, other], axis=axis), jnp.stack([other, mine], axis=axis)
    )


def mm(left, right, dims, out=F32):
    return lax.dot_general(
        left, right, ((dims[0], dims[1]), ((), ())), preferred_element_type=F32
    ).astype(out)


def rms_forward(rows):
    rstd = lax.rsqrt(jnp.mean(rows * rows, axis=1, keepdims=True) + EPS)
    return rows * rstd, rstd


def rms_backward(d_normed, scaled, rstd, gain):
    gain_term = jnp.sum(d_normed * scaled, axis=0)
    inner = d_normed * gain[None, :]
    d_values = rstd * (inner - scaled * jnp.mean(inner * scaled, axis=1, keepdims=True))
    return d_values, gain_term


def heads_to_lanes(ref):
    return jnp.concatenate(
        [ref[HEAD_SIZE * h : HEAD_SIZE * (h + 1), :] for h in range(GROUP)], axis=1
    )


def chunk_slots(c, zhi, x, core):
    slots = []
    for i in range(CHUNK // BLOCK):
        n = c * (CHUNK // BLOCK) + i
        slots.append(((n >> 3) ^ zhi) * 8 + ((n & 1) ^ core) * 4 + (((n >> 1) - x) & 3))
    return slots


def allowed_mask(c, st, block):
    keys = lax.broadcasted_iota(jnp.int32, (CHUNK, 1), 0) + c * CHUNK
    lanes = lax.broadcasted_iota(jnp.int32, (1, GROUP * BLOCK), 1) % BLOCK
    return (keys >= st) & (keys <= block * BLOCK + lanes)


def over_chunks(step, state, first, clear, last):
    clear = jnp.minimum(clear, last)
    state = lax.fori_loop(first, clear, lambda c, v: step(c, v, True), state)
    state = lax.fori_loop(clear, last, lambda c, v: step(c, v, False), state)
    return step(last, state, True)


def attention_forward(sc, q_ref, cos_ref, sin_ref, st_ref, kv_ref, o_ref, ob_ref, qr_ref, lse_ref):
    b = pl.program_id(0)
    zhi, x, core, first = sc[0], sc[1], sc[2], sc[3 + b]
    block = zhi * 8 + 2 * ((x + b) & 3) + core
    cos, sin = cos_ref[...], sin_ref[...]
    turned = []
    for h in range(GROUP):
        u1 = q_ref[HEAD_SIZE * h : HEAD_SIZE * h + 32, :]
        u2 = q_ref[HEAD_SIZE * h + 32 : HEAD_SIZE * h + 64, :]
        turned.append(jnp.concatenate([u1 * cos - u2 * sin, u2 * cos + u1 * sin], axis=0))
    q = jnp.concatenate(turned, axis=1).astype(BF16) * jnp.asarray(SCALE, BF16)
    qr_ref[0] = q
    st = jnp.concatenate([st_ref[0]] * GROUP, axis=1)

    def step(c, state, masked):
        m, l, acc = state
        slots = chunk_slots(c, zhi, x, core)
        k = jnp.concatenate([kv_ref[n, :HEAD_SIZE, :] for n in slots], axis=1)
        v = jnp.concatenate([kv_ref[n, HEAD_SIZE:, :] for n in slots], axis=1)
        s = lax.dot_general(k, q, (((0,), (0,)), ((), ())), preferred_element_type=F32)
        if masked:
            s = jnp.where(allowed_mask(c, st, block), s, NEG)
        m2 = jnp.maximum(m, jnp.max(s, axis=0, keepdims=True))
        p = jnp.exp(s - m2)
        al = jnp.exp(m - m2)
        l = l * al + jnp.sum(p, axis=0, keepdims=True)
        acc = acc * al + lax.dot_general(
            v, p.astype(BF16), (((1,), (0,)), ((), ())), preferred_element_type=F32
        )
        return m2, l, acc

    rows = GROUP * BLOCK
    state = (
        jnp.full((1, rows), NEG, F32),
        jnp.zeros((1, rows), F32),
        jnp.zeros((HEAD_SIZE, rows), F32),
    )
    m, l, acc = over_chunks(step, state, first, sc[7 + b], block // (CHUNK // BLOCK))
    o = acc / l
    for h in range(GROUP):
        part = o[:, BLOCK * h : BLOCK * (h + 1)]
        o_ref[HEAD_SIZE * h : HEAD_SIZE * (h + 1), :] = part
        ob_ref[HEAD_SIZE * h : HEAD_SIZE * (h + 1), :] = part.astype(BF16)
    lse_ref[0] = m + jnp.log(l)


def attention_backward(
    sc, qr_ref, do_ref, o_ref, lse_ref, cos_ref, sin_ref, st_ref, kv_ref, dq_ref, dkv_ref, acc_ref
):
    b = pl.program_id(0)
    zhi, x, core, first = sc[0], sc[1], sc[2], sc[3 + b]
    block = zhi * 8 + 2 * ((x + b) & 3) + core

    @pl.when(b == 0)
    def _():
        acc_ref[...] = jnp.zeros_like(acc_ref)

    q = qr_ref[0]
    do = heads_to_lanes(do_ref)
    delta = jnp.sum(do.astype(F32) * heads_to_lanes(o_ref), axis=0, keepdims=True)
    q_rows = q.T
    do_rows = do.T
    lse = lse_ref[0]
    st = jnp.concatenate([st_ref[0]] * GROUP, axis=1)

    def step(c, dq, masked):
        slots = chunk_slots(c, zhi, x, core)
        k = jnp.concatenate([kv_ref[n, :HEAD_SIZE, :] for n in slots], axis=1)
        v = jnp.concatenate([kv_ref[n, HEAD_SIZE:, :] for n in slots], axis=1)
        s = lax.dot_general(k, q, (((0,), (0,)), ((), ())), preferred_element_type=F32)
        if masked:
            s = jnp.where(allowed_mask(c, st, block), s, NEG)
        p = jnp.exp(s - lse)
        dp = lax.dot_general(v, do, (((0,), (0,)), ((), ())), preferred_element_type=F32)
        ds = (p * (dp - delta)).astype(BF16)
        pb = p.astype(BF16)
        dk = jnp.dot(ds, q_rows, preferred_element_type=F32)
        dv = jnp.dot(pb, do_rows, preferred_element_type=F32)
        both = jnp.concatenate([dk, dv], axis=1)
        for i, n in enumerate(slots):
            acc_ref[n] += both[BLOCK * i : BLOCK * (i + 1)]
        return dq + jnp.dot(k, ds, preferred_element_type=F32)

    dq = jnp.zeros((HEAD_SIZE, GROUP * BLOCK), F32)
    dq = over_chunks(step, dq, first, sc[7 + b], block // (CHUNK // BLOCK))
    dq = dq * SCALE
    cos, sin = cos_ref[...], sin_ref[...]
    for h in range(GROUP):
        g1 = dq[:32, BLOCK * h : BLOCK * (h + 1)]
        g2 = dq[32:, BLOCK * h : BLOCK * (h + 1)]
        dq_ref[HEAD_SIZE * h : HEAD_SIZE * h + 32, :] = (g1 * cos + g2 * sin).astype(BF16)
        dq_ref[HEAD_SIZE * h + 32 : HEAD_SIZE * h + 64, :] = (g2 * cos - g1 * sin).astype(BF16)

    @pl.when(b == NX - 1)
    def _():
        for n in range(16):
            dkv_ref[n] = acc_ref[n].T.astype(BF16)


VMEM_LIMIT = 48 * 1024 * 1024


def call_forward(sc, qkv_t, cos, sin, st, kv):
    rows, toks = GROUP * HEAD_SIZE, NX * BLOCK
    lanes = GROUP * BLOCK
    tile = pl.BlockSpec((rows, BLOCK), lambda b, s: (0, b))
    trig = pl.BlockSpec((32, BLOCK), lambda b, s: (0, b))
    return pl.pallas_call(
        attention_forward,
        grid_spec=pltpu.PrefetchScalarGridSpec(
            num_scalar_prefetch=1,
            grid=(NX,),
            in_specs=[
                tile,
                trig,
                trig,
                pl.BlockSpec((1, 1, BLOCK), lambda b, s: (b, 0, 0)),
                pl.BlockSpec((16, BLOCK, BLOCK), lambda b, s: (0, 0, 0)),
            ],
            out_specs=[
                tile,
                tile,
                pl.BlockSpec((1, HEAD_SIZE, lanes), lambda b, s: (b, 0, 0)),
                pl.BlockSpec((1, 1, lanes), lambda b, s: (b, 0, 0)),
            ],
        ),
        out_shape=[
            jax.ShapeDtypeStruct((rows, toks), F32),
            jax.ShapeDtypeStruct((rows, toks), BF16),
            jax.ShapeDtypeStruct((NX, HEAD_SIZE, lanes), BF16),
            jax.ShapeDtypeStruct((NX, 1, lanes), F32),
        ],
        compiler_params=pltpu.CompilerParams(
            dimension_semantics=("arbitrary",), vmem_limit_bytes=VMEM_LIMIT
        ),
        cost_estimate=cost(1 << 20, 1 << 16),
        name="attention_forward",
    )(sc, qkv_t, cos, sin, st, kv)


def call_backward(sc, qr, do, o, lse, cos, sin, st, kv):
    rows, toks = GROUP * HEAD_SIZE, NX * BLOCK
    lanes = GROUP * BLOCK
    tile = pl.BlockSpec((rows, BLOCK), lambda b, s: (0, b))
    trig = pl.BlockSpec((32, BLOCK), lambda b, s: (0, b))
    whole = pl.BlockSpec((16, BLOCK, BLOCK), lambda b, s: (0, 0, 0))
    return pl.pallas_call(
        attention_backward,
        grid_spec=pltpu.PrefetchScalarGridSpec(
            num_scalar_prefetch=1,
            grid=(NX,),
            in_specs=[
                pl.BlockSpec((1, HEAD_SIZE, lanes), lambda b, s: (b, 0, 0)),
                tile,
                tile,
                pl.BlockSpec((1, 1, lanes), lambda b, s: (b, 0, 0)),
                trig,
                trig,
                pl.BlockSpec((1, 1, BLOCK), lambda b, s: (b, 0, 0)),
                whole,
            ],
            out_specs=[tile, whole],
            scratch_shapes=[pltpu.VMEM((16, BLOCK, BLOCK), F32)],
        ),
        out_shape=[
            jax.ShapeDtypeStruct((rows, toks), BF16),
            jax.ShapeDtypeStruct((16, BLOCK, BLOCK), BF16),
        ],
        compiler_params=pltpu.CompilerParams(
            dimension_semantics=("arbitrary",), vmem_limit_bytes=VMEM_LIMIT
        ),
        cost_estimate=cost(1 << 20, 1 << 16),
        name="attention_backward",
    )(sc, qr, do, o, lse, cos, sin, st, kv)


def project(
    sc, t0, t1, t2a, t2b, t3, mine, other, cos_ref, sin_ref, n_ref, q_ref, kv_ref, w_ref, gain_ref
):
    for ref, c in ((mine, sc[0]), (other, 1 - sc[0])):
        for chip in range(8):
            at = pl.ds(pl.multiple_of((2 * chip + c) * BLOCK, BLOCK), BLOCK)
            w_ref[at, :] = ref[chip, :BLOCK, :]
            info = ref[chip, BLOCK:, :].astype(F32)
            gain_ref[0:1, at] = info[0:1, :BLOCK]
            gain_ref[1:2, at] = info[0:1, BLOCK : 2 * BLOCK]
    for j, t_refs in enumerate(((t0,), (t1,), (t2a, t2b), (t3,))):
        cols = slice(BLOCK * j, BLOCK * (j + 1))
        v = jnp.concatenate([t[...] for t in t_refs], axis=0).astype(F32)
        rstd = lax.rsqrt(jnp.mean(v * v, axis=1, keepdims=True) + EPS)
        n = (v * rstd * gain_ref[0:1, :]).astype(BF16)
        n_ref[cols, :] = n
        qkv = jnp.dot(n, w_ref[...], preferred_element_type=F32).T
        rows = GROUP * HEAD_SIZE
        q_ref[:, cols] = qkv[:rows]
        cos, sin = cos_ref[:, cols], sin_ref[:, cols]
        k1, k2 = qkv[rows : rows + 32], qkv[rows + 32 : rows + 64]
        kv_ref[j, :32, :] = (k1 * cos - k2 * sin).astype(BF16)
        kv_ref[j, 32:64, :] = (k2 * cos + k1 * sin).astype(BF16)
        kv_ref[j, 64:, :] = qkv[rows + 64 :].astype(BF16)


def params(*semantics):
    return pltpu.CompilerParams(
        dimension_semantics=semantics or None, vmem_limit_bytes=VMEM_LIMIT
    )


def cost(flops, moved):
    return pl.CostEstimate(flops=flops, bytes_accessed=moved, transcendentals=0)


def call_project(sc, toks, mine, other, cos, sin):
    dim, cols = toks[0].shape[1], mine.shape[2]
    vmem = pl.BlockSpec(memory_space=pltpu.VMEM)
    return pl.pallas_call(
        project,
        in_specs=[pl.BlockSpec(memory_space=pltpu.SMEM)] + [vmem] * 9,
        out_specs=[vmem] * 5,
        out_shape=[
            jax.ShapeDtypeStruct((NX * BLOCK, dim), BF16),
            jax.ShapeDtypeStruct((GROUP * HEAD_SIZE, NX * BLOCK), F32),
            jax.ShapeDtypeStruct((NX, 2 * HEAD_SIZE, BLOCK), BF16),
            jax.ShapeDtypeStruct((dim, cols), BF16),
            jax.ShapeDtypeStruct((2, dim), F32),
        ],
        compiler_params=params(),
        cost_estimate=cost(1 << 20, 1 << 16),
        name="project",
    )(sc, *toks, mine, other, cos, sin)


def out_project(sc, o_ref, a_ref, b_ref, a2_ref, b2_ref, p0, p1, p2, p3, w_ref):
    first, core = sc[0], sc[1]
    for ref, p, c in (
        (a_ref, first, core),
        (b_ref, 1 - first, core),
        (a2_ref, first, 1 - core),
        (b2_ref, 1 - first, 1 - core),
    ):
        w_ref[pl.ds(pl.multiple_of((2 * p + c) * BLOCK, BLOCK), BLOCK), :] = ref[...]
    for half in range(2):
        at = slice(1024 * half, 1024 * (half + 1))
        d = lax.dot_general(
            o_ref[...], w_ref[:, at], (((0,), (0,)), ((), ())), preferred_element_type=F32
        ).astype(BF16)
        for j, p in enumerate((p0, p1, p2, p3)):
            p[:, at] = d[BLOCK * j : BLOCK * (j + 1)]


def call_out_project(sc, o, *w):
    vmem = pl.BlockSpec(memory_space=pltpu.VMEM)
    return pl.pallas_call(
        out_project,
        in_specs=[pl.BlockSpec(memory_space=pltpu.SMEM)] + [vmem] * 5,
        out_specs=[vmem] * 5,
        out_shape=[jax.ShapeDtypeStruct((BLOCK, 2048), BF16)] * 4
        + [jax.ShapeDtypeStruct((4 * BLOCK, 2048), BF16)],
        compiler_params=params(),
        cost_estimate=cost(1 << 20, 1 << 16),
        name="out_project",
    )(sc, o, *w)


def spread(in_ref, gu_ref, dn_ref, qkv_ref, out_ref):
    def part(row, rows, at, width):
        return in_ref[0, row : row + rows, at : at + width].astype(F32)

    for x in range(NX):
        for half in range(2):
            to = FF_TILE * (4 * half + x)
            gu_ref[:, to : to + FF_TILE] = part(16 * x, 16, FF_TILE * half, FF_TILE)
    for j in range(11):
        dn_ref[32 * j : 32 * (j + 1), :] = part(64, 32, 256 * j, 256)
    k, v = [], []
    for x in range(NX):
        row, at = 96 + 16 * (x % 2), 1152 * (x // 2)
        qkv_ref[:, 512 * x : 512 * (x + 1)] = part(row, 16, at, 512)
        k.append(part(row, 16, at + 512, 64))
        v.append(part(row, 16, at + 576, 64))
    qkv_ref[:, 2048:2304] = jnp.concatenate(k, axis=1)
    qkv_ref[:, 2304:] = jnp.concatenate(v, axis=1)
    for upper in range(2):
        for half in range(2):
            at = 1152 * upper + 640 + 256 * half
            to = 64 * half + 32 * upper
            out_ref[to : to + 32, :] = part(96, 32, at, 256)


def call_spread(both):
    return pl.pallas_call(
        spread,
        grid=(8,),
        in_specs=[pl.BlockSpec((1,) + both.shape[1:], lambda r: (r, 0, 0))],
        out_specs=[
            pl.BlockSpec((16, 8 * FF_TILE), lambda r: (r, 0)),
            pl.BlockSpec((352, 256), lambda r: (0, r)),
            pl.BlockSpec((16, 2560), lambda r: (r, 0)),
            pl.BlockSpec((BLOCK, 256), lambda r: (0, r)),
        ],
        out_shape=[
            jax.ShapeDtypeStruct((BLOCK, 8 * FF_TILE), F32),
            jax.ShapeDtypeStruct((352, 2048), F32),
            jax.ShapeDtypeStruct((BLOCK, 2560), F32),
            jax.ShapeDtypeStruct((BLOCK, 2048), F32),
        ],
        compiler_params=params("arbitrary"),
        cost_estimate=cost(1 << 20, 1 << 16),
        name="spread",
    )(both)


FF_TILE = 1408


def pack(sc, w_ref, g1_ref, g2_ref, st_ref, gu_ref, dn_ref, wide_ref, gus_ref, dns_ref):
    st = st_ref[...]
    info = [g1_ref[...].astype(F32), g2_ref[...].astype(F32)]
    info += [(st // 256).astype(F32), (st % 256).astype(F32), jnp.zeros((1, BLOCK), F32)]
    info = jnp.broadcast_to(jnp.concatenate(info, axis=1), (16, 5 * BLOCK)).astype(BF16)
    for x in range(NX):
        j = (x - sc[1]) & 3
        k = w_ref[:, 2048 + 64 * x : 2048 + 64 * (x + 1)]
        v = w_ref[:, 2304 + 64 * x : 2304 + 64 * (x + 1)]
        kv = jnp.concatenate([k, v], axis=1)
        for zhi in range(2):
            wide_ref[NX * zhi + x, :BLOCK, :512] = w_ref[:, 512 * x : 512 * (x + 1)]
            wide_ref[NX * zhi + x, :BLOCK, 512:] = kv
            wide_ref[NX * zhi + x, BLOCK:, :] = info
        gus_ref[j, :, :FF_TILE] = gu_ref[:, FF_TILE * x : FF_TILE * (x + 1)]
        up = 4 * FF_TILE + FF_TILE * x
        gus_ref[j, :, FF_TILE:] = gu_ref[:, up : up + FF_TILE]
    for j in range(11):
        dns_ref[:, 256 * j : 256 * (j + 1)] = dn_ref[32 * j : 32 * (j + 1), :]


def call_pack(sc, w_qkv, gain_1, gain_2, starts, w_gu, w_dn):
    vec = pl.BlockSpec((1, BLOCK), lambda i, s: (0, 0))
    return pl.pallas_call(
        pack,
        grid_spec=pltpu.PrefetchScalarGridSpec(
            num_scalar_prefetch=1,
            grid=(1,),
            in_specs=[
                pl.BlockSpec((BLOCK, 2560), lambda i, s: (0, 0)),
                vec,
                vec,
                vec,
                pl.BlockSpec((16, 8 * FF_TILE), lambda i, s: (s[0], 0)),
                pl.BlockSpec((352, 256), lambda i, s: (0, s[0])),
            ],
            out_specs=[
                pl.BlockSpec((8, BLOCK + 16, 640), lambda i, s: (0, 0, 0)),
                pl.BlockSpec((NX, 16, 2 * FF_TILE), lambda i, s: (0, 0, 0)),
                pl.BlockSpec((32, 2 * FF_TILE), lambda i, s: (0, 0)),
            ],
        ),
        out_shape=[
            jax.ShapeDtypeStruct((8, BLOCK + 16, 640), BF16),
            jax.ShapeDtypeStruct((NX, 16, 2 * FF_TILE), BF16),
            jax.ShapeDtypeStruct((32, 2 * FF_TILE), BF16),
        ],
        compiler_params=params("arbitrary"),
        cost_estimate=cost(1 << 20, 1 << 16),
        name="pack",
    )(sc, w_qkv, gain_1[None], gain_2[None], starts[None], w_gu, w_dn)


def down_back(c0, c1, c2, c3, w_ref, d_ref, wdn_ref):
    r = pl.program_id(0)
    for p in range(2):
        for c in range(2):
            for j in range(11):
                at = (2 * p + c) * 352 + 32 * j
                wdn_ref[at : at + 32, :] = w_ref[0, p, c, :, 256 * j : 256 * (j + 1)]
    cots = jnp.concatenate([c0[...], c1[...], c2[...], c3[...]], axis=0)
    part = lax.dot_general(
        cots, wdn_ref[...], (((1,), (1,)), ((), ())), preferred_element_type=F32
    )

    @pl.when(r == 0)
    def _():
        d_ref[...] = part

    @pl.when(r > 0)
    def _():
        d_ref[...] += part


def call_down_back(cots, ffn):
    return pl.pallas_call(
        down_back,
        grid=(8,),
        in_specs=[pl.BlockSpec((BLOCK, 256), lambda r: (0, r))] * 4
        + [pl.BlockSpec((1, 2, 2, 32, 2 * FF_TILE), lambda r: (r, 0, 0, 2, 0))],
        out_specs=[
            pl.BlockSpec((NX * BLOCK, FF_TILE), lambda r: (0, 0)),
            pl.BlockSpec((FF_TILE, 256), lambda r: (0, r)),
        ],
        out_shape=[
            jax.ShapeDtypeStruct((NX * BLOCK, FF_TILE), F32),
            jax.ShapeDtypeStruct((FF_TILE, 2048), BF16),
        ],
        compiler_params=params("arbitrary"),
        cost_estimate=cost(1 << 33, 1 << 20),
        name="down_back",
    )(*cots, ffn)


def natural(w_ref, pick, me):
    parts = []
    for zhi, x, c in pick:
        at = pl.ds(pl.multiple_of(((me - x) & 3) * 16, 16), 16)
        parts.append(w_ref[:, zhi, c, at, :].reshape(BLOCK, BLOCK))
    return jnp.concatenate(parts, axis=0)


ORDER = [(zhi, x, c) for zhi in range(2) for x in range(NX) for c in range(2)]
FF_STEPS = FF_TILE // BLOCK


def feed_forward(
    sc, n0, n1, n2, n3, wg_ref, wu_ref, w_ref, d_ref, o0, o1, o2, o3, act_ref, dgu_ref, n_s, act_s, dg_s
):
    k = pl.program_id(0)

    @pl.when(k == 0)
    def _():
        for j, n in enumerate((n0, n1, n2, n3)):
            n_s[BLOCK * j : BLOCK * (j + 1), :] = n[...]

    @pl.when(k < FF_STEPS)
    def _():
        w = [natural(ref, ORDER, sc[0]) for ref in (wg_ref, wu_ref)]
        w = jnp.concatenate(w, axis=1)
        both = jnp.dot(n_s[...], w, preferred_element_type=F32)
        gate, up = both[:, :BLOCK], both[:, BLOCK:]
        d_act = d_ref[...]
        sig = 1.0 / (1.0 + jnp.exp(-gate))
        silu = gate * sig
        at = pl.ds(pl.multiple_of(k * BLOCK, BLOCK), BLOCK)
        up_at = pl.ds(pl.multiple_of(FF_TILE + k * BLOCK, BLOCK), BLOCK)
        act_s[:, at] = (silu * up).astype(BF16)
        d_gate = d_act * up * (sig * (1.0 + gate * (1.0 - sig)))
        dg_s[:, at] = d_gate.astype(BF16)
        dg_s[:, up_at] = (d_act * silu).astype(BF16)

    @pl.when(k == FF_STEPS)
    def _():
        act_ref[...] = act_s[...]
        dgu_ref[...] = dg_s[...]

    @pl.when(k >= FF_STEPS)
    def _():
        w = jnp.concatenate(
            [w_ref[:, 0, c].reshape(BLOCK, 2 * FF_TILE) for c in range(2)], axis=0
        )
        d = lax.dot_general(
            dg_s[...], w, (((1,), (1,)), ((), ())), preferred_element_type=F32
        ).astype(BF16)
        for j, o in enumerate((o0, o1, o2, o3)):
            o[...] = d[BLOCK * j : BLOCK * (j + 1)]


def call_feed_forward(x, n2, ffn, d_act):
    def tile(k):
        return jnp.minimum(k, FF_STEPS - 1)

    def later(k):
        return jnp.maximum(k - FF_STEPS, 0)

    def row_block(k, s):
        return (0, later(k) >> 2, 0, (s[0] - later(k)) & 3, 0)

    whole = pl.BlockSpec((BLOCK, 2048), lambda k, s: (0, 0))
    out = pl.BlockSpec((BLOCK, 256), lambda k, s: (0, later(k)))
    return pl.pallas_call(
        feed_forward,
        grid_spec=pltpu.PrefetchScalarGridSpec(
            num_scalar_prefetch=1,
            grid=(FF_STEPS + 8,),
            in_specs=[whole] * 4
            + [
                pl.BlockSpec((8, 2, 2, 64, BLOCK), lambda k, s: (0, 0, 0, 0, tile(k))),
                pl.BlockSpec((8, 2, 2, 64, BLOCK), lambda k, s: (0, 0, 0, 0, FF_STEPS + tile(k))),
                pl.BlockSpec((8, 1, 2, 16, 2 * FF_TILE), row_block),
                pl.BlockSpec((NX * BLOCK, BLOCK), lambda k, s: (0, tile(k))),
            ],
            out_specs=[out] * 4
            + [
                pl.BlockSpec((NX * BLOCK, FF_TILE), lambda k, s: (0, 0)),
                pl.BlockSpec((NX * BLOCK, 2 * FF_TILE), lambda k, s: (0, 0)),
            ],
            scratch_shapes=[
                pltpu.VMEM((NX * BLOCK, 2048), BF16),
                pltpu.VMEM((NX * BLOCK, FF_TILE), BF16),
                pltpu.VMEM((NX * BLOCK, 2 * FF_TILE), BF16),
            ],
        ),
        out_shape=[jax.ShapeDtypeStruct((BLOCK, 2048), BF16)] * 4
        + [
            jax.ShapeDtypeStruct((NX * BLOCK, FF_TILE), BF16),
            jax.ShapeDtypeStruct((NX * BLOCK, 2 * FF_TILE), BF16),
        ],
        compiler_params=params("arbitrary"),
        cost_estimate=cost(1 << 20, 1 << 16),
        name="feed_forward",
    )(x[None], *n2, ffn, ffn, ffn, d_act)


def ffn_grads(sc, n0, n1, n2, n3, dgu_ref, act_ref, c0, c1, c2, c3, *rest):
    i = pl.program_id(0)
    added, outs, act_t, g_ref = rest[:-4], rest[-4:-2], rest[-2], rest[-1]

    def put(which, place, value):
        if added:
            value = value + added[which][place].astype(F32)
        outs[which][place] = value.astype(BF16)

    @pl.when(i < NX)
    def _():
        lhs = []
        for zhi in range(2):
            shard = (zhi * NX + jnp.minimum(i, NX - 1)) * 2 + sc[0]
            at = pl.ds(pl.multiple_of(shard * BLOCK, BLOCK), BLOCK)
            lhs.append(jnp.concatenate([n[:, at] for n in (n0, n1, n2, n3)], axis=0))
        lhs = jnp.concatenate(lhs, axis=1)
        for half in range(2):
            cols = slice(FF_TILE * half, FF_TILE * (half + 1))
            g_ref[:, :FF_TILE] = lax.dot_general(
                lhs, dgu_ref[:, cols], (((0,), (0,)), ((), ())), preferred_element_type=F32
            )
            for zhi in range(2):
                for zlo in range(2):
                    for y in range(4):
                        row = zhi * BLOCK + (zlo * 4 + y) * 16
                        part = g_ref[row : row + 16, :FF_TILE]
                        put(0, (y, zlo * 2 + zhi, slice(None), cols), part)

    @pl.when(i == NX)
    def _():
        act_t[...] = act_ref[...].T

    @pl.when(i >= NX)
    def _():
        lhs = []
        for p in range(2):
            for j in range(11):
                row = (2 * p + sc[0]) * 352 + 32 * j + 16 * (i - NX)
                lhs.append(act_t[pl.ds(pl.multiple_of(row, 16), 16), :])
        lhs = jnp.concatenate(lhs, axis=0)
        for zlo in range(2):
            cols = slice(1024 * zlo, 1024 * (zlo + 1))
            cots = jnp.concatenate([c[:, cols] for c in (c0, c1, c2, c3)], axis=0)
            g = jnp.dot(lhs, cots, preferred_element_type=F32)
            for p in range(2):
                for j in range(11):
                    row = p * 176 + 16 * j
                    for y in range(4):
                        part = g[row : row + 16, 256 * y : 256 * (y + 1)]
                        to = slice(256 * j, 256 * (j + 1))
                        put(1, (zlo * 2 + p, y, slice(None), to), part)


def call_ffn_grads(core, n2, d_gu, act, cots, *added):
    const = pl.BlockSpec((BLOCK, 2048), lambda i, s: (0, 0))
    tile = (4, 4, 16, 2 * FF_TILE)
    outs = [
        pl.BlockSpec(tile, lambda i, s: (0, 0, jnp.minimum(i, NX - 1), 0)),
        pl.BlockSpec(tile, lambda i, s: (0, 0, jnp.maximum(i - NX, 0), 0)),
    ]
    return pl.pallas_call(
        ffn_grads,
        grid_spec=pltpu.PrefetchScalarGridSpec(
            num_scalar_prefetch=1,
            grid=(NX + 2,),
            in_specs=[const] * 4
            + [pl.BlockSpec((NX * BLOCK, 2 * FF_TILE), lambda i, s: (0, 0))]
            + [pl.BlockSpec((NX * BLOCK, FF_TILE), lambda i, s: (0, 0))]
            + [const] * 4
            + outs[: len(added)],
            out_specs=outs,
            scratch_shapes=[
                pltpu.VMEM((FF_TILE, NX * BLOCK), BF16),
                pltpu.VMEM((2 * BLOCK, FF_TILE), F32),
            ],
        ),
        out_shape=[
            jax.ShapeDtypeStruct((4, 4, 64, 2 * FF_TILE), BF16),
            jax.ShapeDtypeStruct((4, 4, 32, 2 * FF_TILE), BF16),
        ],
        compiler_params=params("arbitrary"),
        cost_estimate=cost(1 << 33, 1 << 20),
        name="ffn_grads_mine" if added else "ffn_grads_other",
    )(core[None], *n2, d_gu, act, *cots, *added)


def attention_grads(sc, n_ref, dq_ref, o_ref, db_ref, *rest):
    added, out_ref, qkv_s, out_s = rest[:-3], rest[-3], rest[-2], rest[-1]

    def put(place, value):
        if added:
            value = value + added[0][place].astype(F32)
        out_ref[place] = value.astype(BF16)

    for zhi in range(2):
        lhs = []
        for x in range(NX):
            at = pl.ds(pl.multiple_of(((zhi * NX + x) * 2 + sc[0]) * BLOCK, BLOCK), BLOCK)
            lhs.append(n_ref[:, at])
        lhs = jnp.concatenate(lhs, axis=1)
        qkv_s[...] = lax.dot_general(
            lhs, dq_ref[...], (((0,), (1,)), ((), ())), preferred_element_type=F32
        )
        for x in range(NX):
            for replica in range(8):
                row = BLOCK * x + 16 * replica
                to = slice(16 * x, 16 * (x + 1))
                put((replica % 4, replica // 4 * 2 + zhi, to, slice(0, 640)), qkv_s[row : row + 16, :])
    for p in range(2):
        rows = o_ref[pl.ds(pl.multiple_of((2 * p + sc[0]) * BLOCK, BLOCK), BLOCK), :]
        out_s[...] = jnp.dot(rows, db_ref[...], preferred_element_type=F32)
        for replica in range(8):
            for half in range(2):
                part = out_s[64 * half : 64 * (half + 1), 256 * replica : 256 * (replica + 1)]
                at = 640 + 256 * half
                put((replica % 4, replica // 4 * 2 + p, slice(None), slice(at, at + 256)), part)


def call_attention_grads(core, n1, d_qkv, ob, d_br, *added):
    vmem = pl.BlockSpec(memory_space=pltpu.VMEM)
    return pl.pallas_call(
        attention_grads,
        in_specs=[pl.BlockSpec(memory_space=pltpu.SMEM)] + [vmem] * (4 + len(added)),
        out_specs=vmem,
        out_shape=jax.ShapeDtypeStruct((4, 4, 64, 1152), BF16),
        scratch_shapes=[pltpu.VMEM((4 * BLOCK, 640), F32), pltpu.VMEM((BLOCK, 2048), F32)],
        compiler_params=params(),
        cost_estimate=cost(1 << 33, 1 << 20),
        name="attention_grads_mine" if added else "attention_grads_other",
    )(core[None], n1, d_qkv, ob, d_br, *added)


def shift_x(a, k):
    return lax.ppermute(a, "x", [(i, (i + k) % NX) for i in range(NX)])


def gathered_x(a, between=lambda: ()):
    half = a.shape[0] // 2
    t1, t3 = shift_x(a, 3), shift_x(a, 1)
    t1, t3 = lax.optimization_barrier((t1, t3, *between()))[:2]
    return [a, t1, jnp.concatenate([shift_x(t1[:half], 3), shift_x(t3[half:], 1)]), t3]


def moved_x(parts):
    half = parts[2].shape[0] // 2
    up, down = shift_x(parts[2][:half], 1), shift_x(parts[2][half:], 3)
    up = (parts[1][:half].astype(F32) + up.astype(F32)).astype(BF16)
    down = (parts[3][half:].astype(F32) + down.astype(F32)).astype(BF16)
    up = jnp.concatenate([up, parts[1][half:]])
    down = jnp.concatenate([parts[3][:half], down])
    return [parts[0], shift_x(up, 1), shift_x(down, 3)]


def added(parts):
    return sum(p.astype(F32) for p in parts)


def summed_x(parts):
    return added(moved_x(parts))


def sent(parts, axes, me=0):
    out = []
    for j in range(4):
        part = lax.dynamic_index_in_dim(parts, (me + j) % 4, 0, keepdims=False)
        out.append(lax.ppermute(part, axes, [(i, (i + j) % 4) for i in range(4)]) if j else part)
    return out


def total(parts):
    return parts.astype(F32).sum(axis=0).astype(BF16)


def pieces(a):
    return [a[BLOCK * j : BLOCK * (j + 1)] for j in range(NX)]


def summed(t, axes):
    return exchange(t, axes).astype(F32).sum(axis=0).astype(BF16)


def to_heads(first):
    pairs = []
    for s_zhi in range(2):
        for s_x in range(NX):
            d_zhi = s_x % 2 if first else 1 - s_x % 2
            pairs.append((s_zhi * NX + s_x, d_zhi * NX + 2 * s_zhi + s_x // 2))
    return pairs


def to_owners(first):
    return [(d, s) for s, d in to_heads(first)]


def after(a, *others):
    return lax.optimization_barrier((a, *others))[0]


def body(tok, cot, starts, gain_1, w_qkv, w_out, gain_2, w_gu, w_dn):
    zlo, y, zhi, x, core = (lax.axis_index(a) for a in AXES)
    replica = zlo * 4 + y
    rows, dim = tok.shape
    q_cols = GROUP * HEAD_SIZE
    ff_shard = w_dn.shape[0]
    slab = rows // 8

    t1, t3 = shift_x(tok, 3), shift_x(tok, 1)
    toks = [tok, t1, shift_x(t1[: rows // 2], 3), shift_x(t3[rows // 2 :], 1), t3]
    w_far = swap(w_out, "zhi")
    place = jnp.stack([replica, x])
    wide, gu_slab, dn_slab = call_pack(place, w_qkv, gain_1, gain_2, starts, w_gu, w_dn)
    qkv_cols = wide.shape[2]
    wide = exchange(wide, CHIP)

    gu_slab = jnp.concatenate(sent(gu_slab, "x"), axis=0)
    dn_slab = lax.ppermute(dn_slab, CHIP, to_heads(True))
    slabs = jnp.concatenate([gu_slab, dn_slab])
    slabs = after(slabs, wide, t1, t3)
    ffn = lax.all_gather(slabs, YZC, axis=0)
    ffn = ffn.reshape(8, 2, 2, NX * slab + 32, 2 * FF_TILE)

    inputs = tok.astype(F32)
    scaled_one, rstd_one = rms_forward(inputs)
    blocks = (x + jnp.arange(NX, dtype=jnp.int32)) % NX
    block_ids = zhi * 8 + 2 * blocks + core
    st = lax.dynamic_slice_in_dim(wide, zhi * NX, NX, 0)[:, rows, 2 * rows : 4 * rows]
    st = st.astype(F32).reshape(NX, 2, rows)
    st = (st[:, 0] * 256.0 + st[:, 1]).astype(jnp.int32)[blocks]
    where_at = block_ids[:, None] * rows + jnp.arange(rows, dtype=jnp.int32)[None, :]
    pos = (where_at - st).reshape(1, NX * rows).astype(F32)
    freqs = jnp.exp(jnp.arange(32, dtype=F32) * (-2.0 * math.log(ROPE_BASE) / HEAD_SIZE))
    angles = freqs[:, None] * pos
    cos, sin = jnp.cos(angles), jnp.sin(angles)
    n1, q_t, kv, wq, gains = call_project(core[None], toks, wide, swap(wide, "core"), cos, sin)
    gain_one, gain_two = gains[0], gains[1]
    kv = jnp.concatenate([kv, swap(kv, "core")], axis=0)
    near, far = jnp.where(zhi == 0, w_out, w_far), jnp.where(zhi == 0, w_far, w_out)
    even = x % 2 == 0
    part_a, part_b = jnp.where(even, near, far), jnp.where(even, far, near)
    part_a, part_b, cot_in = lax.optimization_barrier((part_a, part_b, cot, kv))[:3]
    kv = jnp.concatenate([kv, swap(kv, "zhi")], axis=0)
    part_a = lax.ppermute(part_a, "x", [(0, 0), (1, 2), (2, 1), (3, 3)])
    part_b = lax.ppermute(part_b, "x", [(0, 2), (1, 0), (2, 3), (3, 1)])
    firsts = jnp.min(st, axis=1) // CHUNK
    clears = (jnp.max(st, axis=1) + CHUNK - 1) // CHUNK
    sc = jnp.concatenate([zhi[None], x[None], core[None], firsts, clears]).astype(jnp.int32)
    st = st[:, None, :]
    o, ob, qr, lse = call_forward(sc, q_t, cos, sin, st, kv)
    cots = [cot_in, shift_x(cot_in, 3), shift_x(cot_in, 2), shift_x(cot_in, 1)]
    ob, *cots = lax.optimization_barrier((ob, *cots))
    part_a, part_b = after(part_a, ob), after(part_b, ob)
    *parts, wo = call_out_project(
        jnp.stack([x // 2, core]), ob, part_a, part_b, swap(part_a, "core"), swap(part_b, "core")
    )
    hidden = inputs + summed_x(parts)

    d_act, wdn = call_down_back(cots, ffn)
    scaled_two, rstd_two = rms_forward(hidden)
    n2 = gathered_x((scaled_two * gain_two[None, :]).astype(BF16), lambda: (d_act,))
    *d_n2, act, d_gu = call_feed_forward(x, n2, ffn, d_act)

    other = call_ffn_grads(1 - core, n2, d_gu, act, cots)
    d_n2 = moved_x(d_n2)
    other = lax.optimization_barrier((*other, *d_n2[1:]))[:2]
    other = [swap(g, "core") for g in other]
    g_gu, g_dn = call_ffn_grads(core, n2, d_gu, act, cots, *other)
    d_mid, gain_two_term = rms_backward(added(d_n2), scaled_two, rstd_two, gain_two)
    d_mid = cot.astype(F32) + d_mid
    d_br = gathered_x(d_mid.astype(BF16), lambda: (g_gu, g_dn))
    z = zlo * 2 + zhi
    g_gu = exchange(g_gu.reshape(4, 4 * 64, 2 * FF_TILE), "y")
    g_dn = sent(g_dn, ("zlo", "zhi"), z)
    d_br = jnp.concatenate(d_br)

    do = mm(wo, d_br, ((1,), (1,)), BF16)
    dq, dkv = call_backward(sc, qr, do, o, lse, cos, sin, st, kv)
    dkv, *g_dn = lax.optimization_barrier((dkv, *g_dn))
    dkv = dkv.reshape(2, 2, NX, 2 * HEAD_SIZE, rows)
    dkv = dkv[:, 0].astype(F32) + swap(dkv[:, 1], "core").astype(F32)
    dkv = dkv[0] + swap(dkv[1].astype(BF16), "zhi").astype(F32)
    g_dn = added(g_dn).astype(BF16)
    dkv = dkv.transpose(1, 0, 2).reshape(2 * HEAD_SIZE, NX * rows)
    k1, k2 = dkv[:32], dkv[32:64]
    dkv = jnp.concatenate([k1 * cos + k2 * sin, k2 * cos - k1 * sin, dkv[64:]], axis=0)
    d_qkv = jnp.concatenate([dq, dkv.astype(BF16)], axis=0)
    d_qkv, g_gu = lax.optimization_barrier((d_qkv, g_gu))
    d_n1 = mm(d_qkv, wq, ((0,), (1,)), BF16)
    d_qkv, ob, g_dn = lax.optimization_barrier((d_qkv, ob, g_dn, d_n1))[:3]
    d_n1 = moved_x(pieces(d_n1))
    other = swap(call_attention_grads(1 - core, n1, d_qkv, ob, d_br), "core")
    g_attn = call_attention_grads(core, n1, d_qkv, ob, d_br, other)

    g_gu, g_attn = lax.optimization_barrier((g_gu, g_attn))
    g_gu = exchange(total(g_gu.reshape(4, 4, 64, 2 * FF_TILE)), ("zlo", "zhi"))
    g_attn = sent(g_attn, "y", y)
    g_dn = sent(after(g_dn, g_attn[1]), "y", y)
    g_attn = sent(added(g_attn).astype(BF16), ("zlo", "zhi"), z)
    g_gu = exchange(total(g_gu).reshape(NX, slab, 2 * FF_TILE), "x")
    g_dn = lax.ppermute(added(g_dn).astype(BF16), CHIP, to_owners(True))
    *g_attn, g_gu, g_dn = lax.optimization_barrier((*g_attn, g_gu, g_dn))
    d_n1 = lax.optimization_barrier((*d_n1, *g_attn))[:3]
    act = after(act, *d_n1)
    mixed = moved_x(pieces(mm(act, wdn, ((1,), (0,)), BF16)))
    d_in, gain_one_term = rms_backward(added(d_n1), scaled_one, rstd_one, gain_one)
    input_grad = (d_mid + d_in).astype(BF16)
    g_attn = added(g_attn).astype(BF16)
    g_out = lax.ppermute(g_attn[:, 640:], CHIP, to_owners(True))
    g_qkv = jnp.stack(sent(g_attn[:, :640].reshape(NX, slab, qkv_cols), "x", x))
    g_qkv = g_qkv[(x - jnp.arange(NX, dtype=jnp.int32)) % NX]
    g_qkv = g_qkv.reshape(NX * slab, qkv_cols)
    attn = [g_qkv[:32], g_out[:32], g_qkv[32:], g_out[32:], jnp.zeros((32, 512), BF16)]
    attn = jnp.concatenate(attn, axis=1)
    both = jnp.concatenate([g_gu.reshape(NX * slab, 2 * FF_TILE), g_dn, attn])
    payload = both = after(both, input_grad)
    both = lax.all_gather(both, REP, axis=0)
    g_gu, g_dn, g_qkv, g_out = call_spread(both)

    terms = jnp.stack([gain_one_term, gain_two_term]).reshape(2, 16, rows).transpose(1, 0, 2)
    terms = exchange(after(terms, payload), SHARD).sum(axis=0)
    terms = everywhere(terms.astype(BF16), REP, 8).astype(F32).sum(axis=0)
    mixed = hidden + added(mixed)

    return (
        mixed.astype(BF16),
        input_grad,
        terms[0],
        g_qkv,
        g_out,
        terms[1],
        g_gu,
        g_dn,
    )


def solution(mesh):
    fine = Mesh(mesh.devices.reshape(2, 4, 2, 4, 2), AXES)
    row, two = P(AXES), P(AXES, None)
    vec, mat = P(SHARD), P(SHARD, None)
    return jax.shard_map(
        body,
        mesh=fine,
        in_specs=(two, two, row, vec, mat, mat, vec, mat, mat),
        out_specs=(two, two, vec, mat, mat, vec, mat, mat),
        check_vma=False,
    )
```

```python
import math

import jax
import jax.numpy as jnp
from jax import lax
from jax.experimental import pallas as pl
from jax.experimental.pallas import tpu as pltpu
from jax.sharding import Mesh
from jax.sharding import PartitionSpec as P

QUERY_HEADS = 32
KEY_VALUE_HEADS = 4
HEAD_SIZE = 64
GROUP = QUERY_HEADS // KEY_VALUE_HEADS
EPS = 1e-05
ROPE_BASE = 10000.0
NEG = -1e30
BLOCK = 128
CHUNK = 4 * BLOCK
SCALE = 1.0 / math.sqrt(HEAD_SIZE)

AXES = ("zlo", "y", "zhi", "x", "core")
REP = ("zlo", "y")
SHARD = ("zhi", "x", "core")
CHIP = ("zhi", "x")
YZ = ("zlo", "y", "zhi")
YZC = ("zlo", "y", "zhi", "core")
NX = 4

F32 = jnp.float32
BF16 = jnp.bfloat16


def exchange(a, axes):
    return lax.all_to_all(a, axes, split_axis=0, concat_axis=0, tiled=True)


def everywhere(a, axes, n):
    return exchange(jnp.broadcast_to(a[None], (n,) + a.shape), axes)


def swap(a, axis):
    return lax.ppermute(a, axis, [(0, 1), (1, 0)])


def in_order(coord, mine, other, axis):
    return jnp.where(
        coord == 0, jnp.stack([mine, other], axis=axis), jnp.stack([other, mine], axis=axis)
    )


def mm(left, right, dims, out=F32):
    return lax.dot_general(
        left, right, ((dims[0], dims[1]), ((), ())), preferred_element_type=F32
    ).astype(out)


def rms_forward(rows):
    rstd = lax.rsqrt(jnp.mean(rows * rows, axis=1, keepdims=True) + EPS)
    return rows * rstd, rstd


def rms_backward(d_normed, scaled, rstd, gain):
    gain_term = jnp.sum(d_normed * scaled, axis=0)
    inner = d_normed * gain[None, :]
    d_values = rstd * (inner - scaled * jnp.mean(inner * scaled, axis=1, keepdims=True))
    return d_values, gain_term


def heads_to_lanes(ref):
    return jnp.concatenate(
        [ref[HEAD_SIZE * h : HEAD_SIZE * (h + 1), :] for h in range(GROUP)], axis=1
    )


def chunk_slots(c, zhi, x, core):
    slots = []
    for i in range(CHUNK // BLOCK):
        n = c * (CHUNK // BLOCK) + i
        slots.append(((n >> 3) ^ zhi) * 8 + ((n & 1) ^ core) * 4 + (((n >> 1) - x) & 3))
    return slots


def allowed_mask(c, st, block):
    keys = lax.broadcasted_iota(jnp.int32, (CHUNK, 1), 0) + c * CHUNK
    lanes = lax.broadcasted_iota(jnp.int32, (1, GROUP * BLOCK), 1) % BLOCK
    return (keys >= st) & (keys <= block * BLOCK + lanes)


def over_chunks(step, state, first, clear, last):
    clear = jnp.minimum(clear, last)
    state = lax.fori_loop(first, clear, lambda c, v: step(c, v, True), state)
    state = lax.fori_loop(clear, last, lambda c, v: step(c, v, False), state)
    return step(last, state, True)


def attention_forward(sc, q_ref, cos_ref, sin_ref, st_ref, kv_ref, o_ref, ob_ref, qr_ref, lse_ref):
    b = pl.program_id(0)
    zhi, x, core, first = sc[0], sc[1], sc[2], sc[3 + b]
    block = zhi * 8 + 2 * ((x + b) & 3) + core
    cos, sin = cos_ref[...], sin_ref[...]
    turned = []
    for h in range(GROUP):
        u1 = q_ref[HEAD_SIZE * h : HEAD_SIZE * h + 32, :]
        u2 = q_ref[HEAD_SIZE * h + 32 : HEAD_SIZE * h + 64, :]
        turned.append(jnp.concatenate([u1 * cos - u2 * sin, u2 * cos + u1 * sin], axis=0))
    q = jnp.concatenate(turned, axis=1).astype(BF16) * jnp.asarray(SCALE, BF16)
    qr_ref[0] = q
    st = jnp.concatenate([st_ref[0]] * GROUP, axis=1)

    def step(c, state, masked):
        m, l, acc = state
        slots = chunk_slots(c, zhi, x, core)
        k = jnp.concatenate([kv_ref[n, :HEAD_SIZE, :] for n in slots], axis=1)
        v = jnp.concatenate([kv_ref[n, HEAD_SIZE:, :] for n in slots], axis=1)
        s = lax.dot_general(k, q, (((0,), (0,)), ((), ())), preferred_element_type=F32)
        if masked:
            s = jnp.where(allowed_mask(c, st, block), s, NEG)
        m2 = jnp.maximum(m, jnp.max(s, axis=0, keepdims=True))
        p = jnp.exp(s - m2)
        al = jnp.exp(m - m2)
        l = l * al + jnp.sum(p, axis=0, keepdims=True)
        acc = acc * al + lax.dot_general(
            v, p.astype(BF16), (((1,), (0,)), ((), ())), preferred_element_type=F32
        )
        return m2, l, acc

    rows = GROUP * BLOCK
    state = (
        jnp.full((1, rows), NEG, F32),
        jnp.zeros((1, rows), F32),
        jnp.zeros((HEAD_SIZE, rows), F32),
    )
    m, l, acc = over_chunks(step, state, first, sc[7 + b], block // (CHUNK // BLOCK))
    o = acc / l
    for h in range(GROUP):
        part = o[:, BLOCK * h : BLOCK * (h + 1)]
        o_ref[HEAD_SIZE * h : HEAD_SIZE * (h + 1), :] = part
        ob_ref[HEAD_SIZE * h : HEAD_SIZE * (h + 1), :] = part.astype(BF16)
    lse_ref[0] = m + jnp.log(l)


def attention_backward(
    sc, qr_ref, do_ref, o_ref, lse_ref, cos_ref, sin_ref, st_ref, kv_ref, dq_ref, dkv_ref, acc_ref
):
    b = pl.program_id(0)
    zhi, x, core, first = sc[0], sc[1], sc[2], sc[3 + b]
    block = zhi * 8 + 2 * ((x + b) & 3) + core

    @pl.when(b == 0)
    def _():
        acc_ref[...] = jnp.zeros_like(acc_ref)

    q = qr_ref[0]
    do = heads_to_lanes(do_ref)
    delta = jnp.sum(do.astype(F32) * heads_to_lanes(o_ref), axis=0, keepdims=True)
    q_rows = q.T
    do_rows = do.T
    lse = lse_ref[0]
    st = jnp.concatenate([st_ref[0]] * GROUP, axis=1)

    def step(c, dq, masked):
        slots = chunk_slots(c, zhi, x, core)
        k = jnp.concatenate([kv_ref[n, :HEAD_SIZE, :] for n in slots], axis=1)
        v = jnp.concatenate([kv_ref[n, HEAD_SIZE:, :] for n in slots], axis=1)
        s = lax.dot_general(k, q, (((0,), (0,)), ((), ())), preferred_element_type=F32)
        if masked:
            s = jnp.where(allowed_mask(c, st, block), s, NEG)
        p = jnp.exp(s - lse)
        dp = lax.dot_general(v, do, (((0,), (0,)), ((), ())), preferred_element_type=F32)
        ds = (p * (dp - delta)).astype(BF16)
        pb = p.astype(BF16)
        dk = jnp.dot(ds, q_rows, preferred_element_type=F32)
        dv = jnp.dot(pb, do_rows, preferred_element_type=F32)
        both = jnp.concatenate([dk, dv], axis=1)
        for i, n in enumerate(slots):
            acc_ref[n] += both[BLOCK * i : BLOCK * (i + 1)]
        return dq + jnp.dot(k, ds, preferred_element_type=F32)

    dq = jnp.zeros((HEAD_SIZE, GROUP * BLOCK), F32)
    dq = over_chunks(step, dq, first, sc[7 + b], block // (CHUNK // BLOCK))
    dq = dq * SCALE
    cos, sin = cos_ref[...], sin_ref[...]
    for h in range(GROUP):
        g1 = dq[:32, BLOCK * h : BLOCK * (h + 1)]
        g2 = dq[32:, BLOCK * h : BLOCK * (h + 1)]
        dq_ref[HEAD_SIZE * h : HEAD_SIZE * h + 32, :] = (g1 * cos + g2 * sin).astype(BF16)
        dq_ref[HEAD_SIZE * h + 32 : HEAD_SIZE * h + 64, :] = (g2 * cos - g1 * sin).astype(BF16)

    @pl.when(b == NX - 1)
    def _():
        for n in range(16):
            dkv_ref[n] = acc_ref[n].T.astype(BF16)


VMEM_LIMIT = 48 * 1024 * 1024


def call_forward(sc, qkv_t, cos, sin, st, kv):
    rows, toks = GROUP * HEAD_SIZE, NX * BLOCK
    lanes = GROUP * BLOCK
    tile = pl.BlockSpec((rows, BLOCK), lambda b, s: (0, b))
    trig = pl.BlockSpec((32, BLOCK), lambda b, s: (0, b))
    return pl.pallas_call(
        attention_forward,
        grid_spec=pltpu.PrefetchScalarGridSpec(
            num_scalar_prefetch=1,
            grid=(NX,),
            in_specs=[
                tile,
                trig,
                trig,
                pl.BlockSpec((1, 1, BLOCK), lambda b, s: (b, 0, 0)),
                pl.BlockSpec((16, BLOCK, BLOCK), lambda b, s: (0, 0, 0)),
            ],
            out_specs=[
                tile,
                tile,
                pl.BlockSpec((1, HEAD_SIZE, lanes), lambda b, s: (b, 0, 0)),
                pl.BlockSpec((1, 1, lanes), lambda b, s: (b, 0, 0)),
            ],
        ),
        out_shape=[
            jax.ShapeDtypeStruct((rows, toks), F32),
            jax.ShapeDtypeStruct((rows, toks), BF16),
            jax.ShapeDtypeStruct((NX, HEAD_SIZE, lanes), BF16),
            jax.ShapeDtypeStruct((NX, 1, lanes), F32),
        ],
        compiler_params=pltpu.CompilerParams(
            dimension_semantics=("arbitrary",), vmem_limit_bytes=VMEM_LIMIT
        ),
        cost_estimate=cost(1 << 20, 1 << 16),
        name="attention_forward",
    )(sc, qkv_t, cos, sin, st, kv)


def call_backward(sc, qr, do, o, lse, cos, sin, st, kv):
    rows, toks = GROUP * HEAD_SIZE, NX * BLOCK
    lanes = GROUP * BLOCK
    tile = pl.BlockSpec((rows, BLOCK), lambda b, s: (0, b))
    trig = pl.BlockSpec((32, BLOCK), lambda b, s: (0, b))
    whole = pl.BlockSpec((16, BLOCK, BLOCK), lambda b, s: (0, 0, 0))
    return pl.pallas_call(
        attention_backward,
        grid_spec=pltpu.PrefetchScalarGridSpec(
            num_scalar_prefetch=1,
            grid=(NX,),
            in_specs=[
                pl.BlockSpec((1, HEAD_SIZE, lanes), lambda b, s: (b, 0, 0)),
                tile,
                tile,
                pl.BlockSpec((1, 1, lanes), lambda b, s: (b, 0, 0)),
                trig,
                trig,
                pl.BlockSpec((1, 1, BLOCK), lambda b, s: (b, 0, 0)),
                whole,
            ],
            out_specs=[tile, whole],
            scratch_shapes=[pltpu.VMEM((16, BLOCK, BLOCK), F32)],
        ),
        out_shape=[
            jax.ShapeDtypeStruct((rows, toks), BF16),
            jax.ShapeDtypeStruct((16, BLOCK, BLOCK), BF16),
        ],
        compiler_params=pltpu.CompilerParams(
            dimension_semantics=("arbitrary",), vmem_limit_bytes=VMEM_LIMIT
        ),
        cost_estimate=cost(1 << 20, 1 << 16),
        name="attention_backward",
    )(sc, qr, do, o, lse, cos, sin, st, kv)


def project(
    sc, t0, t1, t2a, t2b, t3, mine, other, cos_ref, sin_ref, n_ref, q_ref, kv_ref, w_ref, gain_ref
):
    for ref, c in ((mine, sc[0]), (other, 1 - sc[0])):
        for chip in range(8):
            at = pl.ds(pl.multiple_of((2 * chip + c) * BLOCK, BLOCK), BLOCK)
            w_ref[at, :] = ref[chip, :BLOCK, :]
            info = ref[chip, BLOCK:, :].astype(F32)
            gain_ref[0:1, at] = info[0:1, :BLOCK]
            gain_ref[1:2, at] = info[0:1, BLOCK : 2 * BLOCK]
    for j, t_refs in enumerate(((t0,), (t1,), (t2a, t2b), (t3,))):
        cols = slice(BLOCK * j, BLOCK * (j + 1))
        v = jnp.concatenate([t[...] for t in t_refs], axis=0).astype(F32)
        rstd = lax.rsqrt(jnp.mean(v * v, axis=1, keepdims=True) + EPS)
        n = (v * rstd * gain_ref[0:1, :]).astype(BF16)
        n_ref[cols, :] = n
        qkv = jnp.dot(n, w_ref[...], preferred_element_type=F32).T
        rows = GROUP * HEAD_SIZE
        q_ref[:, cols] = qkv[:rows]
        cos, sin = cos_ref[:, cols], sin_ref[:, cols]
        k1, k2 = qkv[rows : rows + 32], qkv[rows + 32 : rows + 64]
        kv_ref[j, :32, :] = (k1 * cos - k2 * sin).astype(BF16)
        kv_ref[j, 32:64, :] = (k2 * cos + k1 * sin).astype(BF16)
        kv_ref[j, 64:, :] = qkv[rows + 64 :].astype(BF16)


def params(*semantics):
    return pltpu.CompilerParams(
        dimension_semantics=semantics or None, vmem_limit_bytes=VMEM_LIMIT
    )


def cost(flops, moved):
    return pl.CostEstimate(flops=flops, bytes_accessed=moved, transcendentals=0)


def call_project(sc, toks, mine, other, cos, sin):
    dim, cols = toks[0].shape[1], mine.shape[2]
    vmem = pl.BlockSpec(memory_space=pltpu.VMEM)
    return pl.pallas_call(
        project,
        in_specs=[pl.BlockSpec(memory_space=pltpu.SMEM)] + [vmem] * 9,
        out_specs=[vmem] * 5,
        out_shape=[
            jax.ShapeDtypeStruct((NX * BLOCK, dim), BF16),
            jax.ShapeDtypeStruct((GROUP * HEAD_SIZE, NX * BLOCK), F32),
            jax.ShapeDtypeStruct((NX, 2 * HEAD_SIZE, BLOCK), BF16),
            jax.ShapeDtypeStruct((dim, cols), BF16),
            jax.ShapeDtypeStruct((2, dim), F32),
        ],
        compiler_params=params(),
        cost_estimate=cost(1 << 20, 1 << 16),
        name="project",
    )(sc, *toks, mine, other, cos, sin)


def out_project(sc, o_ref, a_ref, b_ref, a2_ref, b2_ref, p0, p1, p2, p3, w_ref):
    first, core = sc[0], sc[1]
    for ref, p, c in (
        (a_ref, first, core),
        (b_ref, 1 - first, core),
        (a2_ref, first, 1 - core),
        (b2_ref, 1 - first, 1 - core),
    ):
        w_ref[pl.ds(pl.multiple_of((2 * p + c) * BLOCK, BLOCK), BLOCK), :] = ref[...]
    for half in range(2):
        at = slice(1024 * half, 1024 * (half + 1))
        d = lax.dot_general(
            o_ref[...], w_ref[:, at], (((0,), (0,)), ((), ())), preferred_element_type=F32
        ).astype(BF16)
        for j, p in enumerate((p0, p1, p2, p3)):
            p[:, at] = d[BLOCK * j : BLOCK * (j + 1)]


def call_out_project(sc, o, *w):
    vmem = pl.BlockSpec(memory_space=pltpu.VMEM)
    return pl.pallas_call(
        out_project,
        in_specs=[pl.BlockSpec(memory_space=pltpu.SMEM)] + [vmem] * 5,
        out_specs=[vmem] * 5,
        out_shape=[jax.ShapeDtypeStruct((BLOCK, 2048), BF16)] * 4
        + [jax.ShapeDtypeStruct((4 * BLOCK, 2048), BF16)],
        compiler_params=params(),
        cost_estimate=cost(1 << 20, 1 << 16),
        name="out_project",
    )(sc, o, *w)


def spread(in_ref, gu_ref, dn_ref, qkv_ref, out_ref):
    def part(row, rows, at, width):
        return in_ref[0, row : row + rows, at : at + width].astype(F32)

    for x in range(NX):
        for half in range(2):
            to = FF_TILE * (4 * half + x)
            gu_ref[:, to : to + FF_TILE] = part(16 * x, 16, FF_TILE * half, FF_TILE)
    for j in range(11):
        dn_ref[32 * j : 32 * (j + 1), :] = part(64, 32, 256 * j, 256)
    k, v = [], []
    for x in range(NX):
        row, at = 96 + 16 * (x % 2), 1152 * (x // 2)
        qkv_ref[:, 512 * x : 512 * (x + 1)] = part(row, 16, at, 512)
        k.append(part(row, 16, at + 512, 64))
        v.append(part(row, 16, at + 576, 64))
    qkv_ref[:, 2048:2304] = jnp.concatenate(k, axis=1)
    qkv_ref[:, 2304:] = jnp.concatenate(v, axis=1)
    for upper in range(2):
        for half in range(2):
            at = 1152 * upper + 640 + 256 * half
            to = 64 * half + 32 * upper
            out_ref[to : to + 32, :] = part(96, 32, at, 256)


def call_spread(both):
    return pl.pallas_call(
        spread,
        grid=(8,),
        in_specs=[pl.BlockSpec((1,) + both.shape[1:], lambda r: (r, 0, 0))],
        out_specs=[
            pl.BlockSpec((16, 8 * FF_TILE), lambda r: (r, 0)),
            pl.BlockSpec((352, 256), lambda r: (0, r)),
            pl.BlockSpec((16, 2560), lambda r: (r, 0)),
            pl.BlockSpec((BLOCK, 256), lambda r: (0, r)),
        ],
        out_shape=[
            jax.ShapeDtypeStruct((BLOCK, 8 * FF_TILE), F32),
            jax.ShapeDtypeStruct((352, 2048), F32),
            jax.ShapeDtypeStruct((BLOCK, 2560), F32),
            jax.ShapeDtypeStruct((BLOCK, 2048), F32),
        ],
        compiler_params=params("arbitrary"),
        cost_estimate=cost(1 << 20, 1 << 16),
        name="spread",
    )(both)


FF_TILE = 1408


def pack(sc, w_ref, g1_ref, g2_ref, st_ref, gu_ref, dn_ref, wide_ref, gus_ref, dns_ref):
    st = st_ref[...]
    info = [g1_ref[...].astype(F32), g2_ref[...].astype(F32)]
    info += [(st // 256).astype(F32), (st % 256).astype(F32), jnp.zeros((1, BLOCK), F32)]
    info = jnp.broadcast_to(jnp.concatenate(info, axis=1), (16, 5 * BLOCK)).astype(BF16)
    for x in range(NX):
        j = (x - sc[1]) & 3
        k = w_ref[:, 2048 + 64 * x : 2048 + 64 * (x + 1)]
        v = w_ref[:, 2304 + 64 * x : 2304 + 64 * (x + 1)]
        kv = jnp.concatenate([k, v], axis=1)
        for zhi in range(2):
            wide_ref[NX * zhi + x, :BLOCK, :512] = w_ref[:, 512 * x : 512 * (x + 1)]
            wide_ref[NX * zhi + x, :BLOCK, 512:] = kv
            wide_ref[NX * zhi + x, BLOCK:, :] = info
        gus_ref[j, :, :FF_TILE] = gu_ref[:, FF_TILE * x : FF_TILE * (x + 1)]
        up = 4 * FF_TILE + FF_TILE * x
        gus_ref[j, :, FF_TILE:] = gu_ref[:, up : up + FF_TILE]
    for j in range(11):
        dns_ref[:, 256 * j : 256 * (j + 1)] = dn_ref[32 * j : 32 * (j + 1), :]


def call_pack(sc, w_qkv, gain_1, gain_2, starts, w_gu, w_dn):
    vec = pl.BlockSpec((1, BLOCK), lambda i, s: (0, 0))
    return pl.pallas_call(
        pack,
        grid_spec=pltpu.PrefetchScalarGridSpec(
            num_scalar_prefetch=1,
            grid=(1,),
            in_specs=[
                pl.BlockSpec((BLOCK, 2560), lambda i, s: (0, 0)),
                vec,
                vec,
                vec,
                pl.BlockSpec((16, 8 * FF_TILE), lambda i, s: (s[0], 0)),
                pl.BlockSpec((352, 256), lambda i, s: (0, s[0])),
            ],
            out_specs=[
                pl.BlockSpec((8, BLOCK + 16, 640), lambda i, s: (0, 0, 0)),
                pl.BlockSpec((NX, 16, 2 * FF_TILE), lambda i, s: (0, 0, 0)),
                pl.BlockSpec((32, 2 * FF_TILE), lambda i, s: (0, 0)),
            ],
        ),
        out_shape=[
            jax.ShapeDtypeStruct((8, BLOCK + 16, 640), BF16),
            jax.ShapeDtypeStruct((NX, 16, 2 * FF_TILE), BF16),
            jax.ShapeDtypeStruct((32, 2 * FF_TILE), BF16),
        ],
        compiler_params=params("arbitrary"),
        cost_estimate=cost(1 << 20, 1 << 16),
        name="pack",
    )(sc, w_qkv, gain_1[None], gain_2[None], starts[None], w_gu, w_dn)


def down_back(c0, c1, c2, c3, w_ref, d_ref, wdn_ref):
    r = pl.program_id(0)
    for p in range(2):
        for c in range(2):
            for j in range(11):
                at = (2 * p + c) * 352 + 32 * j
                wdn_ref[0, at : at + 32, :] = w_ref[0, p, c, :, 256 * j : 256 * (j + 1)]
    cols = pl.ds(pl.multiple_of(r * 256, 256), 256)
    cots = jnp.concatenate([c[:, cols] for c in (c0, c1, c2, c3)], axis=0)
    part = lax.dot_general(
        cots, wdn_ref[0], (((1,), (1,)), ((), ())), preferred_element_type=F32
    )

    @pl.when(r == 0)
    def _():
        d_ref[...] = part

    @pl.when(r > 0)
    def _():
        d_ref[...] += part


def call_down_back(cots, ffn):
    return pl.pallas_call(
        down_back,
        grid=(8,),
        in_specs=[pl.BlockSpec((BLOCK, 2048), lambda r: (0, 0))] * 4
        + [pl.BlockSpec((1, 2, 2, 32, 2 * FF_TILE), lambda r: (r, 0, 0, 2, 0))],
        out_specs=[
            pl.BlockSpec((NX * BLOCK, FF_TILE), lambda r: (0, 0)),
            pl.BlockSpec((1, FF_TILE, 256), lambda r: (r, 0, 0)),
        ],
        out_shape=[
            jax.ShapeDtypeStruct((NX * BLOCK, FF_TILE), F32),
            jax.ShapeDtypeStruct((8, FF_TILE, 256), BF16),
        ],
        compiler_params=params("arbitrary"),
        cost_estimate=cost(1 << 33, 1 << 20),
        name="down_back",
    )(*cots, ffn)


def down_forward(act_ref, w_ref, o0, o1, o2, o3):
    d = jnp.dot(act_ref[...], w_ref[0], preferred_element_type=F32).astype(BF16)
    for j, o in enumerate((o0, o1, o2, o3)):
        o[...] = d[BLOCK * j : BLOCK * (j + 1)]


def call_down_forward(act, wdn):
    return pl.pallas_call(
        down_forward,
        grid=(8,),
        in_specs=[
            pl.BlockSpec((NX * BLOCK, FF_TILE), lambda r: (0, 0)),
            pl.BlockSpec((1, FF_TILE, 256), lambda r: (r, 0, 0)),
        ],
        out_specs=[pl.BlockSpec((BLOCK, 256), lambda r: (0, r))] * 4,
        out_shape=[jax.ShapeDtypeStruct((BLOCK, 2048), BF16)] * 4,
        compiler_params=params("arbitrary"),
        cost_estimate=cost(1 << 20, 1 << 16),
        name="down_forward",
    )(act, wdn)


ORDER = [(zhi, x, c) for zhi in range(2) for x in range(NX) for c in range(2)]
FF_STEPS = FF_TILE // BLOCK


def feed_forward(
    sc, n0, n1, n2, n3, ffn_ref, d_ref, o0, o1, o2, o3, act_ref, dgu_ref, n_s, w_s, sems
):
    k = pl.program_id(0)

    def natural(at):
        parts = []
        for zhi, x, c in ORDER:
            rows = pl.ds(pl.multiple_of(((sc[0] - x) & 3) * 16, 16), 16)
            parts.append(w_s[:, zhi, c, rows, at].reshape(BLOCK, BLOCK))
        return jnp.concatenate(parts, axis=0)

    @pl.when(k == 0)
    def _():
        copies = [
            pltpu.make_async_copy(ffn_ref.at[r, :, :, :64, :], w_s.at[r], sems.at[r])
            for r in range(8)
        ]
        for copy in copies:
            copy.start()
        for j, n in enumerate((n0, n1, n2, n3)):
            n_s[BLOCK * j : BLOCK * (j + 1), :] = n[...]
        for copy in copies:
            copy.wait()

    @pl.when(k < FF_STEPS)
    def _():
        at = pl.ds(pl.multiple_of(k * BLOCK, BLOCK), BLOCK)
        up_at = pl.ds(pl.multiple_of(FF_TILE + k * BLOCK, BLOCK), BLOCK)
        w = jnp.concatenate([natural(at), natural(up_at)], axis=1)
        both = jnp.dot(n_s[...], w, preferred_element_type=F32)
        gate, up = both[:, :BLOCK], both[:, BLOCK:]
        d_act = d_ref[...]
        sig = 1.0 / (1.0 + jnp.exp(-gate))
        silu = gate * sig
        act_ref[:, at] = (silu * up).astype(BF16)
        d_gate = d_act * up * (sig * (1.0 + gate * (1.0 - sig)))
        dgu_ref[:, at] = d_gate.astype(BF16)
        dgu_ref[:, up_at] = (d_act * silu).astype(BF16)

    @pl.when(k >= FF_STEPS)
    def _():
        i = k - FF_STEPS
        rows = pl.ds(pl.multiple_of(((sc[0] - i) & 3) * 16, 16), 16)
        w = jnp.concatenate(
            [w_s[:, i >> 2, c, rows, :].reshape(BLOCK, 2 * FF_TILE) for c in range(2)], axis=0
        )
        d = lax.dot_general(
            dgu_ref[...], w, (((1,), (1,)), ((), ())), preferred_element_type=F32
        ).astype(BF16)
        for j, o in enumerate((o0, o1, o2, o3)):
            o[...] = d[BLOCK * j : BLOCK * (j + 1)]


def call_feed_forward(x, n2, ffn, d_act):
    def tile(k):
        return jnp.minimum(k, FF_STEPS - 1)

    def later(k):
        return jnp.maximum(k - FF_STEPS, 0)

    whole = pl.BlockSpec((BLOCK, 2048), lambda k, s: (0, 0))
    out = pl.BlockSpec((BLOCK, 256), lambda k, s: (0, later(k)))
    return pl.pallas_call(
        feed_forward,
        grid_spec=pltpu.PrefetchScalarGridSpec(
            num_scalar_prefetch=1,
            grid=(FF_STEPS + 8,),
            in_specs=[whole] * 4
            + [
                pl.BlockSpec(memory_space=pl.ANY),
                pl.BlockSpec((NX * BLOCK, BLOCK), lambda k, s: (0, tile(k))),
            ],
            out_specs=[out] * 4
            + [
                pl.BlockSpec((NX * BLOCK, FF_TILE), lambda k, s: (0, 0)),
                pl.BlockSpec((NX * BLOCK, 2 * FF_TILE), lambda k, s: (0, 0)),
            ],
            scratch_shapes=[
                pltpu.VMEM((NX * BLOCK, 2048), BF16),
                pltpu.VMEM((8, 2, 2, 64, 2 * FF_TILE), BF16),
                pltpu.SemaphoreType.DMA((8,)),
            ],
        ),
        out_shape=[jax.ShapeDtypeStruct((BLOCK, 2048), BF16)] * 4
        + [
            jax.ShapeDtypeStruct((NX * BLOCK, FF_TILE), BF16),
            jax.ShapeDtypeStruct((NX * BLOCK, 2 * FF_TILE), BF16),
        ],
        compiler_params=params("arbitrary"),
        cost_estimate=cost(1 << 20, 1 << 16),
        name="feed_forward",
    )(x[None], *n2, ffn, d_act)


def ffn_grads(sc, n0, n1, n2, n3, dgu_ref, act_ref, c0, c1, c2, c3, *rest):
    i = pl.program_id(0)
    added, outs, act_t, g_ref = rest[:-4], rest[-4:-2], rest[-2], rest[-1]

    def put(which, place, value):
        if added:
            value = value + added[which][place].astype(F32)
        outs[which][place] = value.astype(BF16)

    @pl.when(i < NX)
    def _():
        lhs = []
        for zhi in range(2):
            shard = (zhi * NX + jnp.minimum(i, NX - 1)) * 2 + sc[0]
            at = pl.ds(pl.multiple_of(shard * BLOCK, BLOCK), BLOCK)
            lhs.append(jnp.concatenate([n[:, at] for n in (n0, n1, n2, n3)], axis=0))
        lhs = jnp.concatenate(lhs, axis=1)
        for half in range(2):
            cols = slice(FF_TILE * half, FF_TILE * (half + 1))
            g_ref[:, :FF_TILE] = lax.dot_general(
                lhs, dgu_ref[:, cols], (((0,), (0,)), ((), ())), preferred_element_type=F32
            )
            for zhi in range(2):
                for zlo in range(2):
                    for y in range(4):
                        row = zhi * BLOCK + (zlo * 4 + y) * 16
                        part = g_ref[row : row + 16, :FF_TILE]
                        put(0, (y, zlo * 2 + zhi, slice(None), cols), part)

    @pl.when(i == NX)
    def _():
        act_t[...] = act_ref[...].T

    @pl.when(i >= NX)
    def _():
        lhs = []
        for p in range(2):
            for j in range(11):
                row = (2 * p + sc[0]) * 352 + 32 * j + 16 * (i - NX)
                lhs.append(act_t[pl.ds(pl.multiple_of(row, 16), 16), :])
        lhs = jnp.concatenate(lhs, axis=0)
        for zlo in range(2):
            cols = slice(1024 * zlo, 1024 * (zlo + 1))
            cots = jnp.concatenate([c[:, cols] for c in (c0, c1, c2, c3)], axis=0)
            g = jnp.dot(lhs, cots, preferred_element_type=F32)
            for p in range(2):
                for j in range(11):
                    row = p * 176 + 16 * j
                    for y in range(4):
                        part = g[row : row + 16, 256 * y : 256 * (y + 1)]
                        to = slice(256 * j, 256 * (j + 1))
                        put(1, (zlo * 2 + p, y, slice(None), to), part)


def call_ffn_grads(core, n2, d_gu, act, cots, *added):
    const = pl.BlockSpec((BLOCK, 2048), lambda i, s: (0, 0))
    tile = (4, 4, 16, 2 * FF_TILE)
    outs = [
        pl.BlockSpec(tile, lambda i, s: (0, 0, jnp.minimum(i, NX - 1), 0)),
        pl.BlockSpec(tile, lambda i, s: (0, 0, jnp.maximum(i - NX, 0), 0)),
    ]
    return pl.pallas_call(
        ffn_grads,
        grid_spec=pltpu.PrefetchScalarGridSpec(
            num_scalar_prefetch=1,
            grid=(NX + 2,),
            in_specs=[const] * 4
            + [pl.BlockSpec((NX * BLOCK, 2 * FF_TILE), lambda i, s: (0, 0))]
            + [pl.BlockSpec((NX * BLOCK, FF_TILE), lambda i, s: (0, 0))]
            + [const] * 4
            + outs[: len(added)],
            out_specs=outs,
            scratch_shapes=[
                pltpu.VMEM((FF_TILE, NX * BLOCK), BF16),
                pltpu.VMEM((2 * BLOCK, FF_TILE), F32),
            ],
        ),
        out_shape=[
            jax.ShapeDtypeStruct((4, 4, 64, 2 * FF_TILE), BF16),
            jax.ShapeDtypeStruct((4, 4, 32, 2 * FF_TILE), BF16),
        ],
        compiler_params=params("arbitrary"),
        cost_estimate=cost(1 << 33, 1 << 20),
        name="ffn_grads_mine" if added else "ffn_grads_other",
    )(core[None], *n2, d_gu, act, *cots, *added)


def attention_grads(sc, n_ref, dq_ref, o_ref, db_ref, *rest):
    added, out_ref, qkv_s, out_s = rest[:-3], rest[-3], rest[-2], rest[-1]

    def put(place, value):
        if added:
            value = value + added[0][place].astype(F32)
        out_ref[place] = value.astype(BF16)

    for zhi in range(2):
        lhs = []
        for x in range(NX):
            at = pl.ds(pl.multiple_of(((zhi * NX + x) * 2 + sc[0]) * BLOCK, BLOCK), BLOCK)
            lhs.append(n_ref[:, at])
        lhs = jnp.concatenate(lhs, axis=1)
        qkv_s[...] = lax.dot_general(
            lhs, dq_ref[...], (((0,), (1,)), ((), ())), preferred_element_type=F32
        )
        for x in range(NX):
            for replica in range(8):
                row = BLOCK * x + 16 * replica
                to = slice(16 * x, 16 * (x + 1))
                put((replica % 4, replica // 4 * 2 + zhi, to, slice(0, 640)), qkv_s[row : row + 16, :])
    for p in range(2):
        rows = o_ref[pl.ds(pl.multiple_of((2 * p + sc[0]) * BLOCK, BLOCK), BLOCK), :]
        out_s[...] = jnp.dot(rows, db_ref[...], preferred_element_type=F32)
        for replica in range(8):
            for half in range(2):
                part = out_s[64 * half : 64 * (half + 1), 256 * replica : 256 * (replica + 1)]
                at = 640 + 256 * half
                put((replica % 4, replica // 4 * 2 + p, slice(None), slice(at, at + 256)), part)


def call_attention_grads(core, n1, d_qkv, ob, d_br, *added):
    vmem = pl.BlockSpec(memory_space=pltpu.VMEM)
    return pl.pallas_call(
        attention_grads,
        in_specs=[pl.BlockSpec(memory_space=pltpu.SMEM)] + [vmem] * (4 + len(added)),
        out_specs=vmem,
        out_shape=jax.ShapeDtypeStruct((4, 4, 64, 1152), BF16),
        scratch_shapes=[pltpu.VMEM((4 * BLOCK, 640), F32), pltpu.VMEM((BLOCK, 2048), F32)],
        compiler_params=params(),
        cost_estimate=cost(1 << 33, 1 << 20),
        name="attention_grads_mine" if added else "attention_grads_other",
    )(core[None], n1, d_qkv, ob, d_br, *added)


def shift_x(a, k):
    return lax.ppermute(a, "x", [(i, (i + k) % NX) for i in range(NX)])


def gathered_x(a, between=lambda: ()):
    half = a.shape[0] // 2
    t1, t3 = shift_x(a, 3), shift_x(a, 1)
    t1, t3 = lax.optimization_barrier((t1, t3, *between()))[:2]
    return [a, t1, jnp.concatenate([shift_x(t1[:half], 3), shift_x(t3[half:], 1)]), t3]


def moved_x(parts):
    half = parts[2].shape[0] // 2
    up, down = shift_x(parts[2][:half], 1), shift_x(parts[2][half:], 3)
    up = (parts[1][:half].astype(F32) + up.astype(F32)).astype(BF16)
    down = (parts[3][half:].astype(F32) + down.astype(F32)).astype(BF16)
    up = jnp.concatenate([up, parts[1][half:]])
    down = jnp.concatenate([parts[3][:half], down])
    return [parts[0], shift_x(up, 1), shift_x(down, 3)]


def added(parts):
    return sum(p.astype(F32) for p in parts)


def summed_x(parts):
    return added(moved_x(parts))


def sent(parts, axes, me=0):
    out = []
    for j in range(4):
        part = lax.dynamic_index_in_dim(parts, (me + j) % 4, 0, keepdims=False)
        out.append(lax.ppermute(part, axes, [(i, (i + j) % 4) for i in range(4)]) if j else part)
    return out


def total(parts):
    return parts.astype(F32).sum(axis=0).astype(BF16)


def pieces(a):
    return [a[BLOCK * j : BLOCK * (j + 1)] for j in range(NX)]


def summed(t, axes):
    return exchange(t, axes).astype(F32).sum(axis=0).astype(BF16)


def to_heads(first):
    pairs = []
    for s_zhi in range(2):
        for s_x in range(NX):
            d_zhi = s_x % 2 if first else 1 - s_x % 2
            pairs.append((s_zhi * NX + s_x, d_zhi * NX + 2 * s_zhi + s_x // 2))
    return pairs


def to_owners(first):
    return [(d, s) for s, d in to_heads(first)]


def after(a, *others):
    return lax.optimization_barrier((a, *others))[0]


def body(tok, cot, starts, gain_1, w_qkv, w_out, gain_2, w_gu, w_dn):
    zlo, y, zhi, x, core = (lax.axis_index(a) for a in AXES)
    replica = zlo * 4 + y
    rows, dim = tok.shape
    q_cols = GROUP * HEAD_SIZE
    ff_shard = w_dn.shape[0]
    slab = rows // 8

    t1, t3 = shift_x(tok, 3), shift_x(tok, 1)
    toks = [tok, t1, shift_x(t1[: rows // 2], 3), shift_x(t3[rows // 2 :], 1), t3]
    w_far = swap(w_out, "zhi")
    place = jnp.stack([replica, x])
    wide, gu_slab, dn_slab = call_pack(place, w_qkv, gain_1, gain_2, starts, w_gu, w_dn)
    qkv_cols = wide.shape[2]
    wide = exchange(wide, CHIP)

    gu_slab = jnp.concatenate(sent(gu_slab, "x"), axis=0)
    dn_slab = lax.ppermute(dn_slab, CHIP, to_heads(True))
    slabs = jnp.concatenate([gu_slab, dn_slab])
    slabs = after(slabs, wide, t1, t3)
    ffn = lax.all_gather(slabs, YZC, axis=0)
    ffn = ffn.reshape(8, 2, 2, NX * slab + 32, 2 * FF_TILE)

    inputs = tok.astype(F32)
    scaled_one, rstd_one = rms_forward(inputs)
    blocks = (x + jnp.arange(NX, dtype=jnp.int32)) % NX
    block_ids = zhi * 8 + 2 * blocks + core
    st = lax.dynamic_slice_in_dim(wide, zhi * NX, NX, 0)[:, rows, 2 * rows : 4 * rows]
    st = st.astype(F32).reshape(NX, 2, rows)
    st = (st[:, 0] * 256.0 + st[:, 1]).astype(jnp.int32)[blocks]
    where_at = block_ids[:, None] * rows + jnp.arange(rows, dtype=jnp.int32)[None, :]
    pos = (where_at - st).reshape(1, NX * rows).astype(F32)
    freqs = jnp.exp(jnp.arange(32, dtype=F32) * (-2.0 * math.log(ROPE_BASE) / HEAD_SIZE))
    angles = freqs[:, None] * pos
    cos, sin = jnp.cos(angles), jnp.sin(angles)
    n1, q_t, kv, wq, gains = call_project(core[None], toks, wide, swap(wide, "core"), cos, sin)
    gain_one, gain_two = gains[0], gains[1]
    kv = jnp.concatenate([kv, swap(kv, "core")], axis=0)
    near, far = jnp.where(zhi == 0, w_out, w_far), jnp.where(zhi == 0, w_far, w_out)
    even = x % 2 == 0
    part_a, part_b = jnp.where(even, near, far), jnp.where(even, far, near)
    part_a, part_b, cot_in = lax.optimization_barrier((part_a, part_b, cot, kv))[:3]
    kv = jnp.concatenate([kv, swap(kv, "zhi")], axis=0)
    part_a = lax.ppermute(part_a, "x", [(0, 0), (1, 2), (2, 1), (3, 3)])
    part_b = lax.ppermute(part_b, "x", [(0, 2), (1, 0), (2, 3), (3, 1)])
    firsts = jnp.min(st, axis=1) // CHUNK
    clears = (jnp.max(st, axis=1) + CHUNK - 1) // CHUNK
    sc = jnp.concatenate([zhi[None], x[None], core[None], firsts, clears]).astype(jnp.int32)
    st = st[:, None, :]
    o, ob, qr, lse = call_forward(sc, q_t, cos, sin, st, kv)
    cots = [cot_in, shift_x(cot_in, 3), shift_x(cot_in, 2), shift_x(cot_in, 1)]
    ob, *cots = lax.optimization_barrier((ob, *cots))
    part_a, part_b = after(part_a, ob), after(part_b, ob)
    *parts, wo = call_out_project(
        jnp.stack([x // 2, core]), ob, part_a, part_b, swap(part_a, "core"), swap(part_b, "core")
    )
    hidden = inputs + summed_x(parts)

    d_act, wdn = call_down_back(cots, ffn)
    scaled_two, rstd_two = rms_forward(hidden)
    n2 = gathered_x((scaled_two * gain_two[None, :]).astype(BF16), lambda: (d_act,))
    *d_n2, act, d_gu = call_feed_forward(x, n2, ffn, d_act)

    other = call_ffn_grads(1 - core, n2, d_gu, act, cots)
    d_n2 = moved_x(d_n2)
    other = lax.optimization_barrier((*other, *d_n2[1:]))[:2]
    other = [swap(g, "core") for g in other]
    g_gu, g_dn = call_ffn_grads(core, n2, d_gu, act, cots, *other)
    d_mid, gain_two_term = rms_backward(added(d_n2), scaled_two, rstd_two, gain_two)
    d_mid = cot.astype(F32) + d_mid
    d_br = gathered_x(d_mid.astype(BF16), lambda: (g_gu, g_dn))
    z = zlo * 2 + zhi
    g_gu = exchange(g_gu.reshape(4, 4 * 64, 2 * FF_TILE), "y")
    g_dn = sent(g_dn, ("zlo", "zhi"), z)
    d_br = jnp.concatenate(d_br)

    do = mm(wo, d_br, ((1,), (1,)), BF16)
    dq, dkv = call_backward(sc, qr, do, o, lse, cos, sin, st, kv)
    dkv, *g_dn = lax.optimization_barrier((dkv, *g_dn))
    dkv = dkv.reshape(2, 2, NX, 2 * HEAD_SIZE, rows)
    dkv = dkv[:, 0].astype(F32) + swap(dkv[:, 1], "core").astype(F32)
    dkv = dkv[0] + swap(dkv[1].astype(BF16), "zhi").astype(F32)
    g_dn = added(g_dn).astype(BF16)
    dkv = dkv.transpose(1, 0, 2).reshape(2 * HEAD_SIZE, NX * rows)
    k1, k2 = dkv[:32], dkv[32:64]
    dkv = jnp.concatenate([k1 * cos + k2 * sin, k2 * cos - k1 * sin, dkv[64:]], axis=0)
    d_qkv = jnp.concatenate([dq, dkv.astype(BF16)], axis=0)
    d_qkv, g_gu = lax.optimization_barrier((d_qkv, g_gu))
    d_n1 = mm(d_qkv, wq, ((0,), (1,)), BF16)
    d_qkv, ob, g_dn = lax.optimization_barrier((d_qkv, ob, g_dn, d_n1))[:3]
    d_n1 = moved_x(pieces(d_n1))
    other = swap(call_attention_grads(1 - core, n1, d_qkv, ob, d_br), "core")
    g_attn = call_attention_grads(core, n1, d_qkv, ob, d_br, other)

    g_gu, g_attn = lax.optimization_barrier((g_gu, g_attn))
    g_gu = exchange(total(g_gu.reshape(4, 4, 64, 2 * FF_TILE)), ("zlo", "zhi"))
    g_attn = sent(g_attn, "y", y)
    g_dn = sent(after(g_dn, g_attn[1]), "y", y)
    g_attn = sent(added(g_attn).astype(BF16), ("zlo", "zhi"), z)
    g_gu = exchange(total(g_gu).reshape(NX, slab, 2 * FF_TILE), "x")
    g_dn = lax.ppermute(added(g_dn).astype(BF16), CHIP, to_owners(True))
    *g_attn, g_gu, g_dn = lax.optimization_barrier((*g_attn, g_gu, g_dn))
    d_n1 = lax.optimization_barrier((*d_n1, *g_attn))[:3]
    act = after(act, *d_n1)
    mixed = moved_x(call_down_forward(act, wdn))
    d_in, gain_one_term = rms_backward(added(d_n1), scaled_one, rstd_one, gain_one)
    input_grad = (d_mid + d_in).astype(BF16)
    g_attn = added(g_attn).astype(BF16)
    g_out = lax.ppermute(g_attn[:, 640:], CHIP, to_owners(True))
    g_qkv = jnp.stack(sent(g_attn[:, :640].reshape(NX, slab, qkv_cols), "x", x))
    g_qkv = g_qkv[(x - jnp.arange(NX, dtype=jnp.int32)) % NX]
    g_qkv = g_qkv.reshape(NX * slab, qkv_cols)
    attn = [g_qkv[:32], g_out[:32], g_qkv[32:], g_out[32:], jnp.zeros((32, 512), BF16)]
    attn = jnp.concatenate(attn, axis=1)
    both = jnp.concatenate([g_gu.reshape(NX * slab, 2 * FF_TILE), g_dn, attn])
    payload = both = after(both, input_grad)
    both = lax.all_gather(both, REP, axis=0)
    g_gu, g_dn, g_qkv, g_out = call_spread(both)

    terms = jnp.stack([gain_one_term, gain_two_term]).reshape(2, 16, rows).transpose(1, 0, 2)
    terms = exchange(after(terms, payload), SHARD).sum(axis=0)
    terms = everywhere(terms.astype(BF16), REP, 8).astype(F32).sum(axis=0)
    mixed = hidden + added(mixed)

    return (
        mixed.astype(BF16),
        input_grad,
        terms[0],
        g_qkv,
        g_out,
        terms[1],
        g_gu,
        g_dn,
    )


def solution(mesh):
    fine = Mesh(mesh.devices.reshape(2, 4, 2, 4, 2), AXES)
    row, two = P(AXES), P(AXES, None)
    vec, mat = P(SHARD), P(SHARD, None)
    return jax.shard_map(
        body,
        mesh=fine,
        in_specs=(two, two, row, vec, mat, mat, vec, mat, mat),
        out_specs=(two, two, vec, mat, mat, vec, mat, mat),
        check_vma=False,
    )
```
